32 devices in a mesh: seq: 8 (over z, x), mp: 4 (over y, core).
Axes of the slice: x: 2, y: 2, z: 4, core: 2. Of those that a mesh axis runs over, the one named last changes fastest.
Arguments:
- voxels: bfloat16 [6144, 1024], P('seq'), may hold values from -6 to 6
- destination: int32 [6144], P('seq'), may hold values from 0 to 12287, as said below
- cond: bfloat16 [4096, 1024], P('seq'), may hold values from -40 to 40
- norm_gain: float32 [1024], replicated, may hold values from 0.1 to 1.9
- qkv_weight: bfloat16 [3, 1024, 1024], P(None, None, 'mp'), may hold values from -0.1875 to 0.1875
- self_out_weight: bfloat16 [1024, 1024], P('mp'), may hold values from -0.1875 to 0.1875
- cross_norm_gain: float32 [1024], replicated, may hold values from 0.1 to 1.9
- cross_q_weight: bfloat16 [1024, 1024], P(None, 'mp'), may hold values from -0.5 to 0.5
- cond_kv_weight: bfloat16 [2, 1024, 1024], P(None, None, 'mp'), may hold values from -0.1875 to 0.1875
- cross_out_weight: bfloat16 [1024, 1024], P('mp'), may hold values from -0.1875 to 0.1875
Outputs:
- layer_out: bfloat16 [6144, 1024], P(('seq', 'mp'))
The draws below stay inside these ranges and needn't reach their ends.
Inputs may be any that keep to these rules, and one draw needn't show every extreme that they name: Write owner = destination // 1536. No two voxels share a destination. Among the rows of one index of seq no owner occurs more than 192 times, on every index some owner occurs exactly 192 times, and some owner occurs 192 times on every index.
All inputs are finite; a program needn't handle non-finite values.
Results may differ from the reference program's by a relative error of at most 0.033.
The reference program's roundings to bfloat16 on the way count: a program that leaves them out, or rounds other values in their place, can miss the bound.
Values may be sent and summed in bfloat16 or wider, within the bound.
No kernel may reach another device: no remote copies, remote signals or barrier semaphores. Data moves between devices by JAX's collectives and lax.ppermute only.
A program may use at most 64 MiB of HBM per device.

```python
import jax
import jax.numpy as jnp
from jax import lax

D = 1024
HEADS = 16
HD = 64
DC = 1024
COND = 4096
WBLK = 64
VOX_DEV = 768
VOX = 6144
SLOTS = 1536
N_SEQ = 8


def draw_cond(key, part):
    values = jax.random.normal(jax.random.fold_in(key, 11), (COND, DC), jnp.float32)
    return jnp.clip(values, -40.0, 40.0).astype(jnp.bfloat16)


def draw_destination(key, part):
    base = jax.random.fold_in(key, 101)
    slot_total = 2 * VOX_DEV
    capacity = slot_total // N_SEQ
    position = jnp.arange(slot_total, dtype=jnp.int32)

    def owner_order(order_key):
        return jax.random.randint(order_key, (slot_total,), 0, 4096, dtype=jnp.int32)

    def shuffle_rows(row_key):
        return jax.random.permutation(row_key, VOX_DEV).astype(jnp.int32)
    order_keys = jax.random.split(jax.random.fold_in(base, 1), N_SEQ)
    order_scores = jax.vmap(owner_order)(order_keys) * slot_total + position[None, :]
    order_scores = order_scores.at[:, 0].set(-2).at[:, slot_total - 1].set(-1)
    orders = jnp.argsort(order_scores, axis=1, stable=True).astype(jnp.int32)
    groups = orders.reshape(N_SEQ, N_SEQ, capacity)
    shift = jax.random.randint(jax.random.fold_in(base, 2), (), 0, N_SEQ, dtype=jnp.int32)
    hot_owner = jax.random.randint(jax.random.fold_in(base, 3), (), 0, N_SEQ, dtype=jnp.int32)
    indices = jnp.arange(N_SEQ, dtype=jnp.int32)
    group_index = (indices[None, :] - indices[:, None] + shift) % N_SEQ
    reserved = jnp.take_along_axis(groups, jnp.broadcast_to(group_index[:, :, None], (N_SEQ, N_SEQ, capacity)), axis=1)
    reserved = jnp.transpose(reserved, (1, 0, 2)).reshape(N_SEQ, slot_total)
    forced_owner = (indices + shift) % N_SEQ
    forced = jnp.where(indices[None, :] == forced_owner[:, None], 32768, 0).astype(jnp.int32)
    forced = forced + jnp.where(indices == hot_owner, 16384, 0).astype(jnp.int32)[None, :]
    bias = jax.random.randint(jax.random.fold_in(base, 4), (N_SEQ,), 0, 6144, dtype=jnp.int32)
    noise = jax.random.randint(jax.random.fold_in(base, 5), (N_SEQ, N_SEQ, capacity), 0, 4096, dtype=jnp.int32)
    scores = noise + (bias[None, :] + forced)[:, :, None]
    ranked = scores.reshape(N_SEQ, slot_total) * slot_total + position[None, :]
    chosen = lax.top_k(ranked, VOX_DEV)[1].astype(jnp.int32)
    owners = chosen // capacity
    slot_ids = jnp.take_along_axis(reserved, chosen, axis=1)
    row_keys = jax.random.split(jax.random.fold_in(base, 6), N_SEQ)
    shuffles = jax.vmap(shuffle_rows)(row_keys)
    owners = jnp.take_along_axis(owners, shuffles, axis=1)
    slot_ids = jnp.take_along_axis(slot_ids, shuffles, axis=1)
    return (owners * slot_total + slot_ids).reshape(N_SEQ * VOX_DEV).astype(jnp.int32)


def level_of(stream_key, shape, cuts, smallest, top_value):
    level = 1.0
    for axis_at, parts in cuts:
        heights = jax.random.uniform(jax.random.fold_in(jax.random.fold_in(stream_key, 6), axis_at), (parts,), jnp.float32, smallest / len(cuts), top_value / len(cuts))
        level = level * jnp.repeat(jnp.exp(heights), shape[axis_at] // parts).reshape((-1,) + (1,) * (len(shape) - 1 - axis_at))
    return level


def normal_values(stream_key, shape, scale, reach, shards=(), kind=jnp.bfloat16):
    result = scale * jax.random.normal(stream_key, shape, jnp.float32)
    if shards:
        result = result * level_of(stream_key, shape, shards, -0.22, 0.18)
    return jnp.clip(result, -reach, reach).astype(kind)


def setup_inputs(seed: int = 0) -> dict:
    streams_of = jax.random.split(jax.random.key(seed), 11)
    voxels = normal_values(streams_of[0], (VOX, D), 1.0, 6.0, ((0, 8),))
    destination = draw_destination(jax.random.fold_in(streams_of[10], 71), 0)
    cond = draw_cond(jax.random.fold_in(streams_of[10], 71), 0)
    norm_gain = jnp.clip(1.0 + 0.18 * jax.random.normal(streams_of[3], (D,), jnp.float32), 0.1, 1.9)
    qkv_weight = normal_values(streams_of[4], (3, D, D), D ** -0.5, 0.1875, ((2, 4),))
    self_out_weight = normal_values(streams_of[5], (D, D), D ** -0.5, 0.1875, ((0, 4),))
    cross_norm_gain = jnp.clip(1.0 + 0.18 * jax.random.normal(streams_of[6], (D,), jnp.float32), 0.1, 1.9)
    cross_q_weight = normal_values(streams_of[7], (D, D), (D // 9) ** -0.5, 0.5, ((1, 4),))
    cond_kv_weight = normal_values(streams_of[8], (2, DC, D), DC ** -0.5, 0.1875, ((2, 4),))
    cross_out_weight = normal_values(streams_of[9], (D, D), D ** -0.5, 0.1875, ((0, 4),))
    return dict(voxels=voxels, destination=destination, cond=cond, norm_gain=norm_gain, qkv_weight=qkv_weight, self_out_weight=self_out_weight, cross_norm_gain=cross_norm_gain, cross_q_weight=cross_q_weight, cond_kv_weight=cond_kv_weight, cross_out_weight=cross_out_weight)


def rms_norm(matrix, gain):
    values = matrix.astype(jnp.float32)
    spread = lax.optimization_barrier(jnp.mean(values * values, axis=-1, keepdims=True))
    return (values * lax.rsqrt(spread + 1e-06) * gain).astype(jnp.bfloat16)

def window_block(queries, keyset, valset, occupied, head_count):
    window_count = queries.shape[0] // WBLK
    query_heads = queries.astype(jnp.float32).reshape(window_count, WBLK, head_count, HD)
    key_heads = keyset.astype(jnp.float32).reshape(window_count, WBLK, head_count, HD)
    value_heads = valset.astype(jnp.float32).reshape(window_count, WBLK, head_count, HD)
    scores = jnp.einsum('wqhd,wkhd->whqk', query_heads, key_heads) * HD ** (-0.5)
    diagonal = jnp.arange(WBLK, dtype=jnp.int32)[:, None] == jnp.arange(WBLK, dtype=jnp.int32)[None, :]
    allowed = occupied.reshape(window_count, 1, WBLK) | diagonal[None]
    weights = jnp.where(allowed[:, None], jnp.exp(scores), 0.0)
    totals = lax.optimization_barrier(jnp.sum(weights, axis=-1))
    mixed = jnp.einsum('whqk,wkhd->wqhd', weights.astype(jnp.bfloat16).astype(jnp.float32), value_heads)
    mixed = mixed / jnp.transpose(totals, (0, 2, 1))[:, :, :, None]
    return mixed.astype(jnp.bfloat16).reshape(window_count * WBLK, head_count * HD)

def attend_block(query_block, key_rows, value_rows, head_count):
    queries = query_block.astype(jnp.float32).reshape(query_block.shape[0], head_count, HD)
    keyset = key_rows.astype(jnp.float32).reshape(key_rows.shape[0], head_count, HD)
    valset = value_rows.astype(jnp.float32).reshape(value_rows.shape[0], head_count, HD)
    scores = jnp.einsum('qhd,khd->hqk', queries, keyset) * HD ** (-0.5)
    row_max = lax.optimization_barrier(jnp.max(scores, axis=-1, keepdims=True))
    weights = jnp.exp(scores - row_max)
    totals = lax.optimization_barrier(jnp.sum(weights, axis=-1))
    mixed = jnp.einsum('hqk,khd->qhd', weights.astype(jnp.bfloat16).astype(jnp.float32), valset)
    mixed = mixed / jnp.transpose(totals)[:, :, None]
    return mixed.astype(jnp.bfloat16).reshape(query_block.shape[0], head_count * HD)

def reference(voxels, destination, cond, norm_gain, qkv_weight, self_out_weight, cross_norm_gain, cross_q_weight, cond_kv_weight, cross_out_weight):
    normed = rms_norm(voxels, norm_gain)
    projected = [jnp.dot(normed, qkv_weight[index], preferred_element_type=jnp.float32).astype(jnp.bfloat16) for index in range(3)]
    total_slots = N_SEQ * SLOTS
    layouts = [jnp.zeros((total_slots, D), jnp.bfloat16).at[destination].set(item).reshape(N_SEQ, SLOTS, D) for item in projected]
    occupied = jnp.zeros((total_slots,), jnp.bool_).at[destination].set(True).reshape(N_SEQ, SLOTS)

    def attend_owner(operands):
        return window_block(operands[0], operands[1], operands[2], operands[3], HEADS)
    mixed = lax.map(attend_owner, (layouts[0], layouts[1], layouts[2], occupied))
    window_mix = mixed.reshape(total_slots, D)[destination]
    hidden = voxels.astype(jnp.float32) + jnp.dot(window_mix, self_out_weight, preferred_element_type=jnp.float32)
    normed2 = rms_norm(hidden, cross_norm_gain)
    cross_query = jnp.dot(normed2, cross_q_weight, preferred_element_type=jnp.float32).astype(jnp.bfloat16)
    cond_key = jnp.dot(cond, cond_kv_weight[0], preferred_element_type=jnp.float32).astype(jnp.bfloat16)
    cond_value = jnp.dot(cond, cond_kv_weight[1], preferred_element_type=jnp.float32).astype(jnp.bfloat16)
    block_size = min(512, VOX)

    def cross_inner(query_block):
        return attend_block(query_block, cond_key, cond_value, HEADS)
    cross_mix = lax.map(cross_inner, cross_query.reshape(VOX // block_size, block_size, D)).reshape(VOX, D)
    layer_out = hidden + jnp.dot(cross_mix, cross_out_weight, preferred_element_type=jnp.float32)
    return layer_out.astype(jnp.bfloat16)
```

```python
import functools
import math

import jax
import jax.numpy as jnp
from jax import lax
from jax.experimental import pallas as pl
from jax.experimental.pallas import tpu as pltpu
from jax.sharding import PartitionSpec as P

HD = 64
WBLK = 64
LANES = 128
ID_ROWS = 16
VMEM_LIMIT = 48 * 1024 * 1024
CORE_SWAP = ((0, 1), (1, 0), (2, 3), (3, 2))
CHIP_SWAP = ((0, 2), (2, 0), (1, 3), (3, 1))


def low_lanes(shape):
    return lax.broadcasted_iota(jnp.int32, shape, 1) < HD


def swap_halves(values):
    return pltpu.roll(values, HD, 1)


def project_kernel(core_ref, vox_ref, gain_ref, ids_ref, own_ref, other_ref, out_ref, normed_ref):
    step = pl.program_id(0)
    rows = vox_ref.shape[0]
    packed = rows // 2

    @pl.when(step == 0)
    def _():
        values = vox_ref[...].astype(jnp.float32)
        spread = jnp.mean(values * values, axis=-1, keepdims=True)
        normed_ref[...] = (values * lax.rsqrt(spread + 1e-06) * gain_ref[...]).astype(jnp.bfloat16)

    def emit(weight_ref):
        normed = normed_ref[...]
        low = low_lanes((rows, LANES))
        low_packed = low_lanes((packed, LANES))
        query, key, value = (
            jnp.dot(normed, weight_ref[part], preferred_element_type=jnp.float32)
            for part in range(3)
        )
        query = query * HD ** (-0.5)
        first, second = query[:packed], query[packed:]
        pairs = (
            (
                jnp.where(low, key, swap_halves(value)),
                jnp.where(low_packed, first, swap_halves(second)),
            ),
            (
                jnp.where(low, swap_halves(key), value),
                jnp.where(low_packed, swap_halves(first), second),
            ),
        )
        for head, (keyval, queries) in enumerate(pairs):
            out_ref[head, :rows] = keyval.astype(jnp.bfloat16)
            out_ref[head, rows : rows + ID_ROWS] = ids_ref[...]
            out_ref[head, rows + ID_ROWS :] = queries.astype(jnp.bfloat16)

    @pl.when(step < 2)
    def _():
        emit(own_ref)

    @pl.when(step >= 2)
    def _():
        emit(other_ref)


def project(core, vox, gain, ids, own_weight, other_weight):
    rows, width = vox.shape
    local_width = own_weight.shape[2]
    heads = 2 * local_width // HD
    pair_steps = heads // 2
    half_steps = pair_steps // 2
    blob = rows + ID_ROWS + rows // 2

    def out_map(step, core_ref):
        side = step // half_steps
        absolute = jnp.where(side == 0, core_ref[0], 1 - core_ref[0])
        return (absolute * half_steps + step % half_steps, 0, 0)

    return pl.pallas_call(
        project_kernel,
        out_shape=jax.ShapeDtypeStruct((heads, blob, LANES), jnp.bfloat16),
        grid_spec=pltpu.PrefetchScalarGridSpec(
            num_scalar_prefetch=1,
            grid=(pair_steps,),
            in_specs=[
                pl.BlockSpec((rows, width), lambda step, core_ref: (0, 0)),
                pl.BlockSpec((1, width), lambda step, core_ref: (0, 0)),
                pl.BlockSpec((ID_ROWS, LANES), lambda step, core_ref: (0, 0)),
                pl.BlockSpec(
                    (3, width, LANES),
                    lambda step, core_ref: (0, 0, jnp.minimum(step, half_steps - 1)),
                ),
                pl.BlockSpec(
                    (3, width, LANES),
                    lambda step, core_ref: (0, 0, jnp.maximum(step - half_steps, 0)),
                ),
            ],
            out_specs=pl.BlockSpec((2, blob, LANES), out_map),
            scratch_shapes=[pltpu.VMEM((rows, width), jnp.bfloat16)],
        ),
        compiler_params=pltpu.CompilerParams(vmem_limit_bytes=VMEM_LIMIT),
    )(core, vox, gain, ids, own_weight, other_weight)


def read_ids(ref, index, rows):
    tile = ref[index, rows : rows + ID_ROWS].astype(jnp.float32)
    return tile[:8] * 256.0 + tile[8:]


def window_kernel(mine_ref, theirs_ref, out_ref):
    source = pl.program_id(0)
    sources = mine_ref.shape[0]
    packed = out_ref.shape[1]
    rows = 2 * packed
    groups = rows // LANES
    low_packed = low_lanes((packed, LANES))
    wire = mine_ref[source, rows + ID_ROWS :].astype(jnp.float32)
    query = jnp.concatenate(
        [jnp.where(low_packed, wire, 0.0), jnp.where(low_packed, swap_halves(wire), 0.0)], axis=0
    ).astype(jnp.bfloat16)
    columns = jnp.transpose(read_ids(mine_ref, source, rows))
    query_ids = jnp.concatenate([columns[:, g : g + 1] for g in range(groups)], axis=0)
    low = low_lanes((rows, LANES))
    one = jnp.ones((), jnp.bfloat16)

    def fold(ref, index, total):
        keyval = ref[index, :rows]
        key_ids = read_ids(ref, index, rows)
        scores = lax.dot_general(
            query, keyval, (((1,), (1,)), ((), ())), preferred_element_type=jnp.float32
        )
        weights = jnp.concatenate(
            [
                jnp.where(
                    query_ids == key_ids[g : g + 1],
                    jnp.exp(scores[:, g * LANES : (g + 1) * LANES]),
                    0.0,
                ).astype(jnp.bfloat16)
                for g in range(groups)
            ],
            axis=1,
        )
        return total + jnp.dot(
            weights, jnp.where(low, one, keyval), preferred_element_type=jnp.float32
        )

    def body(index, total):
        return fold(theirs_ref, index, fold(mine_ref, index, total))

    total = lax.fori_loop(0, sources, body, jnp.zeros((rows, LANES), jnp.float32))
    mixed = total / swap_halves(total)
    out_ref[0] = jnp.where(low_packed, swap_halves(mixed[:packed]), mixed[packed:]).astype(
        jnp.bfloat16
    )


def window_mixing(mine, theirs, packed):
    sources, blob, _ = mine.shape
    return pl.pallas_call(
        window_kernel,
        out_shape=jax.ShapeDtypeStruct((sources, packed, LANES), jnp.bfloat16),
        grid=(sources,),
        in_specs=[
            pl.BlockSpec(mine.shape, lambda source: (0, 0, 0)),
            pl.BlockSpec(theirs.shape, lambda source: (0, 0, 0)),
        ],
        out_specs=pl.BlockSpec((1, packed, LANES), lambda source: (source, 0, 0)),
        compiler_params=pltpu.CompilerParams(vmem_limit_bytes=VMEM_LIMIT),
    )(mine, theirs)


def cross_kernel(query_ref, key_ref, value_ref, out_ref, score_ref):
    rows = query_ref.shape[0]
    tokens = key_ref.shape[0]
    chunk = math.gcd(tokens, 512)
    low = low_lanes((rows, LANES))
    wire = query_ref[...]
    zero = jnp.zeros((), jnp.bfloat16)
    ones = jnp.ones((chunk, LANES), jnp.bfloat16)
    mixes = []
    for head in range(2):
        query = jnp.where(low == (head == 0), wire, zero)
        peak = jnp.full((rows, LANES), -jnp.inf, jnp.float32)
        for start in range(0, tokens, chunk):
            scores = lax.dot_general(
                query,
                key_ref[start : start + chunk],
                (((1,), (1,)), ((), ())),
                preferred_element_type=jnp.float32,
            )
            score_ref[head, :, start : start + chunk] = scores
            for g in range(chunk // LANES):
                peak = jnp.maximum(peak, scores[:, g * LANES : (g + 1) * LANES])
        row_max = jnp.max(peak, axis=-1, keepdims=True)
        total = jnp.zeros((rows, 2 * LANES), jnp.float32)
        for start in range(0, tokens, chunk):
            weights = jnp.exp(score_ref[head, :, start : start + chunk] - row_max).astype(
                jnp.bfloat16
            )
            values = jnp.concatenate([value_ref[start : start + chunk], ones], axis=1)
            total = total + jnp.dot(weights, values, preferred_element_type=jnp.float32)
        mixes.append(total[:, :LANES] / total[:, LANES:])
    out_ref[...] = jnp.where(low, mixes[0], mixes[1]).astype(jnp.bfloat16)


def cross_mixing(queries, keyval):
    rows, local_width = queries.shape
    tokens = keyval.shape[0]
    pairs = local_width // LANES
    block = rows // 2
    return pl.pallas_call(
        cross_kernel,
        out_shape=jax.ShapeDtypeStruct((rows, local_width), jnp.bfloat16),
        grid=(pairs, rows // block),
        in_specs=[
            pl.BlockSpec((block, LANES), lambda pair, part: (part, pair)),
            pl.BlockSpec((tokens, LANES), lambda pair, part: (0, pair)),
            pl.BlockSpec((tokens, LANES), lambda pair, part: (0, pairs + pair)),
        ],
        out_specs=pl.BlockSpec((block, LANES), lambda pair, part: (part, pair)),
        scratch_shapes=[pltpu.VMEM((2, block, tokens), jnp.float32)],
        compiler_params=pltpu.CompilerParams(vmem_limit_bytes=VMEM_LIMIT),
    )(queries, keyval, keyval)


def swap(array, pairs):
    return lax.ppermute(array, "mp", pairs)


def by_head(
    voxels,
    destination,
    cond,
    norm_gain,
    qkv_weight,
    self_out_weight,
    cross_norm_gain,
    cross_q_weight,
    cond_kv_weight,
    cross_out_weight,
):
    model_index = lax.axis_index("mp")
    core = model_index % 2
    chip = model_index // 2
    row_count, width = voxels.shape
    local_width = qkv_weight.shape[2]
    share = row_count // 4
    rows = 2 * share
    head_count = 2 * local_width // HD

    other_qkv = swap(qkv_weight, CORE_SWAP)
    cond_pair = [
        jnp.dot(cond, cond_kv_weight[part], preferred_element_type=jnp.float32).astype(jnp.bfloat16)
        for part in range(2)
    ]
    own_keyval = lax.all_gather(jnp.concatenate(cond_pair, axis=1), "seq", axis=0, tiled=True)

    vox = lax.dynamic_index_in_dim(
        voxels.reshape(2, 2, share, width), core, axis=1, keepdims=False
    ).reshape(rows, width)
    window_ids = (
        lax.dynamic_index_in_dim(
            destination.reshape(2, 2, share), core, axis=1, keepdims=False
        ).reshape(rows // LANES, LANES)
        // WBLK
    )
    blank = jnp.zeros((8 - rows // LANES, LANES), jnp.int32)
    ids = jnp.concatenate([window_ids // 256, blank, window_ids % 256, blank], axis=0).astype(
        jnp.bfloat16
    )
    sent = project(
        core.reshape(1).astype(jnp.int32), vox, norm_gain.reshape(1, width), ids, qkv_weight, other_qkv
    )

    chip_out = swap(jnp.concatenate([self_out_weight, cross_out_weight], axis=0), CHIP_SWAP)
    other_q = swap(cross_q_weight, CORE_SWAP)

    mine = lax.all_to_all(sent, "seq", split_axis=0, concat_axis=0, tiled=True)
    theirs = swap(mine[:, : rows + ID_ROWS], CORE_SWAP)
    mixed = window_mixing(mine, theirs, share)
    returned = lax.all_to_all(mixed, "seq", split_axis=0, concat_axis=0, tiled=True)
    near_mix = (
        returned.reshape(head_count, share, 2, HD).transpose(2, 1, 0, 3).reshape(rows, head_count * HD)
    )
    far_mix = swap(near_mix, CHIP_SWAP)

    own_out = jnp.concatenate([self_out_weight, cross_out_weight], axis=0)
    own_other_out = swap(own_out, CORE_SWAP)
    chip_other_out = swap(chip_out, CORE_SWAP)
    split = self_out_weight.shape[0]

    def in_order(first, second):
        return jnp.where(
            core == 0,
            jnp.concatenate([first[:split], second[:split]], axis=0),
            jnp.concatenate([second[:split], first[:split]], axis=0),
        )

    summed = jnp.dot(
        near_mix, in_order(own_out, own_other_out), preferred_element_type=jnp.float32
    ) + jnp.dot(far_mix, in_order(chip_out, chip_other_out), preferred_element_type=jnp.float32)
    hidden = vox.astype(jnp.float32) + summed
    spread = jnp.mean(hidden * hidden, axis=-1, keepdims=True)
    normed = (hidden * lax.rsqrt(spread + 1e-06) * cross_norm_gain).astype(jnp.bfloat16)
    own_hidden = lax.dynamic_slice_in_dim(hidden, chip * share, share, 0)

    def queries_of(weight):
        return (
            jnp.dot(normed, weight, preferred_element_type=jnp.float32).astype(jnp.bfloat16)
            * HD ** (-0.5)
        ).astype(jnp.bfloat16)

    other_keyval = swap(own_keyval, CORE_SWAP)
    own_cross = cross_mixing(queries_of(cross_q_weight), own_keyval)
    other_cross = cross_mixing(queries_of(other_q), other_keyval)
    both = jnp.concatenate([own_cross, other_cross], axis=1).reshape(2, share, 2 * local_width)
    kept = lax.dynamic_index_in_dim(both, chip, axis=0, keepdims=False)
    arrived = swap(lax.dynamic_index_in_dim(both, 1 - chip, axis=0, keepdims=False), CHIP_SWAP)
    near_out = jnp.concatenate([own_out[split:], own_other_out[split:]], axis=0)
    far_out = jnp.concatenate([chip_out[split:], chip_other_out[split:]], axis=0)
    crossed = jnp.dot(kept, near_out, preferred_element_type=jnp.float32) + jnp.dot(
        arrived, far_out, preferred_element_type=jnp.float32
    )
    return (own_hidden + crossed).astype(jnp.bfloat16)


def rms_norm(matrix, gain):
    values = matrix.astype(jnp.float32)
    spread = jnp.mean(values * values, axis=-1, keepdims=True)
    return (values * lax.rsqrt(spread + 1e-06) * gain).astype(jnp.bfloat16)


def window_attention(queries, keyset, valset, occupied, head_count):
    slot_count = queries.shape[0]
    window_count = slot_count // WBLK
    query_heads = queries.reshape(window_count, WBLK, head_count, HD)
    key_heads = keyset.reshape(window_count, WBLK, head_count, HD)
    value_heads = valset.reshape(window_count, WBLK, head_count, HD)
    scores = jnp.einsum(
        "wqhd,wkhd->whqk", query_heads, key_heads, preferred_element_type=jnp.float32
    ) * HD ** (-0.5)
    diagonal = (
        jnp.arange(WBLK, dtype=jnp.int32)[:, None] == jnp.arange(WBLK, dtype=jnp.int32)[None, :]
    )
    allowed = occupied.reshape(window_count, 1, WBLK) | diagonal[None]
    weights = jnp.where(allowed[:, None], jnp.exp(scores), 0.0)
    totals = jnp.sum(weights, axis=-1)
    mixed = jnp.einsum(
        "whqk,wkhd->wqhd",
        weights.astype(jnp.bfloat16),
        value_heads,
        preferred_element_type=jnp.float32,
    )
    mixed = mixed / jnp.transpose(totals, (0, 2, 1))[:, :, :, None]
    return mixed.astype(jnp.bfloat16).reshape(slot_count, head_count * HD)


def by_owner(
    voxels,
    destination,
    cond,
    norm_gain,
    qkv_weight,
    self_out_weight,
    cross_norm_gain,
    cross_q_weight,
    cond_kv_weight,
    cross_out_weight,
):
    peer_count = lax.axis_size("seq")
    part_count = lax.axis_size("mp")
    model_index = lax.axis_index("mp")
    row_count = voxels.shape[0]
    local_width = qkv_weight.shape[2]
    head_count = local_width // HD
    capacity = 2 * row_count // peer_count
    slot_count = peer_count * capacity
    owner_ids = destination // slot_count
    slot_ids = destination % slot_count
    matches = (owner_ids[:, None] == jnp.arange(peer_count, dtype=jnp.int32)[None, :]).astype(
        jnp.int32
    )
    within = jnp.sum(matches * (jnp.cumsum(matches, axis=0) - 1), axis=1)
    send_index = owner_ids * capacity + within
    normed = rms_norm(voxels, norm_gain)
    place_buffer = (
        jnp.full((slot_count,), slot_count, jnp.int32)
        .at[send_index]
        .set(slot_ids)
        .reshape(peer_count, capacity)
    )
    projected = jnp.einsum(
        "rd,cdh->rch", normed, qkv_weight, preferred_element_type=jnp.float32
    ).astype(jnp.bfloat16)
    send_buffer = (
        jnp.zeros((slot_count, 3 * local_width), jnp.bfloat16)
        .at[send_index]
        .set(projected.reshape(row_count, 3 * local_width))
    )
    received, places = (
        lax.all_to_all(
            send_buffer.reshape(peer_count, capacity, 3 * local_width),
            "seq",
            split_axis=0,
            concat_axis=0,
            tiled=True,
        ),
        lax.all_to_all(place_buffer, "seq", split_axis=0, concat_axis=0, tiled=True),
    )
    received = received.reshape(slot_count, 3 * local_width)
    places = places.reshape(slot_count)
    layout = (
        jnp.zeros((slot_count, 3 * local_width), jnp.bfloat16).at[places].set(received, mode="drop")
    )
    occupied = jnp.zeros((slot_count,), jnp.bool_).at[places].set(True, mode="drop")
    mixed = window_attention(
        layout[:, :local_width],
        layout[:, local_width : 2 * local_width],
        layout[:, 2 * local_width :],
        occupied,
        head_count,
    )
    outgoing = mixed[jnp.minimum(places, slot_count - 1)]
    returned = lax.all_to_all(
        outgoing.reshape(peer_count, capacity, local_width),
        "seq",
        split_axis=0,
        concat_axis=0,
        tiled=True,
    )
    window_mix = returned.reshape(slot_count, local_width)[send_index]
    row_share = row_count // part_count
    summed_out = lax.psum(
        jnp.dot(window_mix, self_out_weight, preferred_element_type=jnp.float32), "mp"
    )
    hidden = voxels.astype(jnp.float32) + summed_out
    normed2 = rms_norm(hidden, cross_norm_gain)
    own_hidden = lax.dynamic_slice_in_dim(hidden, model_index * row_share, row_share, 0)
    cross_query = (
        jnp.dot(normed2, cross_q_weight, preferred_element_type=jnp.float32)
        .astype(jnp.bfloat16)
        .reshape(row_count, head_count, HD)
    )
    cond_pair = jnp.einsum(
        "td,cdh->cth", cond, cond_kv_weight, preferred_element_type=jnp.float32
    ).astype(jnp.bfloat16)

    def fold_block(running, key_block, value_block):
        row_max, totals, mixed_sum = running
        scores = jnp.einsum(
            "qhd,khd->qhk", cross_query, key_block, preferred_element_type=jnp.float32
        ) * HD ** (-0.5)
        new_max = jnp.maximum(row_max, jnp.max(scores, axis=-1))
        rescale = jnp.exp(row_max - new_max)
        weights = jnp.exp(scores - new_max[:, :, None])
        totals = totals * rescale + jnp.sum(weights, axis=-1)
        update = jnp.einsum(
            "qhk,khd->qhd",
            weights.astype(jnp.bfloat16),
            value_block,
            preferred_element_type=jnp.float32,
        )
        return (new_max, totals, mixed_sum * rescale[:, :, None] + update)

    start_state = (
        jnp.full((row_count, head_count), -1e30, jnp.float32),
        jnp.zeros((row_count, head_count), jnp.float32),
        jnp.zeros((row_count, head_count, HD), jnp.float32),
    )
    key_piece = lax.all_gather(cond_pair[0], "seq", axis=0, tiled=True)
    value_piece = lax.all_gather(cond_pair[1], "seq", axis=0, tiled=True)
    token_count = key_piece.shape[0]
    sub_block = math.gcd(token_count, 512)
    key_blocks = key_piece.reshape(token_count // sub_block, sub_block, head_count, HD)
    value_blocks = value_piece.reshape(token_count // sub_block, sub_block, head_count, HD)

    def advance(state, operands):
        return (fold_block(state, operands[0], operands[1]), None)

    folded, unused = lax.scan(advance, start_state, (key_blocks, value_blocks))
    row_max, totals, mixed_sum = folded
    cross_mix = (
        (mixed_sum / totals[:, :, None]).astype(jnp.bfloat16).reshape(row_count, local_width)
    )
    cross_sum = lax.psum_scatter(
        jnp.dot(cross_mix, cross_out_weight, preferred_element_type=jnp.float32),
        "mp",
        scatter_dimension=0,
        tiled=True,
    )
    return (own_hidden + cross_sum).astype(jnp.bfloat16)


def solution(mesh):
    heads_match = mesh.shape["mp"] == 4 and mesh.shape["seq"] == 8
    return jax.shard_map(
        by_head if heads_match else by_owner,
        mesh=mesh,
        in_specs=(
            P("seq", None),
            P("seq"),
            P("seq", None),
            P(),
            P(None, None, "mp"),
            P("mp", None),
            P(),
            P(None, "mp"),
            P(None, None, "mp"),
            P("mp", None),
        ),
        out_specs=P(("seq", "mp"), None),
        check_vma=False,
    )
```

```python
import functools
import math

import jax
import jax.numpy as jnp
from jax import lax
from jax.experimental import pallas as pl
from jax.experimental.pallas import tpu as pltpu
from jax.sharding import PartitionSpec as P

HD = 64
WBLK = 64
LANES = 128
ID_ROWS = 16
VMEM_LIMIT = 48 * 1024 * 1024
CORE_SWAP = ((0, 1), (1, 0), (2, 3), (3, 2))
CHIP_SWAP = ((0, 2), (2, 0), (1, 3), (3, 1))


def low_lanes(shape):
    return lax.broadcasted_iota(jnp.int32, shape, 1) < HD


def swap_halves(values):
    return pltpu.roll(values, HD, 1)


def project_kernel(core_ref, vox_ref, gain_ref, ids_ref, own_ref, other_ref, out_ref, normed_ref):
    step = pl.program_id(0)
    rows = vox_ref.shape[0]
    packed = rows // 2

    @pl.when(step == 0)
    def _():
        values = vox_ref[...].astype(jnp.float32)
        spread = jnp.mean(values * values, axis=-1, keepdims=True)
        normed_ref[...] = (values * lax.rsqrt(spread + 1e-06) * gain_ref[...]).astype(jnp.bfloat16)

    def emit(weight_ref):
        normed = normed_ref[...]
        low = low_lanes((rows, LANES))
        low_packed = low_lanes((packed, LANES))
        query, key, value = (
            jnp.dot(normed, weight_ref[part], preferred_element_type=jnp.float32)
            for part in range(3)
        )
        query = query * HD ** (-0.5)
        first, second = query[:packed], query[packed:]
        pairs = (
            (
                jnp.where(low, key, swap_halves(value)),
                jnp.where(low_packed, first, swap_halves(second)),
            ),
            (
                jnp.where(low, swap_halves(key), value),
                jnp.where(low_packed, swap_halves(first), second),
            ),
        )
        for head, (keyval, queries) in enumerate(pairs):
            out_ref[head, :rows] = keyval.astype(jnp.bfloat16)
            out_ref[head, rows : rows + ID_ROWS] = ids_ref[...]
            out_ref[head, rows + ID_ROWS :] = queries.astype(jnp.bfloat16)

    @pl.when(step < 2)
    def _():
        emit(own_ref)

    @pl.when(step >= 2)
    def _():
        emit(other_ref)


def project(core, vox, gain, ids, own_weight, other_weight):
    rows, width = vox.shape
    local_width = own_weight.shape[2]
    heads = 2 * local_width // HD
    pair_steps = heads // 2
    half_steps = pair_steps // 2
    blob = rows + ID_ROWS + rows // 2

    def out_map(step, core_ref):
        side = step // half_steps
        absolute = jnp.where(side == 0, core_ref[0], 1 - core_ref[0])
        return (absolute * half_steps + step % half_steps, 0, 0)

    return pl.pallas_call(
        project_kernel,
        out_shape=jax.ShapeDtypeStruct((heads, blob, LANES), jnp.bfloat16),
        grid_spec=pltpu.PrefetchScalarGridSpec(
            num_scalar_prefetch=1,
            grid=(pair_steps,),
            in_specs=[
                pl.BlockSpec((rows, width), lambda step, core_ref: (0, 0)),
                pl.BlockSpec((1, width), lambda step, core_ref: (0, 0)),
                pl.BlockSpec((ID_ROWS, LANES), lambda step, core_ref: (0, 0)),
                pl.BlockSpec(
                    (3, width, LANES),
                    lambda step, core_ref: (0, 0, jnp.minimum(step, half_steps - 1)),
                ),
                pl.BlockSpec(
                    (3, width, LANES),
                    lambda step, core_ref: (0, 0, jnp.maximum(step - half_steps, 0)),
                ),
            ],
            out_specs=pl.BlockSpec((2, blob, LANES), out_map),
            scratch_shapes=[pltpu.VMEM((rows, width), jnp.bfloat16)],
        ),
        compiler_params=pltpu.CompilerParams(vmem_limit_bytes=VMEM_LIMIT),
    )(core, vox, gain, ids, own_weight, other_weight)


def read_ids(ref, index, rows):
    tile = ref[index, rows : rows + ID_ROWS].astype(jnp.float32)
    return tile[:8] * 256.0 + tile[8:]


def window_kernel(mine_ref, theirs_ref, out_ref):
    source = pl.program_id(0)
    sources = mine_ref.shape[0]
    packed = out_ref.shape[1]
    rows = 2 * packed
    groups = rows // LANES
    low_packed = low_lanes((packed, LANES))
    wire = mine_ref[source, rows + ID_ROWS :].astype(jnp.float32)
    query = jnp.concatenate(
        [jnp.where(low_packed, wire, 0.0), jnp.where(low_packed, swap_halves(wire), 0.0)], axis=0
    ).astype(jnp.bfloat16)
    columns = jnp.transpose(read_ids(mine_ref, source, rows))
    query_ids = jnp.concatenate([columns[:, g : g + 1] for g in range(groups)], axis=0)

    def fold(ref, index, state):
        sums, total = state
        keyval = ref[index, :rows]
        key_ids = read_ids(ref, index, rows)
        scores = lax.dot_general(
            query, keyval, (((1,), (1,)), ((), ())), preferred_element_type=jnp.float32
        )
        weights = [
            jnp.where(
                query_ids == key_ids[g : g + 1],
                jnp.exp(scores[:, g * LANES : (g + 1) * LANES]),
                0.0,
            )
            for g in range(groups)
        ]
        sums = functools.reduce(jnp.add, weights, sums)
        rounded = jnp.concatenate([part.astype(jnp.bfloat16) for part in weights], axis=1)
        return sums, total + jnp.dot(rounded, keyval, preferred_element_type=jnp.float32)

    def body(index, state):
        return fold(theirs_ref, index, fold(mine_ref, index, state))

    nothing = jnp.zeros((rows, LANES), jnp.float32)
    sums, total = lax.fori_loop(0, sources, body, (nothing, nothing))
    mixed = total / jnp.sum(sums, axis=-1, keepdims=True)
    out_ref[0] = jnp.where(low_packed, swap_halves(mixed[:packed]), mixed[packed:]).astype(
        jnp.bfloat16
    )


def window_mixing(mine, theirs, packed):
    sources, blob, _ = mine.shape
    return pl.pallas_call(
        window_kernel,
        out_shape=jax.ShapeDtypeStruct((sources, packed, LANES), jnp.bfloat16),
        grid=(sources,),
        in_specs=[
            pl.BlockSpec(mine.shape, lambda source: (0, 0, 0)),
            pl.BlockSpec(theirs.shape, lambda source: (0, 0, 0)),
        ],
        out_specs=pl.BlockSpec((1, packed, LANES), lambda source: (source, 0, 0)),
        compiler_params=pltpu.CompilerParams(vmem_limit_bytes=VMEM_LIMIT),
        cost_estimate=pl.CostEstimate(
            flops=32 * LANES * (sources * packed) ** 2,
            transcendentals=8 * (sources * packed) ** 2,
            bytes_accessed=2 * (mine.size + theirs.size),
        ),
    )(mine, theirs)


def cross_kernel(query_ref, keyval_ref, out_ref, score_ref):
    rows, local_width = query_ref.shape
    tokens = keyval_ref.shape[0]
    chunk = math.gcd(tokens, 512)
    low = low_lanes((rows, LANES))
    zero = jnp.zeros((), jnp.bfloat16)

    def lane_groups(values):
        return [values[:, g : g + LANES] for g in range(0, chunk, LANES)]

    for pair in range(0, local_width, LANES):
        mixes = []
        for head in range(2):
            query = jnp.where(low == (head == 0), query_ref[:, pair : pair + LANES], zero)
            peak = jnp.full((rows, LANES), -jnp.inf, jnp.float32)
            for start in range(0, tokens, chunk):
                scores = lax.dot_general(
                    query,
                    keyval_ref[start : start + chunk, pair : pair + LANES],
                    (((1,), (1,)), ((), ())),
                    preferred_element_type=jnp.float32,
                )
                score_ref[head, :, start : start + chunk] = scores
                peak = functools.reduce(jnp.maximum, lane_groups(scores), peak)
            row_max = jnp.max(peak, axis=-1, keepdims=True)
            sums = jnp.zeros((rows, LANES), jnp.float32)
            total = jnp.zeros((rows, LANES), jnp.float32)
            for start in range(0, tokens, chunk):
                weights = jnp.exp(score_ref[head, :, start : start + chunk] - row_max)
                sums = functools.reduce(jnp.add, lane_groups(weights), sums)
                total = total + jnp.dot(
                    weights.astype(jnp.bfloat16),
                    keyval_ref[
                        start : start + chunk, local_width + pair : local_width + pair + LANES
                    ],
                    preferred_element_type=jnp.float32,
                )
            mixes.append(total / jnp.sum(sums, axis=-1, keepdims=True))
        out_ref[:, pair : pair + LANES] = jnp.where(low, mixes[0], mixes[1]).astype(jnp.bfloat16)


def cross_mixing(queries, keyval):
    rows, local_width = queries.shape
    tokens = keyval.shape[0]
    scored = rows * tokens * local_width // HD
    return pl.pallas_call(
        cross_kernel,
        out_shape=jax.ShapeDtypeStruct((rows, local_width), jnp.bfloat16),
        in_specs=[pl.BlockSpec(memory_space=pltpu.VMEM)] * 2,
        out_specs=pl.BlockSpec(memory_space=pltpu.VMEM),
        scratch_shapes=[pltpu.VMEM((2, rows, tokens), jnp.float32)],
        compiler_params=pltpu.CompilerParams(vmem_limit_bytes=VMEM_LIMIT),
        cost_estimate=pl.CostEstimate(
            flops=8 * LANES * scored,
            transcendentals=scored,
            bytes_accessed=2 * (keyval.size + 2 * queries.size),
        ),
    )(queries, keyval)


def swap(array, pairs):
    return lax.ppermute(array, "mp", pairs)


def by_head(
    voxels,
    destination,
    cond,
    norm_gain,
    qkv_weight,
    self_out_weight,
    cross_norm_gain,
    cross_q_weight,
    cond_kv_weight,
    cross_out_weight,
):
    model_index = lax.axis_index("mp")
    core = model_index % 2
    chip = model_index // 2
    row_count, width = voxels.shape
    local_width = qkv_weight.shape[2]
    share = row_count // 4
    rows = 2 * share
    head_count = 2 * local_width // HD

    other_qkv = swap(qkv_weight, CORE_SWAP)
    cond_pair = [
        jnp.dot(cond, cond_kv_weight[part], preferred_element_type=jnp.float32).astype(jnp.bfloat16)
        for part in range(2)
    ]
    own_keyval = lax.all_gather(jnp.concatenate(cond_pair, axis=1), "seq", axis=0, tiled=True)

    vox = lax.dynamic_index_in_dim(
        voxels.reshape(2, 2, share, width), core, axis=1, keepdims=False
    ).reshape(rows, width)
    window_ids = (
        lax.dynamic_index_in_dim(
            destination.reshape(2, 2, share), core, axis=1, keepdims=False
        ).reshape(rows // LANES, LANES)
        // WBLK
    )
    blank = jnp.zeros((8 - rows // LANES, LANES), jnp.int32)
    ids = jnp.concatenate([window_ids // 256, blank, window_ids % 256, blank], axis=0).astype(
        jnp.bfloat16
    )
    sent = project(
        core.reshape(1).astype(jnp.int32), vox, norm_gain.reshape(1, width), ids, qkv_weight, other_qkv
    )

    chip_out = swap(jnp.concatenate([self_out_weight, cross_out_weight], axis=0), CHIP_SWAP)
    other_q = swap(cross_q_weight, CORE_SWAP)

    mine = lax.all_to_all(sent, "seq", split_axis=0, concat_axis=0, tiled=True)
    theirs = swap(mine[:, : rows + ID_ROWS], CORE_SWAP)
    mixed = window_mixing(mine, theirs, share)
    returned = lax.all_to_all(mixed, "seq", split_axis=0, concat_axis=0, tiled=True)
    near_mix = (
        returned.reshape(head_count, share, 2, HD).transpose(2, 1, 0, 3).reshape(rows, head_count * HD)
    )
    far_mix = swap(near_mix, CHIP_SWAP)
    own_keyval, chip_out, _ = lax.optimization_barrier((own_keyval, chip_out, mixed))

    own_out = jnp.concatenate([self_out_weight, cross_out_weight], axis=0)
    own_other_out = swap(own_out, CORE_SWAP)
    chip_other_out = swap(chip_out, CORE_SWAP)
    split = self_out_weight.shape[0]

    def in_order(first, second):
        return jnp.where(
            core == 0,
            jnp.concatenate([first[:split], second[:split]], axis=0),
            jnp.concatenate([second[:split], first[:split]], axis=0),
        )

    summed = jnp.dot(
        near_mix, in_order(own_out, own_other_out), preferred_element_type=jnp.float32
    ) + jnp.dot(far_mix, in_order(chip_out, chip_other_out), preferred_element_type=jnp.float32)
    hidden = vox.astype(jnp.float32) + summed
    spread = jnp.mean(hidden * hidden, axis=-1, keepdims=True)
    normed = (hidden * lax.rsqrt(spread + 1e-06) * cross_norm_gain).astype(jnp.bfloat16)
    own_hidden = lax.dynamic_slice_in_dim(hidden, chip * share, share, 0)

    def queries_of(weight):
        return (
            jnp.dot(normed, weight, preferred_element_type=jnp.float32).astype(jnp.bfloat16)
            * HD ** (-0.5)
        ).astype(jnp.bfloat16)

    other_keyval = swap(own_keyval, CORE_SWAP)
    own_cross = cross_mixing(queries_of(cross_q_weight), own_keyval)
    other_cross = cross_mixing(queries_of(other_q), other_keyval)
    both = jnp.concatenate([own_cross, other_cross], axis=1).reshape(2, share, 2 * local_width)
    kept = lax.dynamic_index_in_dim(both, chip, axis=0, keepdims=False)
    arrived = swap(lax.dynamic_index_in_dim(both, 1 - chip, axis=0, keepdims=False), CHIP_SWAP)
    near_out = jnp.concatenate([own_out[split:], own_other_out[split:]], axis=0)
    far_out = jnp.concatenate([chip_out[split:], chip_other_out[split:]], axis=0)
    crossed = jnp.dot(kept, near_out, preferred_element_type=jnp.float32) + jnp.dot(
        arrived, far_out, preferred_element_type=jnp.float32
    )
    return (own_hidden + crossed).astype(jnp.bfloat16)


def rms_norm(matrix, gain):
    values = matrix.astype(jnp.float32)
    spread = jnp.mean(values * values, axis=-1, keepdims=True)
    return (values * lax.rsqrt(spread + 1e-06) * gain).astype(jnp.bfloat16)


def window_attention(queries, keyset, valset, occupied, head_count):
    slot_count = queries.shape[0]
    window_count = slot_count // WBLK
    query_heads = queries.reshape(window_count, WBLK, head_count, HD)
    key_heads = keyset.reshape(window_count, WBLK, head_count, HD)
    value_heads = valset.reshape(window_count, WBLK, head_count, HD)
    scores = jnp.einsum(
        "wqhd,wkhd->whqk", query_heads, key_heads, preferred_element_type=jnp.float32
    ) * HD ** (-0.5)
    diagonal = (
        jnp.arange(WBLK, dtype=jnp.int32)[:, None] == jnp.arange(WBLK, dtype=jnp.int32)[None, :]
    )
    allowed = occupied.reshape(window_count, 1, WBLK) | diagonal[None]
    weights = jnp.where(allowed[:, None], jnp.exp(scores), 0.0)
    totals = jnp.sum(weights, axis=-1)
    mixed = jnp.einsum(
        "whqk,wkhd->wqhd",
        weights.astype(jnp.bfloat16),
        value_heads,
        preferred_element_type=jnp.float32,
    )
    mixed = mixed / jnp.transpose(totals, (0, 2, 1))[:, :, :, None]
    return mixed.astype(jnp.bfloat16).reshape(slot_count, head_count * HD)


def by_owner(
    voxels,
    destination,
    cond,
    norm_gain,
    qkv_weight,
    self_out_weight,
    cross_norm_gain,
    cross_q_weight,
    cond_kv_weight,
    cross_out_weight,
):
    peer_count = lax.axis_size("seq")
    part_count = lax.axis_size("mp")
    model_index = lax.axis_index("mp")
    row_count = voxels.shape[0]
    local_width = qkv_weight.shape[2]
    head_count = local_width // HD
    capacity = 2 * row_count // peer_count
    slot_count = peer_count * capacity
    owner_ids = destination // slot_count
    slot_ids = destination % slot_count
    matches = (owner_ids[:, None] == jnp.arange(peer_count, dtype=jnp.int32)[None, :]).astype(
        jnp.int32
    )
    within = jnp.sum(matches * (jnp.cumsum(matches, axis=0) - 1), axis=1)
    send_index = owner_ids * capacity + within
    normed = rms_norm(voxels, norm_gain)
    place_buffer = (
        jnp.full((slot_count,), slot_count, jnp.int32)
        .at[send_index]
        .set(slot_ids)
        .reshape(peer_count, capacity)
    )
    projected = jnp.einsum(
        "rd,cdh->rch", normed, qkv_weight, preferred_element_type=jnp.float32
    ).astype(jnp.bfloat16)
    send_buffer = (
        jnp.zeros((slot_count, 3 * local_width), jnp.bfloat16)
        .at[send_index]
        .set(projected.reshape(row_count, 3 * local_width))
    )
    received, places = (
        lax.all_to_all(
            send_buffer.reshape(peer_count, capacity, 3 * local_width),
            "seq",
            split_axis=0,
            concat_axis=0,
            tiled=True,
        ),
        lax.all_to_all(place_buffer, "seq", split_axis=0, concat_axis=0, tiled=True),
    )
    received = received.reshape(slot_count, 3 * local_width)
    places = places.reshape(slot_count)
    layout = (
        jnp.zeros((slot_count, 3 * local_width), jnp.bfloat16).at[places].set(received, mode="drop")
    )
    occupied = jnp.zeros((slot_count,), jnp.bool_).at[places].set(True, mode="drop")
    mixed = window_attention(
        layout[:, :local_width],
        layout[:, local_width : 2 * local_width],
        layout[:, 2 * local_width :],
        occupied,
        head_count,
    )
    outgoing = mixed[jnp.minimum(places, slot_count - 1)]
    returned = lax.all_to_all(
        outgoing.reshape(peer_count, capacity, local_width),
        "seq",
        split_axis=0,
        concat_axis=0,
        tiled=True,
    )
    window_mix = returned.reshape(slot_count, local_width)[send_index]
    row_share = row_count // part_count
    summed_out = lax.psum(
        jnp.dot(window_mix, self_out_weight, preferred_element_type=jnp.float32), "mp"
    )
    hidden = voxels.astype(jnp.float32) + summed_out
    normed2 = rms_norm(hidden, cross_norm_gain)
    own_hidden = lax.dynamic_slice_in_dim(hidden, model_index * row_share, row_share, 0)
    cross_query = (
        jnp.dot(normed2, cross_q_weight, preferred_element_type=jnp.float32)
        .astype(jnp.bfloat16)
        .reshape(row_count, head_count, HD)
    )
    cond_pair = jnp.einsum(
        "td,cdh->cth", cond, cond_kv_weight, preferred_element_type=jnp.float32
    ).astype(jnp.bfloat16)

    def fold_block(running, key_block, value_block):
        row_max, totals, mixed_sum = running
        scores = jnp.einsum(
            "qhd,khd->qhk", cross_query, key_block, preferred_element_type=jnp.float32
        ) * HD ** (-0.5)
        new_max = jnp.maximum(row_max, jnp.max(scores, axis=-1))
        rescale = jnp.exp(row_max - new_max)
        weights = jnp.exp(scores - new_max[:, :, None])
        totals = totals * rescale + jnp.sum(weights, axis=-1)
        update = jnp.einsum(
            "qhk,khd->qhd",
            weights.astype(jnp.bfloat16),
            value_block,
            preferred_element_type=jnp.float32,
        )
        return (new_max, totals, mixed_sum * rescale[:, :, None] + update)

    start_state = (
        jnp.full((row_count, head_count), -1e30, jnp.float32),
        jnp.zeros((row_count, head_count), jnp.float32),
        jnp.zeros((row_count, head_count, HD), jnp.float32),
    )
    key_piece = lax.all_gather(cond_pair[0], "seq", axis=0, tiled=True)
    value_piece = lax.all_gather(cond_pair[1], "seq", axis=0, tiled=True)
    token_count = key_piece.shape[0]
    sub_block = math.gcd(token_count, 512)
    key_blocks = key_piece.reshape(token_count // sub_block, sub_block, head_count, HD)
    value_blocks = value_piece.reshape(token_count // sub_block, sub_block, head_count, HD)

    def advance(state, operands):
        return (fold_block(state, operands[0], operands[1]), None)

    folded, unused = lax.scan(advance, start_state, (key_blocks, value_blocks))
    row_max, totals, mixed_sum = folded
    cross_mix = (
        (mixed_sum / totals[:, :, None]).astype(jnp.bfloat16).reshape(row_count, local_width)
    )
    cross_sum = lax.psum_scatter(
        jnp.dot(cross_mix, cross_out_weight, preferred_element_type=jnp.float32),
        "mp",
        scatter_dimension=0,
        tiled=True,
    )
    return (own_hidden + cross_sum).astype(jnp.bfloat16)


def solution(mesh):
    heads_match = mesh.shape["mp"] == 4 and mesh.shape["seq"] == 8
    return jax.shard_map(
        by_head if heads_match else by_owner,
        mesh=mesh,
        in_specs=(
            P("seq", None),
            P("seq"),
            P("seq", None),
            P(),
            P(None, None, "mp"),
            P("mp", None),
            P(),
            P(None, "mp"),
            P(None, None, "mp"),
            P("mp", None),
        ),
        out_specs=P(("seq", "mp"), None),
        check_vma=False,
    )
```

```python
import functools
import math

import jax
import jax.numpy as jnp
from jax import lax
from jax.experimental import pallas as pl
from jax.experimental.pallas import tpu as pltpu
from jax.sharding import PartitionSpec as P

HD = 64
WBLK = 64
LANES = 128
ID_ROWS = 16
VMEM_LIMIT = 48 * 1024 * 1024
CORE_SWAP = ((0, 1), (1, 0), (2, 3), (3, 2))
CHIP_SWAP = ((0, 2), (2, 0), (1, 3), (3, 1))
SIDE_SWAP = tuple((i, i ^ 1) for i in range(8))
NEXT_SWAP = tuple((i, i ^ 2) for i in range(8))
SKIP_SWAP = tuple((i, i ^ 4) for i in range(8))


def low_lanes(shape):
    return lax.broadcasted_iota(jnp.int32, shape, 1) < HD


def swap_halves(values):
    return pltpu.roll(values, HD, 1)


def columns_of(row):
    return jnp.transpose(jnp.broadcast_to(row, (LANES, LANES)))


def one_hot(condition):
    return jnp.where(condition, 1.0, 0.0).astype(jnp.bfloat16)


def project_kernel(
    core_ref, vox_ref, gain_ref, place_ref, own_ref, other_ref, out_ref, rank_ref, normed_ref, ids_ref
):
    step = pl.program_id(0)
    rows = normed_ref.shape[0]
    packed = rows // 2
    groups = place_ref.shape[0]

    @pl.when(step == 0)
    def _():
        places = place_ref[...].astype(jnp.float32)
        place_rows = [places[g : g + 1] for g in range(groups)]
        place_columns = [columns_of(row) for row in place_rows]
        blank = jnp.zeros((8 - groups, LANES), jnp.float32)
        lane = lax.broadcasted_iota(jnp.int32, (LANES, LANES), 1).astype(jnp.float32)
        rank_rows = [
            sum(
                jnp.sum(jnp.where(column < row, 1.0, 0.0), axis=0, keepdims=True)
                for column in place_columns
            )
            for row in place_rows
        ]
        rank_columns = [
            jnp.sum(sum(jnp.where(row < column, 1.0, 0.0) for row in place_rows), axis=1, keepdims=True)
            for column in place_columns
        ]
        window_rows = [
            jnp.floor(
                sum(
                    jnp.sum(
                        jnp.where(rank == lane + float(g * LANES), column, 0.0), axis=0, keepdims=True
                    )
                    for rank, column in zip(rank_columns, place_columns)
                )
                * (1.0 / WBLK)
            )
            for g in range(groups)
        ]
        windows = jnp.concatenate(window_rows + [blank], axis=0)
        high = jnp.floor(windows * (1.0 / 256.0))
        ids_ref[...] = jnp.concatenate([high, windows - 256.0 * high], axis=0).astype(jnp.bfloat16)
        rank_ref[...] = jnp.concatenate(rank_rows + [blank], axis=0)
        wanted = (lax.broadcasted_iota(jnp.int32, (rows, LANES), 0) + core_ref[0] * rows).astype(
            jnp.float32
        )
        order = jnp.concatenate([one_hot(row == wanted) for row in rank_rows], axis=1)
        values = jnp.dot(order, vox_ref[...], preferred_element_type=jnp.float32)
        spread = jnp.mean(values * values, axis=-1, keepdims=True)
        normed_ref[...] = (values * lax.rsqrt(spread + 1e-06) * gain_ref[...]).astype(jnp.bfloat16)

    def emit(weight_ref):
        normed = normed_ref[...]
        low = low_lanes((rows, LANES))
        low_packed = low_lanes((packed, LANES))
        query, key, value = (
            jnp.dot(normed, weight_ref[part], preferred_element_type=jnp.float32)
            for part in range(3)
        )
        query = query * HD ** (-0.5)
        first, second = query[:packed], query[packed:]
        pairs = (
            (
                jnp.where(low, key, swap_halves(value)),
                jnp.where(low_packed, first, swap_halves(second)),
            ),
            (
                jnp.where(low, swap_halves(key), value),
                jnp.where(low_packed, swap_halves(first), second),
            ),
        )
        for head, (keyval, queries) in enumerate(pairs):
            out_ref[head, :rows] = keyval.astype(jnp.bfloat16)
            out_ref[head, rows : rows + ID_ROWS] = ids_ref[...]
            out_ref[head, rows + ID_ROWS :] = queries.astype(jnp.bfloat16)

    @pl.when(step < 2)
    def _():
        emit(own_ref)

    @pl.when(step >= 2)
    def _():
        emit(other_ref)


def project(core, vox, gain, places, own_weight, other_weight):
    row_count, width = vox.shape
    rows = row_count // 2
    local_width = own_weight.shape[2]
    heads = 2 * local_width // HD
    pair_steps = heads // 2
    half_steps = pair_steps // 2
    blob = rows + ID_ROWS + rows // 2

    def out_map(step, core_ref):
        side = step // half_steps
        absolute = jnp.where(side == 0, core_ref[0], 1 - core_ref[0])
        return (absolute * half_steps + step % half_steps, 0, 0)

    def whole(step, core_ref):
        return (0, 0)

    return pl.pallas_call(
        project_kernel,
        out_shape=(
            jax.ShapeDtypeStruct((heads, blob, LANES), jnp.bfloat16),
            jax.ShapeDtypeStruct((8, LANES), jnp.float32),
        ),
        grid_spec=pltpu.PrefetchScalarGridSpec(
            num_scalar_prefetch=1,
            grid=(pair_steps,),
            in_specs=[
                pl.BlockSpec((row_count, width), whole),
                pl.BlockSpec((1, width), whole),
                pl.BlockSpec(places.shape, whole),
                pl.BlockSpec(
                    (3, width, LANES),
                    lambda step, core_ref: (0, 0, jnp.minimum(step, half_steps - 1)),
                ),
                pl.BlockSpec(
                    (3, width, LANES),
                    lambda step, core_ref: (0, 0, jnp.maximum(step - half_steps, 0)),
                ),
            ],
            out_specs=(pl.BlockSpec((2, blob, LANES), out_map), pl.BlockSpec((8, LANES), whole)),
            scratch_shapes=[
                pltpu.VMEM((rows, width), jnp.bfloat16),
                pltpu.VMEM((ID_ROWS, LANES), jnp.bfloat16),
            ],
        ),
        compiler_params=pltpu.CompilerParams(vmem_limit_bytes=VMEM_LIMIT),
    )(core, vox, gain, places, own_weight, other_weight)


def window_kernel(
    core_ref,
    first_ref,
    round_ref,
    mine_ref,
    theirs_ref,
    out_ref,
    key_ref,
    window_ref,
    sum_ref,
    total_ref,
    column_ref,
    query_ref,
):
    source = pl.program_id(0)
    sources = mine_ref.shape[0]
    packed = out_ref.shape[1]
    rows = 2 * packed
    blocks = rows // LANES
    last = 2 * rows // WBLK
    low_packed = low_lanes((packed, LANES))
    core = core_ref[0]

    @pl.when(source == 0)
    def _():
        low = low_lanes((8, LANES))
        real = lax.broadcasted_iota(jnp.int32, (8, LANES), 0) < 2 * blocks
        for index in range(sources):
            key_ref[index, pl.ds(pl.multiple_of(core * rows, LANES), rows)] = mine_ref[index, :rows]
            key_ref[index, pl.ds(pl.multiple_of((1 - core) * rows, LANES), rows)] = theirs_ref[index, :rows]
            key_ref[index, 2 * rows :] = jnp.zeros((2 * LANES, LANES), jnp.bfloat16)
            tile = mine_ref[index, rows : rows + ID_ROWS].astype(jnp.float32)
            even = jnp.where(real, tile[:8] * 256.0 + tile[8:], -1.0)
            window_ref[index, 0] = even
            window_ref[index, 1] = jnp.where(
                low, swap_halves(even), swap_halves(pltpu.roll(even, 7, 0))
            )

    wire = mine_ref[source, rows + ID_ROWS :].astype(jnp.float32)
    query = jnp.concatenate(
        [jnp.where(low_packed, wire, 0.0), jnp.where(low_packed, swap_halves(wire), 0.0)], axis=0
    ).astype(jnp.bfloat16)

    def fold(block, other, turn, query_part, query_ids, sums, total):
        first = first_ref[(source * blocks + block) * sources + other]
        start = jnp.minimum(first + 4 * turn, last)
        keyval = key_ref[other, pl.ds(pl.multiple_of(start * WBLK, WBLK), 2 * LANES)]
        scores = lax.dot_general(
            query_part, keyval, (((1,), (1,)), ((), ())), preferred_element_type=jnp.float32
        )
        weights = [
            jnp.where(
                query_ids == window_ref[other, start % 2, pl.ds(start // 2 + g, 1)],
                jnp.exp(scores[:, g * LANES : (g + 1) * LANES]),
                0.0,
            )
            for g in range(2)
        ]
        rounded = jnp.concatenate([part.astype(jnp.bfloat16) for part in weights], axis=1)
        return (
            sums + weights[0] + weights[1],
            total + jnp.dot(rounded, keyval, preferred_element_type=jnp.float32),
        )

    for block in range(blocks):
        query_part = query[block * LANES : (block + 1) * LANES]
        query_ids = columns_of(window_ref[source, 0, pl.ds(core * blocks + block, 1)])
        query_ref[block] = query_part
        column_ref[block] = query_ids
        sums = jnp.zeros((LANES, LANES), jnp.float32)
        total = jnp.zeros((LANES, LANES), jnp.float32)
        for other in range(sources):
            sums, total = fold(block, other, 0, query_part, query_ids, sums, total)
        sum_ref[block] = sums
        total_ref[block] = total

    def visit(index, carry):
        block, other = index // sources, index % sources

        def more(turn, carry):
            sum_ref[block], total_ref[block] = fold(
                block,
                other,
                turn,
                query_ref[block],
                column_ref[block],
                sum_ref[block],
                total_ref[block],
            )
            return carry

        return lax.fori_loop(1, round_ref[source * blocks * sources + index], more, carry)

    lax.fori_loop(0, blocks * sources, visit, 0)
    mixed = jnp.concatenate(
        [
            total_ref[block] / jnp.sum(sum_ref[block], axis=-1, keepdims=True)
            for block in range(blocks)
        ],
        axis=0,
    )
    out_ref[0] = jnp.where(low_packed, swap_halves(mixed[:packed]), mixed[packed:]).astype(
        jnp.bfloat16
    )


def window_mixing(core, mine, theirs, packed):
    sources = mine.shape[0]
    rows = 2 * packed
    blocks = rows // LANES
    tiles = mine[:, rows : rows + ID_ROWS].astype(jnp.float32)
    windows = tiles[:, : 2 * blocks] * 256.0 + tiles[:, 8 : 8 + 2 * blocks]
    key_low, key_high = windows[:, :, ::WBLK], windows[:, :, WBLK - 1 :: WBLK]
    own = lax.dynamic_slice_in_dim(windows, core[0] * blocks, blocks, 1)
    query_low, query_high = (own[:, :, at, None, None, None] for at in (0, LANES - 1))
    first = jnp.sum((key_high < query_low).astype(jnp.int32), axis=(-2, -1))
    beyond = jnp.sum((key_low <= query_high).astype(jnp.int32), axis=(-2, -1))
    rounds = (beyond - first + 3) // 4
    return pl.pallas_call(
        window_kernel,
        out_shape=jax.ShapeDtypeStruct((sources, packed, LANES), jnp.bfloat16),
        grid_spec=pltpu.PrefetchScalarGridSpec(
            num_scalar_prefetch=3,
            grid=(sources,),
            in_specs=[
                pl.BlockSpec(mine.shape, lambda source, *refs: (0, 0, 0)),
                pl.BlockSpec(theirs.shape, lambda source, *refs: (0, 0, 0)),
            ],
            out_specs=pl.BlockSpec((1, packed, LANES), lambda source, *refs: (source, 0, 0)),
            scratch_shapes=[
                pltpu.VMEM((sources, 2 * rows + 2 * LANES, LANES), jnp.bfloat16),
                pltpu.VMEM((sources, 2, 8, LANES), jnp.float32),
                pltpu.VMEM((blocks, LANES, LANES), jnp.float32),
                pltpu.VMEM((blocks, LANES, LANES), jnp.float32),
                pltpu.VMEM((blocks, LANES, LANES), jnp.float32),
                pltpu.VMEM((blocks, LANES, LANES), jnp.bfloat16),
            ],
        ),
        compiler_params=pltpu.CompilerParams(vmem_limit_bytes=VMEM_LIMIT),
        cost_estimate=pl.CostEstimate(
            flops=12 * LANES * (sources * packed) ** 2,
            transcendentals=2 * (sources * packed) ** 2,
            bytes_accessed=2 * (mine.size + theirs.size),
        ),
    )(core, first.reshape(-1), rounds.reshape(-1), mine, theirs)


def bridge_kernel(
    core_ref,
    chip_ref,
    rank_ref,
    vox_ref,
    gain_ref,
    near_ref,
    near_other_ref,
    far_ref,
    far_other_ref,
    weight_ref,
    other_weight_ref,
    chip_weight_ref,
    chip_other_weight_ref,
    query_weight_ref,
    other_query_weight_ref,
    hidden_ref,
    query_ref,
    other_query_ref,
    mix_ref,
    column_ref,
    kept_ref,
):
    share = hidden_ref.shape[0]
    rows = 2 * share
    core, chip = core_ref[0], chip_ref[0]
    low = low_lanes((share, LANES))
    heads = near_ref.shape[0]
    groups = 2 * rows // LANES
    for side, (own, other) in enumerate(((near_ref, near_other_ref), (far_ref, far_other_ref))):
        for half, ref in enumerate((own, other)):
            offset = pl.multiple_of((core if half == 0 else 1 - core) * rows, LANES)
            for pair in range(heads // 2):
                holder = core if pair < heads // 4 else 1 - core
                head = holder * (heads // 2) + (pair % (heads // 4)) * 2
                first, second = ref[head].astype(jnp.float32), ref[head + 1].astype(jnp.float32)
                at = (side * heads // 2 + pair) * LANES
                mix_ref[pl.ds(offset, share), at : at + LANES] = jnp.where(
                    low, first, swap_halves(second)
                ).astype(jnp.bfloat16)
                mix_ref[pl.ds(offset + share, share), at : at + LANES] = jnp.where(
                    low, swap_halves(first), second
                ).astype(jnp.bfloat16)
    for group in range(groups):
        column_ref[group * LANES : (group + 1) * LANES] = columns_of(rank_ref[group : group + 1])
    begin = pl.multiple_of(core * share, 64)
    ranks = jnp.concatenate(
        [column_ref[pl.ds(begin, share)], column_ref[pl.ds(begin + rows, share)]], axis=0
    )
    lane = lax.broadcasted_iota(jnp.int32, (rows, LANES), 1).astype(jnp.float32)
    order = jnp.concatenate(
        [one_hot(ranks == lane + float(group * LANES)) for group in range(groups)], axis=1
    )
    mix = jnp.dot(order, mix_ref[...], preferred_element_type=jnp.float32).astype(jnp.bfloat16)
    hidden = jnp.concatenate(
        [vox_ref[pl.ds(begin, share)], vox_ref[pl.ds(begin + rows, share)]], axis=0
    ).astype(jnp.float32)
    depth = weight_ref.shape[0]
    refs = (weight_ref, other_weight_ref, chip_weight_ref, chip_other_weight_ref)
    summed = sum(
        jnp.dot(mix[:, i * depth : (i + 1) * depth], ref[...], preferred_element_type=jnp.float32)
        for i, ref in enumerate(refs)
    )
    hidden = hidden + summed
    kept_ref[...] = hidden
    hidden_ref[...] = kept_ref[pl.ds(pl.multiple_of(chip * share, 64), share)]
    spread = jnp.mean(hidden * hidden, axis=-1, keepdims=True)
    normed = (hidden * lax.rsqrt(spread + 1e-06) * gain_ref[...]).astype(jnp.bfloat16)
    for ref, out in (
        (query_weight_ref, query_ref),
        (other_query_weight_ref, other_query_ref),
    ):
        queries = jnp.dot(normed, ref[...], preferred_element_type=jnp.float32)
        out[...] = (queries.astype(jnp.bfloat16).astype(jnp.float32) * HD ** (-0.5)).astype(
            jnp.bfloat16
        )


def bridge(core, chip, ranks, voxels, gain, mixes, weights, query_weights):
    row_count, width = voxels.shape
    rows = row_count // 2
    share = rows // 2
    local_width = query_weights[0].shape[1]
    scalar = pl.BlockSpec(memory_space=pltpu.SMEM)

    def whole(array):
        return pl.BlockSpec(array.shape, lambda step: (0,) * array.ndim)

    operands = (ranks, voxels, gain, *mixes, *weights, *query_weights)
    specs = [whole(array) for array in operands]
    specs[7:11] = [pl.BlockSpec((width // 4, width), lambda step: (0, 0))] * 4
    outs = (
        jax.ShapeDtypeStruct((share, width), jnp.float32),
        jax.ShapeDtypeStruct((rows, local_width), jnp.bfloat16),
        jax.ShapeDtypeStruct((rows, local_width), jnp.bfloat16),
    )
    return pl.pallas_call(
        bridge_kernel,
        out_shape=outs,
        grid=(1,),
        in_specs=[scalar, scalar] + specs,
        out_specs=tuple(whole(out) for out in outs),
        scratch_shapes=[
            pltpu.VMEM((row_count, width), jnp.bfloat16),
            pltpu.VMEM((row_count, LANES), jnp.float32),
            pltpu.VMEM((rows, width), jnp.float32),
        ],
        compiler_params=pltpu.CompilerParams(vmem_limit_bytes=VMEM_LIMIT),
        cost_estimate=pl.CostEstimate(
            flops=8 * rows * width * width, transcendentals=rows, bytes_accessed=8 * width * width
        ),
    )(core, chip, *operands)


def cross_kernel(query_ref, *refs):
    piece_refs, out_ref, score_ref = refs[:-2], refs[-2], refs[-1]
    rows, local_width = query_ref.shape
    low = low_lanes((rows, LANES))
    zero = jnp.zeros((), jnp.bfloat16)
    chunk = piece_refs[0].shape[0]

    def lane_groups(values):
        return [values[:, g : g + LANES] for g in range(0, chunk, LANES)]

    for pair in range(0, local_width, LANES):
        mixes = []
        for head in range(2):
            query = jnp.where(low == (head == 0), query_ref[:, pair : pair + LANES], zero)
            peak = jnp.full((rows, LANES), -jnp.inf, jnp.float32)
            for index, ref in enumerate(piece_refs):
                scores = lax.dot_general(
                    query,
                    ref[:, pair : pair + LANES],
                    (((1,), (1,)), ((), ())),
                    preferred_element_type=jnp.float32,
                )
                score_ref[head, :, index * chunk : (index + 1) * chunk] = scores
                peak = functools.reduce(jnp.maximum, lane_groups(scores), peak)
            row_max = jnp.max(peak, axis=-1, keepdims=True)
            sums = jnp.zeros((rows, LANES), jnp.float32)
            total = jnp.zeros((rows, LANES), jnp.float32)
            for index, ref in enumerate(piece_refs):
                weights = jnp.exp(
                    score_ref[head, :, index * chunk : (index + 1) * chunk] - row_max
                )
                sums = functools.reduce(jnp.add, lane_groups(weights), sums)
                total = total + jnp.dot(
                    weights.astype(jnp.bfloat16),
                    ref[:, local_width + pair : local_width + pair + LANES],
                    preferred_element_type=jnp.float32,
                )
            mixes.append(total / jnp.sum(sums, axis=-1, keepdims=True))
        out_ref[:, pair : pair + LANES] = jnp.where(low, mixes[0], mixes[1]).astype(jnp.bfloat16)


def cross_mixing(queries, pieces):
    rows, local_width = queries.shape
    tokens = sum(piece.shape[0] for piece in pieces)
    scored = rows * tokens * local_width // HD
    return pl.pallas_call(
        cross_kernel,
        out_shape=jax.ShapeDtypeStruct((rows, local_width), jnp.bfloat16),
        in_specs=[pl.BlockSpec(memory_space=pltpu.VMEM)] * (1 + len(pieces)),
        out_specs=pl.BlockSpec(memory_space=pltpu.VMEM),
        scratch_shapes=[pltpu.VMEM((2, rows, tokens), jnp.float32)],
        compiler_params=pltpu.CompilerParams(vmem_limit_bytes=VMEM_LIMIT),
        cost_estimate=pl.CostEstimate(
            flops=8 * LANES * scored,
            transcendentals=scored,
            bytes_accessed=4 * (tokens * local_width + queries.size),
        ),
    )(queries, *pieces)


def finish_kernel(base_ref, mix_ref, weight_ref, out_ref):
    out_ref[...] = (
        base_ref[...] + jnp.dot(mix_ref[...], weight_ref[...], preferred_element_type=jnp.float32)
    ).astype(jnp.bfloat16)


def finish(base, mix, pair):
    def whole(array):
        return pl.BlockSpec(array.shape, lambda step: (0, 0))

    return pl.pallas_call(
        finish_kernel,
        out_shape=jax.ShapeDtypeStruct(base.shape, jnp.bfloat16),
        grid=(1,),
        in_specs=[
            whole(base),
            whole(mix),
            pl.BlockSpec((pair.shape[0] // 2, pair.shape[1]), lambda step: (1, 0)),
        ],
        out_specs=whole(base),
        compiler_params=pltpu.CompilerParams(vmem_limit_bytes=VMEM_LIMIT),
    )(base, mix, pair)


def swap(array, pairs):
    return lax.ppermute(array, "mp", pairs)


def across(array, pairs):
    return lax.ppermute(array, "seq", pairs)


def by_head(
    voxels,
    destination,
    cond,
    norm_gain,
    qkv_weight,
    self_out_weight,
    cross_norm_gain,
    cross_q_weight,
    cond_kv_weight,
    cross_out_weight,
):
    model_index = lax.axis_index("mp").astype(jnp.int32)
    core = (model_index % 2).reshape(1)
    chip = (model_index // 2).reshape(1)
    row_count, width = voxels.shape
    rows = row_count // 2
    share = rows // 2
    depth = self_out_weight.shape[0]

    other_qkv = swap(qkv_weight, CORE_SWAP)
    cond_pair = [
        jnp.dot(cond, cond_kv_weight[part], preferred_element_type=jnp.float32).astype(jnp.bfloat16)
        for part in range(2)
    ]
    own_piece = jnp.concatenate(cond_pair, axis=1)
    voxels, own_piece = lax.optimization_barrier((voxels, own_piece))
    sent, ranks = project(
        core,
        voxels,
        norm_gain.reshape(1, width),
        destination.reshape(row_count // LANES, LANES),
        qkv_weight,
        other_qkv,
    )

    out_pair = jnp.concatenate([self_out_weight, cross_out_weight], axis=0)
    chip_pair = swap(out_pair, CHIP_SWAP)
    other_pair = swap(out_pair, CORE_SWAP)
    other_query_weight = swap(cross_q_weight, CORE_SWAP)
    side_piece = across(own_piece, SIDE_SWAP)
    next_piece = across(own_piece, NEXT_SWAP)

    sent, side_piece, next_piece = lax.optimization_barrier((sent, side_piece, next_piece))
    mine = lax.all_to_all(sent, "seq", split_axis=0, concat_axis=0, tiled=True)
    theirs = swap(mine, CORE_SWAP)
    late_piece, _ = lax.optimization_barrier((own_piece, mine))
    skip_piece = across(late_piece, SKIP_SWAP)
    next_side_piece = across(next_piece, SIDE_SWAP)
    mixed = window_mixing(core, mine, theirs, share)
    mixed, skip_piece, next_side_piece, chip_pair = lax.optimization_barrier(
        (mixed, skip_piece, next_side_piece, chip_pair)
    )
    chip_other_pair = swap(chip_pair, CORE_SWAP)
    last_piece = across(skip_piece, NEXT_SWAP)
    skip_side_piece = across(skip_piece, SIDE_SWAP)
    near = lax.all_to_all(mixed, "seq", split_axis=0, concat_axis=0, tiled=True)
    far = swap(near, CHIP_SWAP)
    near_other = swap(near, CORE_SWAP)
    far, last_piece, skip_side_piece = lax.optimization_barrier((far, last_piece, skip_side_piece))
    last_side_piece = across(last_piece, SIDE_SWAP)
    far_other = swap(far, CORE_SWAP)
    pieces = [
        own_piece,
        side_piece,
        next_piece,
        next_side_piece,
        skip_piece,
        skip_side_piece,
        last_piece,
        last_side_piece,
    ]
    pairs = (out_pair, other_pair, chip_pair, chip_other_pair)
    own_hidden, own_query, other_query = bridge(
        core,
        chip,
        ranks,
        voxels,
        cross_norm_gain.reshape(1, width),
        (near, near_other, far, far_other),
        pairs,
        (cross_q_weight, other_query_weight),
    )

    asked = swap(other_query, CORE_SWAP)
    answered = swap(cross_mixing(asked, pieces), CORE_SWAP)

    def exchanged(mix):
        halves = mix.reshape(2, share, mix.shape[1])
        kept, leaving = (
            lax.dynamic_index_in_dim(halves, at, 0, keepdims=False) for at in (chip[0], 1 - chip[0])
        )
        return kept, swap(leaving, CHIP_SWAP)

    other_kept, other_arrived = exchanged(answered)
    own_kept, own_arrived = exchanged(cross_mixing(own_query, pieces))
    crossed = own_hidden
    for part, pair in (
        (other_kept, other_pair),
        (other_arrived, chip_other_pair),
        (own_kept, out_pair),
    ):
        crossed = crossed + jnp.dot(part, pair[depth:], preferred_element_type=jnp.float32)
    return finish(crossed, own_arrived, chip_pair)


def rms_norm(matrix, gain):
    values = matrix.astype(jnp.float32)
    spread = jnp.mean(values * values, axis=-1, keepdims=True)
    return (values * lax.rsqrt(spread + 1e-06) * gain).astype(jnp.bfloat16)


def window_attention(queries, keyset, valset, occupied, head_count):
    slot_count = queries.shape[0]
    window_count = slot_count // WBLK
    query_heads = queries.reshape(window_count, WBLK, head_count, HD)
    key_heads = keyset.reshape(window_count, WBLK, head_count, HD)
    value_heads = valset.reshape(window_count, WBLK, head_count, HD)
    scores = jnp.einsum(
        "wqhd,wkhd->whqk", query_heads, key_heads, preferred_element_type=jnp.float32
    ) * HD ** (-0.5)
    diagonal = (
        jnp.arange(WBLK, dtype=jnp.int32)[:, None] == jnp.arange(WBLK, dtype=jnp.int32)[None, :]
    )
    allowed = occupied.reshape(window_count, 1, WBLK) | diagonal[None]
    weights = jnp.where(allowed[:, None], jnp.exp(scores), 0.0)
    totals = jnp.sum(weights, axis=-1)
    mixed = jnp.einsum(
        "whqk,wkhd->wqhd",
        weights.astype(jnp.bfloat16),
        value_heads,
        preferred_element_type=jnp.float32,
    )
    mixed = mixed / jnp.transpose(totals, (0, 2, 1))[:, :, :, None]
    return mixed.astype(jnp.bfloat16).reshape(slot_count, head_count * HD)


def by_owner(
    voxels,
    destination,
    cond,
    norm_gain,
    qkv_weight,
    self_out_weight,
    cross_norm_gain,
    cross_q_weight,
    cond_kv_weight,
    cross_out_weight,
):
    peer_count = lax.axis_size("seq")
    part_count = lax.axis_size("mp")
    model_index = lax.axis_index("mp")
    row_count = voxels.shape[0]
    local_width = qkv_weight.shape[2]
    head_count = local_width // HD
    capacity = 2 * row_count // peer_count
    slot_count = peer_count * capacity
    owner_ids = destination // slot_count
    slot_ids = destination % slot_count
    matches = (owner_ids[:, None] == jnp.arange(peer_count, dtype=jnp.int32)[None, :]).astype(
        jnp.int32
    )
    within = jnp.sum(matches * (jnp.cumsum(matches, axis=0) - 1), axis=1)
    send_index = owner_ids * capacity + within
    normed = rms_norm(voxels, norm_gain)
    place_buffer = (
        jnp.full((slot_count,), slot_count, jnp.int32)
        .at[send_index]
        .set(slot_ids)
        .reshape(peer_count, capacity)
    )
    projected = jnp.einsum(
        "rd,cdh->rch", normed, qkv_weight, preferred_element_type=jnp.float32
    ).astype(jnp.bfloat16)
    send_buffer = (
        jnp.zeros((slot_count, 3 * local_width), jnp.bfloat16)
        .at[send_index]
        .set(projected.reshape(row_count, 3 * local_width))
    )
    received, places = (
        lax.all_to_all(
            send_buffer.reshape(peer_count, capacity, 3 * local_width),
            "seq",
            split_axis=0,
            concat_axis=0,
            tiled=True,
        ),
        lax.all_to_all(place_buffer, "seq", split_axis=0, concat_axis=0, tiled=True),
    )
    received = received.reshape(slot_count, 3 * local_width)
    places = places.reshape(slot_count)
    layout = (
        jnp.zeros((slot_count, 3 * local_width), jnp.bfloat16).at[places].set(received, mode="drop")
    )
    occupied = jnp.zeros((slot_count,), jnp.bool_).at[places].set(True, mode="drop")
    mixed = window_attention(
        layout[:, :local_width],
        layout[:, local_width : 2 * local_width],
        layout[:, 2 * local_width :],
        occupied,
        head_count,
    )
    outgoing = mixed[jnp.minimum(places, slot_count - 1)]
    returned = lax.all_to_all(
        outgoing.reshape(peer_count, capacity, local_width),
        "seq",
        split_axis=0,
        concat_axis=0,
        tiled=True,
    )
    window_mix = returned.reshape(slot_count, local_width)[send_index]
    row_share = row_count // part_count
    summed_out = lax.psum(
        jnp.dot(window_mix, self_out_weight, preferred_element_type=jnp.float32), "mp"
    )
    hidden = voxels.astype(jnp.float32) + summed_out
    normed2 = rms_norm(hidden, cross_norm_gain)
    own_hidden = lax.dynamic_slice_in_dim(hidden, model_index * row_share, row_share, 0)
    cross_query = (
        jnp.dot(normed2, cross_q_weight, preferred_element_type=jnp.float32)
        .astype(jnp.bfloat16)
        .reshape(row_count, head_count, HD)
    )
    cond_pair = jnp.einsum(
        "td,cdh->cth", cond, cond_kv_weight, preferred_element_type=jnp.float32
    ).astype(jnp.bfloat16)

    def fold_block(running, key_block, value_block):
        row_max, totals, mixed_sum = running
        scores = jnp.einsum(
            "qhd,khd->qhk", cross_query, key_block, preferred_element_type=jnp.float32
        ) * HD ** (-0.5)
        new_max = jnp.maximum(row_max, jnp.max(scores, axis=-1))
        rescale = jnp.exp(row_max - new_max)
        weights = jnp.exp(scores - new_max[:, :, None])
        totals = totals * rescale + jnp.sum(weights, axis=-1)
        update = jnp.einsum(
            "qhk,khd->qhd",
            weights.astype(jnp.bfloat16),
            value_block,
            preferred_element_type=jnp.float32,
        )
        return (new_max, totals, mixed_sum * rescale[:, :, None] + update)

    start_state = (
        jnp.full((row_count, head_count), -1e30, jnp.float32),
        jnp.zeros((row_count, head_count), jnp.float32),
        jnp.zeros((row_count, head_count, HD), jnp.float32),
    )
    key_piece = lax.all_gather(cond_pair[0], "seq", axis=0, tiled=True)
    value_piece = lax.all_gather(cond_pair[1], "seq", axis=0, tiled=True)
    token_count = key_piece.shape[0]
    sub_block = math.gcd(token_count, 512)
    key_blocks = key_piece.reshape(token_count // sub_block, sub_block, head_count, HD)
    value_blocks = value_piece.reshape(token_count // sub_block, sub_block, head_count, HD)

    def advance(state, operands):
        return (fold_block(state, operands[0], operands[1]), None)

    folded, unused = lax.scan(advance, start_state, (key_blocks, value_blocks))
    row_max, totals, mixed_sum = folded
    cross_mix = (
        (mixed_sum / totals[:, :, None]).astype(jnp.bfloat16).reshape(row_count, local_width)
    )
    cross_sum = lax.psum_scatter(
        jnp.dot(cross_mix, cross_out_weight, preferred_element_type=jnp.float32),
        "mp",
        scatter_dimension=0,
        tiled=True,
    )
    return (own_hidden + cross_sum).astype(jnp.bfloat16)


def solution(mesh):
    heads_match = mesh.shape["mp"] == 4 and mesh.shape["seq"] == 8
    return jax.shard_map(
        by_head if heads_match else by_owner,
        mesh=mesh,
        in_specs=(
            P("seq", None),
            P("seq"),
            P("seq", None),
            P(),
            P(None, None, "mp"),
            P("mp", None),
            P(),
            P(None, "mp"),
            P(None, None, "mp"),
            P("mp", None),
        ),
        out_specs=P(("seq", "mp"), None),
        check_vma=False,
    )
```

```python
import functools
import math

import jax
import jax.numpy as jnp
from jax import lax
from jax.experimental import pallas as pl
from jax.experimental.pallas import tpu as pltpu
from jax.sharding import PartitionSpec as P

HD = 64
WBLK = 64
LANES = 128
ID_ROWS = 16
MEGA = 1024 * 1024
BATCH = 4
CORE_SWAP = ((0, 1), (1, 0), (2, 3), (3, 2))
CHIP_SWAP = ((0, 2), (2, 0), (1, 3), (3, 1))
SIDE_SWAP = tuple((i, i ^ 1) for i in range(8))
NEXT_SWAP = tuple((i, i ^ 2) for i in range(8))
SKIP_SWAP = tuple((i, i ^ 4) for i in range(8))


def low_lanes(shape):
    return lax.broadcasted_iota(jnp.int32, shape, 1) < HD


def swap_halves(values):
    return pltpu.roll(values, HD, 1)


def columns_of(row):
    return jnp.transpose(jnp.broadcast_to(row, (LANES, LANES)))


def one_hot(condition):
    return jnp.where(condition, 1.0, 0.0).astype(jnp.bfloat16)


def project_kernel(
    core_ref, vox_ref, gain_ref, place_ref, own_ref, other_ref, out_ref, rank_ref, normed_ref, ids_ref
):
    step = pl.program_id(0)
    rows = normed_ref.shape[0]
    packed = rows // 2
    groups = place_ref.shape[0]

    @pl.when(step == 0)
    def _():
        places = place_ref[...].astype(jnp.float32)
        place_rows = [places[g : g + 1] for g in range(groups)]
        place_columns = [columns_of(row) for row in place_rows]
        blank = jnp.zeros((8 - groups, LANES), jnp.float32)
        lane = lax.broadcasted_iota(jnp.int32, (LANES, LANES), 1).astype(jnp.float32)
        rank_rows = [
            sum(
                jnp.sum(jnp.where(column < row, 1.0, 0.0), axis=0, keepdims=True)
                for column in place_columns
            )
            for row in place_rows
        ]
        rank_columns = [
            jnp.sum(sum(jnp.where(row < column, 1.0, 0.0) for row in place_rows), axis=1, keepdims=True)
            for column in place_columns
        ]
        window_rows = [
            jnp.floor(
                sum(
                    jnp.sum(
                        jnp.where(rank == lane + float(g * LANES), column, 0.0), axis=0, keepdims=True
                    )
                    for rank, column in zip(rank_columns, place_columns)
                )
                * (1.0 / WBLK)
            )
            for g in range(groups)
        ]
        slot = lax.broadcasted_iota(jnp.int32, (1, LANES), 1)
        bounds = jnp.zeros((1, LANES), jnp.float32)
        for block in range(2 * groups):
            begin = (block % 2) * WBLK
            row = window_rows[block // 2]
            bounds = jnp.where(slot == block, row[:, begin : begin + 1], bounds)
            bounds = jnp.where(
                slot == block + 2 * groups, row[:, begin + WBLK - 1 : begin + WBLK], bounds
            )
        windows = jnp.concatenate(
            window_rows + [bounds] + [jnp.zeros_like(bounds)] * (7 - groups), axis=0
        )
        high = jnp.floor(windows * (1.0 / 256.0))
        ids_ref[...] = jnp.concatenate([high, windows - 256.0 * high], axis=0).astype(jnp.bfloat16)
        rank_ref[...] = jnp.concatenate(rank_rows + [blank], axis=0)
        wanted = (lax.broadcasted_iota(jnp.int32, (rows, LANES), 0) + core_ref[0] * rows).astype(
            jnp.float32
        )
        order = jnp.concatenate([one_hot(row == wanted) for row in rank_rows], axis=1)
        values = jnp.dot(order, vox_ref[...], preferred_element_type=jnp.float32)
        spread = jnp.mean(values * values, axis=-1, keepdims=True)
        normed_ref[...] = (values * lax.rsqrt(spread + 1e-06) * gain_ref[...]).astype(jnp.bfloat16)

    def emit(weight_ref):
        normed = normed_ref[...]
        low = low_lanes((rows, LANES))
        low_packed = low_lanes((packed, LANES))
        query, key, value = (
            jnp.dot(normed, weight_ref[part], preferred_element_type=jnp.float32)
            for part in range(3)
        )
        query = query * HD ** (-0.5)
        for at in range(0, weight_ref.shape[2], LANES):
            keys, values = key[:, at : at + LANES], value[:, at : at + LANES]
            first, second = query[:packed, at : at + LANES], query[packed:, at : at + LANES]
            pairs = (
                (
                    jnp.where(low, keys, swap_halves(values)),
                    jnp.where(low_packed, first, swap_halves(second)),
                ),
                (
                    jnp.where(low, swap_halves(keys), values),
                    jnp.where(low_packed, swap_halves(first), second),
                ),
            )
            for side, (keyval, queries) in enumerate(pairs):
                head = at // HD + side
                out_ref[head, :rows] = keyval.astype(jnp.bfloat16)
                out_ref[head, rows : rows + ID_ROWS] = ids_ref[...]
                out_ref[head, rows + ID_ROWS :] = queries.astype(jnp.bfloat16)

    @pl.when(step == 0)
    def _():
        emit(own_ref)

    @pl.when(step == 1)
    def _():
        emit(other_ref)


def project(core, vox, gain, places, own_weight, other_weight):
    row_count, width = vox.shape
    rows = row_count // 2
    local_width = own_weight.shape[2]
    heads = 2 * local_width // HD
    blob = rows + ID_ROWS + rows // 2

    def out_map(step, core_ref):
        return (jnp.where(step == 0, core_ref[0], 1 - core_ref[0]), 0, 0)

    def whole(step, core_ref):
        return (0, 0)

    return pl.pallas_call(
        project_kernel,
        out_shape=(
            jax.ShapeDtypeStruct((heads, blob, LANES), jnp.bfloat16),
            jax.ShapeDtypeStruct((8, LANES), jnp.float32),
        ),
        grid_spec=pltpu.PrefetchScalarGridSpec(
            num_scalar_prefetch=1,
            grid=(2,),
            in_specs=[
                pl.BlockSpec((row_count, width), whole),
                pl.BlockSpec((1, width), whole),
                pl.BlockSpec(places.shape, whole),
                pl.BlockSpec(own_weight.shape, lambda step, core_ref: (0, 0, 0)),
                pl.BlockSpec(own_weight.shape, lambda step, core_ref: (0, 0, 0)),
            ],
            out_specs=(pl.BlockSpec((heads // 2, blob, LANES), out_map), pl.BlockSpec((8, LANES), whole)),
            scratch_shapes=[
                pltpu.VMEM((rows, width), jnp.bfloat16),
                pltpu.VMEM((ID_ROWS, LANES), jnp.bfloat16),
            ],
        ),
        compiler_params=pltpu.CompilerParams(vmem_limit_bytes=28 * MEGA),
    )(core, vox, gain, places, own_weight, other_weight)


def window_kernel(
    core_ref,
    mine_ref,
    theirs_ref,
    out_ref,
    wire_ref,
    key_ref,
    window_ref,
    query_ref,
    column_ref,
    sum_ref,
    total_ref,
    plan_ref,
    plan_smem,
    late_smem,
    copy_sem,
):
    sources, packed, _ = out_ref.shape
    rows = 2 * packed
    blocks = rows // LANES
    last = 2 * rows // WBLK
    low_packed = low_lanes((packed, LANES))
    core = core_ref[0]

    low = low_lanes((8, LANES))
    real = lax.broadcasted_iota(jnp.int32, (8, LANES), 0) < 2 * blocks
    copies = [
        pltpu.make_async_copy(source, target, copy_sem.at[index])
        for index, (source, target) in enumerate(
            (
                (mine_ref.at[:, pl.ds(rows, ID_ROWS + packed)], wire_ref),
                (
                    mine_ref.at[:, pl.ds(0, rows)],
                    key_ref.at[:, pl.ds(pl.multiple_of(core * rows, LANES), rows)],
                ),
                (
                    theirs_ref.at[:, pl.ds(0, rows)],
                    key_ref.at[:, pl.ds(pl.multiple_of((1 - core) * rows, LANES), rows)],
                ),
            )
        )
    ]
    for copy in copies:
        copy.start()
    key_ref[:, 2 * rows :] = jnp.zeros((sources, 2 * LANES, LANES), jnp.bfloat16)
    copies[0].wait()
    bounds = []
    for index in range(sources):
        tile = wire_ref[index, :ID_ROWS].astype(jnp.float32)
        ids = tile[:8] * 256.0 + tile[8:]
        bounds.append(ids[2 * blocks : 2 * blocks + 1])
        even = jnp.where(real, ids, -1.0)
        window_ref[index, 0] = even
        window_ref[index, 1] = jnp.where(
            low, swap_halves(even), swap_halves(pltpu.roll(even, 7, 0))
        )

    bounds = jnp.concatenate(bounds, axis=0)
    slot = lax.broadcasted_iota(jnp.int32, (sources, LANES), 1)
    lows = jnp.where(slot < last, bounds, jnp.inf)
    highs = jnp.where(slot < last, pltpu.roll(bounds, LANES - last, 1), jnp.inf)
    begins = [
        jnp.where(core == 0, bounds[:, at : at + 1], bounds[:, at + last // 2 : at + last // 2 + 1])
        for at in range(0, last // 2, 2)
    ]
    ends = [
        jnp.where(core == 0, bounds[:, at : at + 1], bounds[:, at + last // 2 : at + last // 2 + 1])
        for at in range(last + 1, last + last // 2, 2)
    ]
    first = jnp.full((sources, LANES), float(last), jnp.float32)
    beyond = first
    for source in range(sources):
        for block in range(blocks):
            here = slot == source * blocks + block
            begin, end = (edges[block][source : source + 1] for edges in (begins, ends))
            first = jnp.where(
                here, jnp.sum(jnp.where(highs < begin, 1.0, 0.0), axis=1, keepdims=True), first
            )
            beyond = jnp.where(
                here, jnp.sum(jnp.where(lows <= end, 1.0, 0.0), axis=1, keepdims=True), beyond
            )
    plan_ref[0] = first.astype(jnp.int32)
    plan_ref[1] = jnp.floor((beyond - first + 3.0) * 0.25).astype(jnp.int32)
    plan_copy = pltpu.make_async_copy(plan_ref, plan_smem, copy_sem.at[3])
    plan_copy.start()
    plan_copy.wait()
    copies[1].wait()
    copies[2].wait()

    def fold(pair, other, turn, query_part, query_ids, sums, total):
        start = jnp.minimum(plan_smem[0, other, pair] + 4 * turn, last)
        keyval = key_ref[other, pl.ds(pl.multiple_of(start * WBLK, WBLK), 2 * LANES)]
        scores = lax.dot_general(
            query_part, keyval, (((1,), (1,)), ((), ())), preferred_element_type=jnp.float32
        )
        weights = [
            jnp.where(
                query_ids == window_ref[other, start % 2, pl.ds(start // 2 + g, 1)],
                jnp.exp(scores[:, g * LANES : (g + 1) * LANES]),
                0.0,
            )
            for g in range(2)
        ]
        rounded = jnp.concatenate([part.astype(jnp.bfloat16) for part in weights], axis=1)
        return (
            sums + weights[0] + weights[1],
            total + jnp.dot(rounded, keyval, preferred_element_type=jnp.float32),
        )

    def sweep(source, carry):
        wire = wire_ref[source, ID_ROWS:].astype(jnp.float32)
        query = jnp.concatenate(
            [jnp.where(low_packed, wire, 0.0), jnp.where(low_packed, swap_halves(wire), 0.0)],
            axis=0,
        ).astype(jnp.bfloat16)
        for block in range(blocks):
            at = source * blocks + block
            query_part = query[block * LANES : (block + 1) * LANES]
            query_ids = columns_of(window_ref[source, 0, pl.ds(core * blocks + block, 1)])
            query_ref[at] = query_part
            column_ref[at] = query_ids
            sums = jnp.zeros((LANES, LANES), jnp.float32)
            total = jnp.zeros((LANES, LANES), jnp.float32)
            for other in range(sources):
                sums, total = fold(at, other, 0, query_part, query_ids, sums, total)
            sum_ref[at] = sums
            total_ref[at] = total
        return carry

    lax.fori_loop(0, sources, sweep, 0)
    spare = sources * blocks
    query_ref[spare] = jnp.zeros((LANES, LANES), jnp.bfloat16)
    column_ref[spare] = jnp.zeros((LANES, LANES), jnp.float32)
    sum_ref[spare] = jnp.zeros((LANES, LANES), jnp.float32)
    total_ref[spare] = jnp.zeros((LANES, LANES), jnp.float32)

    count = jnp.int32(0)
    for other in range(sources):
        for at in range(sources * blocks):
            late_smem[count] = other * LANES + at
            count = count + jnp.where(plan_smem[1, other, at] > 1, 1, 0)
    for i in range(BATCH):
        late_smem[count + i] = spare

    def visit(index, carry):
        pairs = [late_smem[index * BATCH + i] for i in range(BATCH)]
        pairs = [(pair // LANES, pair % LANES) for pair in pairs]
        turns = functools.reduce(jnp.maximum, [plan_smem[1, other, at] for other, at in pairs])

        def more(turn, carry):
            for other, at in pairs:
                sum_ref[at], total_ref[at] = fold(
                    at, other, turn, query_ref[at], column_ref[at], sum_ref[at], total_ref[at]
                )
            return carry

        return lax.fori_loop(1, turns, more, carry)

    lax.fori_loop(0, (count + BATCH - 1) // BATCH, visit, 0)

    for source in range(sources):
        mixed = jnp.concatenate(
            [
                total_ref[at] / jnp.sum(sum_ref[at], axis=-1, keepdims=True)
                for at in range(source * blocks, (source + 1) * blocks)
            ],
            axis=0,
        )
        out_ref[source] = jnp.where(low_packed, swap_halves(mixed[:packed]), mixed[packed:]).astype(
            jnp.bfloat16
        )


def window_mixing(core, mine, theirs, packed):
    sources = mine.shape[0]
    rows = 2 * packed
    blocks = rows // LANES
    vmem = pl.BlockSpec(memory_space=pltpu.VMEM)
    smem = pl.BlockSpec(memory_space=pltpu.SMEM)
    return pl.pallas_call(
        window_kernel,
        out_shape=jax.ShapeDtypeStruct((sources, packed, LANES), jnp.bfloat16),
        in_specs=[smem] + [pl.BlockSpec(memory_space=pltpu.HBM)] * 2,
        out_specs=vmem,
        scratch_shapes=[
            pltpu.VMEM((sources, ID_ROWS + packed, LANES), jnp.bfloat16),
            pltpu.VMEM((sources, 2 * rows + 2 * LANES, LANES), jnp.bfloat16),
            pltpu.VMEM((sources, 2, 8, LANES), jnp.float32),
            pltpu.VMEM((sources * blocks + 1, LANES, LANES), jnp.bfloat16),
            pltpu.VMEM((sources * blocks + 1, LANES, LANES), jnp.float32),
            pltpu.VMEM((sources * blocks + 1, LANES, LANES), jnp.float32),
            pltpu.VMEM((sources * blocks + 1, LANES, LANES), jnp.float32),
            pltpu.VMEM((2, sources, LANES), jnp.int32),
            pltpu.SMEM((2, sources, LANES), jnp.int32),
            pltpu.SMEM((sources * sources * blocks + 2 * BATCH,), jnp.int32),
            pltpu.SemaphoreType.DMA((4,)),
        ],
        compiler_params=pltpu.CompilerParams(vmem_limit_bytes=24 * MEGA),
        cost_estimate=pl.CostEstimate(
            flops=80 * LANES * (sources * packed) ** 2,
            transcendentals=2 * (sources * packed) ** 2,
            bytes_accessed=2 * (mine.size + theirs.size),
        ),
    )(core, mine, theirs)


def fetch(refs, local_ref, copy_sem):
    copies = [
        pltpu.make_async_copy(ref, local_ref.at[index], copy_sem.at[index])
        for index, ref in enumerate(refs)
    ]
    for copy in copies:
        copy.start()
    return copies


def mix_heads(core, own_ref, other_ref, order, weight_ref, copies, mix_ref):
    heads, share, _ = own_ref.shape
    rows = 2 * share
    low = low_lanes((share, LANES))
    for half, ref in enumerate((own_ref, other_ref)):
        offset = pl.multiple_of((core if half == 0 else 1 - core) * rows, LANES)
        for pair in range(heads // 2):
            holder = core if pair < heads // 4 else 1 - core
            head = holder * (heads // 2) + (pair % (heads // 4)) * 2
            first, second = ref[head].astype(jnp.float32), ref[head + 1].astype(jnp.float32)
            at = pair * LANES
            mix_ref[pl.ds(offset, share), at : at + LANES] = jnp.where(
                low, first, swap_halves(second)
            ).astype(jnp.bfloat16)
            mix_ref[pl.ds(offset + share, share), at : at + LANES] = jnp.where(
                low, swap_halves(first), second
            ).astype(jnp.bfloat16)
    mix = jnp.dot(order, mix_ref[...], preferred_element_type=jnp.float32).astype(jnp.bfloat16)
    depth = weight_ref.shape[1]
    for copy in copies:
        copy.wait()
    return sum(
        jnp.dot(
            mix[:, i * depth : (i + 1) * depth], weight_ref[i], preferred_element_type=jnp.float32
        )
        for i in range(len(copies))
    )


def near_kernel(
    core_ref,
    rank_ref,
    vox_ref,
    own_ref,
    other_ref,
    weight_ref,
    other_weight_ref,
    hidden_ref,
    order_ref,
    token_ref,
    mix_ref,
    column_ref,
    local_ref,
    copy_sem,
):
    core = core_ref[0]
    copies = fetch((weight_ref, other_weight_ref), local_ref, copy_sem)
    token_ref[...] = jnp.zeros_like(token_ref)
    rows = hidden_ref.shape[0]
    share = rows // 2
    groups = 2 * rows // LANES
    for group in range(groups):
        column_ref[group * LANES : (group + 1) * LANES] = columns_of(rank_ref[group : group + 1])
    begin = pl.multiple_of(core * share, 64)
    ranks = jnp.concatenate(
        [column_ref[pl.ds(begin, share)], column_ref[pl.ds(begin + rows, share)]], axis=0
    )
    lane = lax.broadcasted_iota(jnp.int32, (rows, LANES), 1).astype(jnp.float32)
    order = jnp.concatenate(
        [one_hot(ranks == lane + float(group * LANES)) for group in range(groups)], axis=1
    )
    order_ref[...] = order
    values = jnp.concatenate(
        [vox_ref[pl.ds(begin, share)], vox_ref[pl.ds(begin + rows, share)]], axis=0
    ).astype(jnp.float32)
    hidden_ref[...] = values + mix_heads(
        core, own_ref, other_ref, order, local_ref, copies, mix_ref
    )


def far_kernel(
    core_ref,
    chip_ref,
    base_ref,
    order_ref,
    gain_ref,
    own_ref,
    other_ref,
    weight_ref,
    other_weight_ref,
    query_weight_ref,
    other_query_weight_ref,
    hidden_ref,
    query_ref,
    other_query_ref,
    mix_ref,
    kept_ref,
    local_ref,
    copy_sem,
    query_local_ref,
    query_sem,
):
    share = hidden_ref.shape[0]
    copies = fetch((weight_ref, other_weight_ref), local_ref, copy_sem)
    query_copies = fetch((query_weight_ref, other_query_weight_ref), query_local_ref, query_sem)
    hidden = base_ref[...] + mix_heads(
        core_ref[0], own_ref, other_ref, order_ref[...], local_ref, copies, mix_ref
    )
    kept_ref[...] = hidden
    hidden_ref[...] = kept_ref[pl.ds(pl.multiple_of(chip_ref[0] * share, 64), share)]
    spread = jnp.mean(hidden * hidden, axis=-1, keepdims=True)
    normed = (hidden * lax.rsqrt(spread + 1e-06) * gain_ref[...]).astype(jnp.bfloat16)
    for index, out in enumerate((query_ref, other_query_ref)):
        query_copies[index].wait()
        queries = jnp.dot(normed, query_local_ref[index], preferred_element_type=jnp.float32)
        out[...] = (queries.astype(jnp.bfloat16).astype(jnp.float32) * HD ** (-0.5)).astype(
            jnp.bfloat16
        )


def whole(array):
    return pl.BlockSpec(array.shape, lambda step: (0,) * array.ndim)


def near_part(core, ranks, voxels, mixes, weights):
    row_count, width = voxels.shape
    rows = row_count // 2
    heads = mixes[0].shape[0]
    outs = (
        jax.ShapeDtypeStruct((rows, width), jnp.float32),
        jax.ShapeDtypeStruct((rows, row_count), jnp.bfloat16),
        jax.ShapeDtypeStruct((8, LANES), jnp.float32),
    )
    return pl.pallas_call(
        near_kernel,
        out_shape=outs,
        grid=(1,),
        in_specs=[pl.BlockSpec(memory_space=pltpu.SMEM)]
        + [whole(array) for array in (ranks, voxels, *mixes)]
        + [pl.BlockSpec(memory_space=pltpu.HBM)] * len(weights),
        out_specs=tuple(whole(out) for out in outs),
        scratch_shapes=[
            pltpu.VMEM((row_count, heads * HD), jnp.bfloat16),
            pltpu.VMEM((row_count, LANES), jnp.float32),
            pltpu.VMEM((len(weights), *weights[0].shape), jnp.bfloat16),
            pltpu.SemaphoreType.DMA((len(weights),)),
        ],
        compiler_params=pltpu.CompilerParams(vmem_limit_bytes=24 * MEGA),
        cost_estimate=pl.CostEstimate(
            flops=10 * rows * width * width, transcendentals=0, bytes_accessed=8 * width * width
        ),
    )(core, ranks, voxels, *mixes, *weights)


def far_part(core, chip, base, order, gain, mixes, weights, query_weights):
    rows, width = base.shape
    share = rows // 2
    local_width = query_weights[0].shape[1]
    heads = mixes[0].shape[0]
    outs = (
        jax.ShapeDtypeStruct((share, width), jnp.float32),
        jax.ShapeDtypeStruct((rows, local_width), jnp.bfloat16),
        jax.ShapeDtypeStruct((rows, local_width), jnp.bfloat16),
    )
    return pl.pallas_call(
        far_kernel,
        out_shape=outs,
        grid=(1,),
        in_specs=[pl.BlockSpec(memory_space=pltpu.SMEM)] * 2
        + [whole(array) for array in (base, order, gain, *mixes)]
        + [pl.BlockSpec(memory_space=pltpu.HBM)] * (len(weights) + len(query_weights)),
        out_specs=tuple(whole(out) for out in outs),
        scratch_shapes=[
            pltpu.VMEM((2 * rows, heads * HD), jnp.bfloat16),
            pltpu.VMEM((rows, width), jnp.float32),
            pltpu.VMEM((len(weights), *weights[0].shape), jnp.bfloat16),
            pltpu.SemaphoreType.DMA((len(weights),)),
            pltpu.VMEM((len(query_weights), *query_weights[0].shape), jnp.bfloat16),
            pltpu.SemaphoreType.DMA((len(query_weights),)),
        ],
        compiler_params=pltpu.CompilerParams(vmem_limit_bytes=24 * MEGA),
        cost_estimate=pl.CostEstimate(
            flops=10 * rows * width * width, transcendentals=rows, bytes_accessed=8 * width * width
        ),
    )(core, chip, base, order, gain, *mixes, *weights, *query_weights)


def cross_kernel(piece_count, merging, query_ref, *refs):
    piece_refs, refs = refs[:piece_count], refs[piece_count:]
    if merging:
        *old_refs, out_ref, score_ref, local_ref, copy_sem = refs
    else:
        *out_refs, score_ref, local_ref, copy_sem = refs
    rows, local_width = query_ref.shape
    low = low_lanes((rows, LANES))
    zero = jnp.zeros((), jnp.bfloat16)
    chunk = piece_refs[0].shape[0]
    copies = [
        pltpu.make_async_copy(ref, local_ref.at[index], copy_sem.at[index])
        for index, ref in enumerate(piece_refs)
    ]
    for copy in copies:
        copy.start()

    def lane_groups(values):
        return [values[:, g : g + LANES] for g in range(0, chunk, LANES)]

    for pair in range(0, local_width, LANES):
        if merging:
            old_peak, old_sums, old_total = (ref[:, pair : pair + LANES] for ref in old_refs)
        results = []
        for head in range(2):
            query = jnp.where(low == (head == 0), query_ref[:, pair : pair + LANES], zero)
            peak = jnp.full((rows, LANES), -jnp.inf, jnp.float32)
            for index in range(piece_count):
                if pair + head == 0:
                    copies[index].wait()
                scores = lax.dot_general(
                    query,
                    local_ref[index, :, pair : pair + LANES],
                    (((1,), (1,)), ((), ())),
                    preferred_element_type=jnp.float32,
                )
                score_ref[head, :, index * chunk : (index + 1) * chunk] = scores
                peak = functools.reduce(jnp.maximum, lane_groups(scores), peak)
            row_max = jnp.max(peak, axis=-1, keepdims=True)
            if merging:
                row_max = jnp.maximum(row_max, old_peak[:, head * HD : head * HD + 1])
            sums = jnp.zeros((rows, LANES), jnp.float32)
            total = jnp.zeros((rows, LANES), jnp.float32)
            for index in range(piece_count):
                weights = jnp.exp(
                    score_ref[head, :, index * chunk : (index + 1) * chunk] - row_max
                )
                sums = functools.reduce(jnp.add, lane_groups(weights), sums)
                total = total + jnp.dot(
                    weights.astype(jnp.bfloat16),
                    local_ref[index, :, local_width + pair : local_width + pair + LANES],
                    preferred_element_type=jnp.float32,
                )
            results.append((row_max, jnp.sum(sums, axis=-1, keepdims=True), total))
        new_peak, new_sums, new_total = (
            jnp.where(low, first, second) for first, second in zip(*results)
        )
        if merging:
            scale = jnp.exp(old_peak - new_peak)
            out_ref[:, pair : pair + LANES] = (
                (new_total + old_total * scale) / (new_sums + old_sums * scale)
            ).astype(jnp.bfloat16)
        else:
            for ref, values in zip(out_refs, (new_peak, new_sums, new_total)):
                ref[:, pair : pair + LANES] = values


def cross_mixing(queries, pieces, state=()):
    rows, local_width = queries.shape
    tokens = sum(piece.shape[0] for piece in pieces)
    scored = rows * tokens * local_width // HD
    block = pl.BlockSpec(memory_space=pltpu.VMEM)
    if state:
        outs = jax.ShapeDtypeStruct((rows, local_width), jnp.bfloat16)
    else:
        outs = (jax.ShapeDtypeStruct((rows, local_width), jnp.float32),) * 3
    return pl.pallas_call(
        functools.partial(cross_kernel, len(pieces), bool(state)),
        out_shape=outs,
        in_specs=[block]
        + [pl.BlockSpec(memory_space=pltpu.HBM)] * len(pieces)
        + [block] * len(state),
        out_specs=block if state else (block,) * 3,
        scratch_shapes=[
            pltpu.VMEM((2, rows, tokens), jnp.float32),
            pltpu.VMEM((len(pieces), *pieces[0].shape), jnp.bfloat16),
            pltpu.SemaphoreType.DMA((len(pieces),)),
        ],
        compiler_params=pltpu.CompilerParams(vmem_limit_bytes=20 * MEGA),
        cost_estimate=pl.CostEstimate(
            flops=16 * LANES * scored,
            transcendentals=scored,
            bytes_accessed=4 * (tokens * local_width + queries.size),
        ),
    )(queries, *pieces, *state)


def finish_kernel(base_ref, mix_ref, weight_ref, out_ref):
    out_ref[...] = (
        base_ref[...] + jnp.dot(mix_ref[...], weight_ref[...], preferred_element_type=jnp.float32)
    ).astype(jnp.bfloat16)


def finish(base, mix, weight):
    return pl.pallas_call(
        finish_kernel,
        out_shape=jax.ShapeDtypeStruct(base.shape, jnp.bfloat16),
        grid=(1,),
        in_specs=[whole(base), whole(mix), whole(weight)],
        out_specs=whole(base),
        compiler_params=pltpu.CompilerParams(vmem_limit_bytes=8 * MEGA),
    )(base, mix, weight)


def swap(array, pairs):
    return lax.ppermute(array, "mp", pairs)


def across(array, pairs):
    return lax.ppermute(array, "seq", pairs)


def by_head(
    voxels,
    destination,
    cond,
    norm_gain,
    qkv_weight,
    self_out_weight,
    cross_norm_gain,
    cross_q_weight,
    cond_kv_weight,
    cross_out_weight,
):
    model_index = lax.axis_index("mp").astype(jnp.int32)
    core = (model_index % 2).reshape(1)
    chip = (model_index // 2).reshape(1)
    row_count, width = voxels.shape
    rows = row_count // 2
    share = rows // 2

    other_qkv = swap(qkv_weight, CORE_SWAP)
    cond_pair = [
        jnp.dot(cond, cond_kv_weight[part], preferred_element_type=jnp.float32).astype(jnp.bfloat16)
        for part in range(2)
    ]
    own_piece = jnp.concatenate(cond_pair, axis=1)
    voxels, own_piece = lax.optimization_barrier((voxels, own_piece))
    sent, ranks = project(
        core,
        voxels,
        norm_gain.reshape(1, width),
        destination.reshape(row_count // LANES, LANES),
        qkv_weight,
        other_qkv,
    )

    mine = lax.all_to_all(sent, "seq", split_axis=0, concat_axis=0, tiled=True)
    theirs = swap(mine, CORE_SWAP)
    side_piece = across(own_piece, SIDE_SWAP)
    next_piece = across(own_piece, NEXT_SWAP)
    chip_self = swap(self_out_weight, CHIP_SWAP)
    late_piece, _ = lax.optimization_barrier((own_piece, mine))
    skip_piece = across(late_piece, SKIP_SWAP)
    mixed = window_mixing(core, mine, theirs, share)
    mixed, side_piece, next_piece, skip_piece, chip_self = lax.optimization_barrier(
        (mixed, side_piece, next_piece, skip_piece, chip_self)
    )

    near = lax.all_to_all(mixed, "seq", split_axis=0, concat_axis=0, tiled=True)
    last_piece = across(skip_piece, NEXT_SWAP)
    next_side_piece = across(next_piece, SIDE_SWAP)
    skip_side_piece = across(skip_piece, SIDE_SWAP)
    chip_cross = swap(cross_out_weight, CHIP_SWAP)
    far = swap(near, CHIP_SWAP)
    near_other = swap(near, CORE_SWAP)
    base, order, token = near_part(
        core,
        ranks,
        voxels,
        (near, near_other),
        (self_out_weight, swap(self_out_weight, CORE_SWAP)),
    )
    far, last_piece, next_side_piece, chip_cross, _ = lax.optimization_barrier(
        (far, last_piece, next_side_piece, chip_cross, token)
    )
    last_side_piece = across(last_piece, SIDE_SWAP)
    far_other = swap(far, CORE_SWAP)
    own_hidden, own_query, other_query = far_part(
        core,
        chip,
        base,
        order,
        cross_norm_gain.reshape(1, width),
        (far, far_other),
        (chip_self, swap(chip_self, CORE_SWAP)),
        (cross_q_weight, swap(cross_q_weight, CORE_SWAP)),
    )

    asked = swap(other_query, CORE_SWAP)
    early = (own_piece, side_piece, next_piece, skip_piece)
    own_state = cross_mixing(own_query, early)
    asked, skip_side_piece, *own_state = lax.optimization_barrier(
        (asked, skip_side_piece, *own_state)
    )
    asked_state = cross_mixing(asked, early)
    last_side_piece, *asked_state = lax.optimization_barrier((last_side_piece, *asked_state))
    late = (next_side_piece, skip_side_piece, last_piece, last_side_piece)
    answered = swap(cross_mixing(asked, late, tuple(asked_state)), CORE_SWAP)

    def halved(mix):
        halves = mix.reshape(2, share, mix.shape[1])
        return (
            lax.dynamic_index_in_dim(halves, at, 0, keepdims=False) for at in (chip[0], 1 - chip[0])
        )

    other_kept, other_leaving = halved(answered)
    other_arrived = swap(other_leaving, CHIP_SWAP)
    own_mix = cross_mixing(own_query, late, tuple(own_state))
    own_mix, other_arrived, other_kept = lax.optimization_barrier(
        (own_mix, other_arrived, other_kept)
    )
    own_kept, own_leaving = halved(own_mix)
    own_arrived = swap(own_leaving, CHIP_SWAP)
    crossed = own_hidden
    for part, weight in (
        (other_kept, swap(cross_out_weight, CORE_SWAP)),
        (other_arrived, swap(chip_cross, CORE_SWAP)),
        (own_kept, cross_out_weight),
    ):
        crossed = crossed + jnp.dot(part, weight, preferred_element_type=jnp.float32)
    return finish(crossed, own_arrived, chip_cross)


def rms_norm(matrix, gain):
    values = matrix.astype(jnp.float32)
    spread = jnp.mean(values * values, axis=-1, keepdims=True)
    return (values * lax.rsqrt(spread + 1e-06) * gain).astype(jnp.bfloat16)


def window_attention(queries, keyset, valset, occupied, head_count):
    slot_count = queries.shape[0]
    window_count = slot_count // WBLK
    query_heads = queries.reshape(window_count, WBLK, head_count, HD)
    key_heads = keyset.reshape(window_count, WBLK, head_count, HD)
    value_heads = valset.reshape(window_count, WBLK, head_count, HD)
    scores = jnp.einsum(
        "wqhd,wkhd->whqk", query_heads, key_heads, preferred_element_type=jnp.float32
    ) * HD ** (-0.5)
    diagonal = (
        jnp.arange(WBLK, dtype=jnp.int32)[:, None] == jnp.arange(WBLK, dtype=jnp.int32)[None, :]
    )
    allowed = occupied.reshape(window_count, 1, WBLK) | diagonal[None]
    weights = jnp.where(allowed[:, None], jnp.exp(scores), 0.0)
    totals = jnp.sum(weights, axis=-1)
    mixed = jnp.einsum(
        "whqk,wkhd->wqhd",
        weights.astype(jnp.bfloat16),
        value_heads,
        preferred_element_type=jnp.float32,
    )
    mixed = mixed / jnp.transpose(totals, (0, 2, 1))[:, :, :, None]
    return mixed.astype(jnp.bfloat16).reshape(slot_count, head_count * HD)


def by_owner(
    voxels,
    destination,
    cond,
    norm_gain,
    qkv_weight,
    self_out_weight,
    cross_norm_gain,
    cross_q_weight,
    cond_kv_weight,
    cross_out_weight,
):
    peer_count = lax.axis_size("seq")
    part_count = lax.axis_size("mp")
    model_index = lax.axis_index("mp")
    row_count = voxels.shape[0]
    local_width = qkv_weight.shape[2]
    head_count = local_width // HD
    capacity = 2 * row_count // peer_count
    slot_count = peer_count * capacity
    owner_ids = destination // slot_count
    slot_ids = destination % slot_count
    matches = (owner_ids[:, None] == jnp.arange(peer_count, dtype=jnp.int32)[None, :]).astype(
        jnp.int32
    )
    within = jnp.sum(matches * (jnp.cumsum(matches, axis=0) - 1), axis=1)
    send_index = owner_ids * capacity + within
    normed = rms_norm(voxels, norm_gain)
    place_buffer = (
        jnp.full((slot_count,), slot_count, jnp.int32)
        .at[send_index]
        .set(slot_ids)
        .reshape(peer_count, capacity)
    )
    projected = jnp.einsum(
        "rd,cdh->rch", normed, qkv_weight, preferred_element_type=jnp.float32
    ).astype(jnp.bfloat16)
    send_buffer = (
        jnp.zeros((slot_count, 3 * local_width), jnp.bfloat16)
        .at[send_index]
        .set(projected.reshape(row_count, 3 * local_width))
    )
    received, places = (
        lax.all_to_all(
            send_buffer.reshape(peer_count, capacity, 3 * local_width),
            "seq",
            split_axis=0,
            concat_axis=0,
            tiled=True,
        ),
        lax.all_to_all(place_buffer, "seq", split_axis=0, concat_axis=0, tiled=True),
    )
    received = received.reshape(slot_count, 3 * local_width)
    places = places.reshape(slot_count)
    layout = (
        jnp.zeros((slot_count, 3 * local_width), jnp.bfloat16).at[places].set(received, mode="drop")
    )
    occupied = jnp.zeros((slot_count,), jnp.bool_).at[places].set(True, mode="drop")
    mixed = window_attention(
        layout[:, :local_width],
        layout[:, local_width : 2 * local_width],
        layout[:, 2 * local_width :],
        occupied,
        head_count,
    )
    outgoing = mixed[jnp.minimum(places, slot_count - 1)]
    returned = lax.all_to_all(
        outgoing.reshape(peer_count, capacity, local_width),
        "seq",
        split_axis=0,
        concat_axis=0,
        tiled=True,
    )
    window_mix = returned.reshape(slot_count, local_width)[send_index]
    row_share = row_count // part_count
    summed_out = lax.psum(
        jnp.dot(window_mix, self_out_weight, preferred_element_type=jnp.float32), "mp"
    )
    hidden = voxels.astype(jnp.float32) + summed_out
    normed2 = rms_norm(hidden, cross_norm_gain)
    own_hidden = lax.dynamic_slice_in_dim(hidden, model_index * row_share, row_share, 0)
    cross_query = (
        jnp.dot(normed2, cross_q_weight, preferred_element_type=jnp.float32)
        .astype(jnp.bfloat16)
        .reshape(row_count, head_count, HD)
    )
    cond_pair = jnp.einsum(
        "td,cdh->cth", cond, cond_kv_weight, preferred_element_type=jnp.float32
    ).astype(jnp.bfloat16)

    def fold_block(running, key_block, value_block):
        row_max, totals, mixed_sum = running
        scores = jnp.einsum(
            "qhd,khd->qhk", cross_query, key_block, preferred_element_type=jnp.float32
        ) * HD ** (-0.5)
        new_max = jnp.maximum(row_max, jnp.max(scores, axis=-1))
        rescale = jnp.exp(row_max - new_max)
        weights = jnp.exp(scores - new_max[:, :, None])
        totals = totals * rescale + jnp.sum(weights, axis=-1)
        update = jnp.einsum(
            "qhk,khd->qhd",
            weights.astype(jnp.bfloat16),
            value_block,
            preferred_element_type=jnp.float32,
        )
        return (new_max, totals, mixed_sum * rescale[:, :, None] + update)

    start_state = (
        jnp.full((row_count, head_count), -1e30, jnp.float32),
        jnp.zeros((row_count, head_count), jnp.float32),
        jnp.zeros((row_count, head_count, HD), jnp.float32),
    )
    key_piece = lax.all_gather(cond_pair[0], "seq", axis=0, tiled=True)
    value_piece = lax.all_gather(cond_pair[1], "seq", axis=0, tiled=True)
    token_count = key_piece.shape[0]
    sub_block = math.gcd(token_count, 512)
    key_blocks = key_piece.reshape(token_count // sub_block, sub_block, head_count, HD)
    value_blocks = value_piece.reshape(token_count // sub_block, sub_block, head_count, HD)

    def advance(state, operands):
        return (fold_block(state, operands[0], operands[1]), None)

    folded, unused = lax.scan(advance, start_state, (key_blocks, value_blocks))
    row_max, totals, mixed_sum = folded
    cross_mix = (
        (mixed_sum / totals[:, :, None]).astype(jnp.bfloat16).reshape(row_count, local_width)
    )
    cross_sum = lax.psum_scatter(
        jnp.dot(cross_mix, cross_out_weight, preferred_element_type=jnp.float32),
        "mp",
        scatter_dimension=0,
        tiled=True,
    )
    return (own_hidden + cross_sum).astype(jnp.bfloat16)


def solution(mesh):
    heads_match = mesh.shape["mp"] == 4 and mesh.shape["seq"] == 8
    return jax.shard_map(
        by_head if heads_match else by_owner,
        mesh=mesh,
        in_specs=(
            P("seq", None),
            P("seq"),
            P("seq", None),
            P(),
            P(None, None, "mp"),
            P("mp", None),
            P(),
            P(None, "mp"),
            P(None, None, "mp"),
            P("mp", None),
        ),
        out_specs=P(("seq", "mp"), None),
        check_vma=False,
    )
```

```python
import functools
import math

import jax
import jax.numpy as jnp
from jax import lax
from jax.experimental import pallas as pl
from jax.experimental.pallas import tpu as pltpu
from jax.sharding import PartitionSpec as P

HD = 64
WBLK = 64
LANES = 128
ID_ROWS = 16
MEGA = 1024 * 1024
BATCH = 4
CORE_SWAP = ((0, 1), (1, 0), (2, 3), (3, 2))
CHIP_SWAP = ((0, 2), (2, 0), (1, 3), (3, 1))
BOTH_SWAP = ((0, 3), (3, 0), (1, 2), (2, 1))
SIDE_SWAP = tuple((i, i ^ 1) for i in range(8))
NEXT_SWAP = tuple((i, i ^ 2) for i in range(8))
SKIP_SWAP = tuple((i, i ^ 4) for i in range(8))


def low_lanes(shape):
    return lax.broadcasted_iota(jnp.int32, shape, 1) < HD


def swap_halves(values):
    return pltpu.roll(values, HD, 1)


def columns_of(row):
    return jnp.transpose(jnp.broadcast_to(row, (LANES, LANES)))


def one_hot(condition):
    return jnp.where(condition, 1.0, 0.0).astype(jnp.bfloat16)


def project_kernel(
    core_ref, seq_ref, vox_ref, gain_ref, place_ref, own_ref, other_ref, *refs
):
    *out_refs, rank_ref, normed_ref, ids_ref, blob_ref, local_ref, copy_sem = refs
    vox_copy = pltpu.make_async_copy(vox_ref, local_ref, copy_sem.at[0])
    step = pl.program_id(0)
    rows = normed_ref.shape[0]
    packed = rows // 2
    groups = place_ref.shape[0]

    @pl.when(step == 0)
    def _():
        vox_copy.start()
        places = place_ref[...].astype(jnp.float32)
        place_rows = [places[g : g + 1] for g in range(groups)]
        place_columns = [columns_of(row) for row in place_rows]
        blank = jnp.zeros((8 - groups, LANES), jnp.float32)
        lane = lax.broadcasted_iota(jnp.int32, (LANES, LANES), 1).astype(jnp.float32)
        rank_rows = [
            sum(
                jnp.sum(jnp.where(column < row, 1.0, 0.0), axis=0, keepdims=True)
                for column in place_columns
            )
            for row in place_rows
        ]
        rank_columns = [
            jnp.sum(sum(jnp.where(row < column, 1.0, 0.0) for row in place_rows), axis=1, keepdims=True)
            for column in place_columns
        ]
        window_rows = [
            jnp.floor(
                sum(
                    jnp.sum(
                        jnp.where(rank == lane + float(g * LANES), column, 0.0), axis=0, keepdims=True
                    )
                    for rank, column in zip(rank_columns, place_columns)
                )
                * (1.0 / WBLK)
            )
            for g in range(groups)
        ]
        slot = lax.broadcasted_iota(jnp.int32, (1, LANES), 1)
        bounds = jnp.zeros((1, LANES), jnp.float32)
        for block in range(2 * groups):
            begin = (block % 2) * WBLK
            row = window_rows[block // 2]
            bounds = jnp.where(slot == block, row[:, begin : begin + 1], bounds)
            bounds = jnp.where(
                slot == block + 2 * groups, row[:, begin + WBLK - 1 : begin + WBLK], bounds
            )
        windows = jnp.concatenate(
            window_rows + [bounds] + [jnp.zeros_like(bounds)] * (7 - groups), axis=0
        )
        high = jnp.floor(windows * (1.0 / 256.0))
        ids_ref[...] = jnp.concatenate([high, windows - 256.0 * high], axis=0).astype(jnp.bfloat16)
        rank_ref[...] = jnp.concatenate(rank_rows + [blank], axis=0)
        wanted = (lax.broadcasted_iota(jnp.int32, (rows, LANES), 0) + core_ref[0] * rows).astype(
            jnp.float32
        )
        order = jnp.concatenate([one_hot(row == wanted) for row in rank_rows], axis=1)
        vox_copy.wait()
        values = jnp.dot(order, local_ref[...], preferred_element_type=jnp.float32)
        spread = jnp.mean(values * values, axis=-1, keepdims=True)
        normed_ref[...] = (values * lax.rsqrt(spread + 1e-06) * gain_ref[...]).astype(jnp.bfloat16)

    def emit(weight_ref, holder):
        normed = normed_ref[...]
        low = low_lanes((rows, LANES))
        low_packed = low_lanes((packed, LANES))
        query, key, value = (
            jnp.dot(normed, weight_ref[part], preferred_element_type=jnp.float32)
            for part in range(3)
        )
        query = query * HD ** (-0.5)
        for at in range(0, weight_ref.shape[2], LANES):
            keys, values = key[:, at : at + LANES], value[:, at : at + LANES]
            first, second = query[:packed, at : at + LANES], query[packed:, at : at + LANES]
            pairs = (
                (
                    jnp.where(low, keys, swap_halves(values)),
                    jnp.where(low_packed, first, swap_halves(second)),
                ),
                (
                    jnp.where(low, swap_halves(keys), values),
                    jnp.where(low_packed, swap_halves(first), second),
                ),
            )
            for side, (keyval, queries) in enumerate(pairs):
                head = holder * (weight_ref.shape[2] // HD) + at // HD + side
                target = head ^ seq_ref[0]
                blob_ref[target, :rows] = keyval.astype(jnp.bfloat16)
                blob_ref[target, rows : rows + ID_ROWS] = ids_ref[...]
                blob_ref[target, rows + ID_ROWS :] = queries.astype(jnp.bfloat16)

    @pl.when(step == 0)
    def _():
        emit(own_ref, core_ref[0])

    @pl.when(step == 1)
    def _():
        emit(other_ref, 1 - core_ref[0])
        for target, out_ref in enumerate(out_refs):
            out_ref[...] = blob_ref[target]


def project(core, seq, vox, gain, places, own_weight, other_weight):
    row_count, width = vox.shape
    rows = row_count // 2
    local_width = own_weight.shape[2]
    heads = 2 * local_width // HD
    blob = rows + ID_ROWS + rows // 2

    def fixed(array):
        return pl.BlockSpec(array.shape, lambda step, *refs: (0,) * array.ndim)

    outs = [jax.ShapeDtypeStruct((blob, LANES), jnp.bfloat16)] * heads
    outs.append(jax.ShapeDtypeStruct((8, LANES), jnp.float32))
    operands = (vox, gain, places, own_weight, other_weight)
    return pl.pallas_call(
        project_kernel,
        out_shape=outs,
        grid_spec=pltpu.PrefetchScalarGridSpec(
            num_scalar_prefetch=2,
            grid=(2,),
            in_specs=[pl.BlockSpec(memory_space=pl.ANY)]
            + [fixed(operand) for operand in operands[1:]],
            out_specs=[fixed(out) for out in outs],
            scratch_shapes=[
                pltpu.VMEM((rows, width), jnp.bfloat16),
                pltpu.VMEM((ID_ROWS, LANES), jnp.bfloat16),
                pltpu.VMEM((heads, blob, LANES), jnp.bfloat16),
                pltpu.VMEM((row_count, width), jnp.bfloat16),
                pltpu.SemaphoreType.DMA((1,)),
            ],
        ),
        compiler_params=pltpu.CompilerParams(vmem_limit_bytes=28 * MEGA),
    )(core, seq, *operands)


def window_kernel(
    core_ref,
    seq_ref,
    *refs,
):
    sources = (len(refs) - 10) // 2
    mine_refs, theirs_refs, refs = refs[:sources], refs[sources : 2 * sources], refs[2 * sources :]
    out_ref, key_ref, window_ref, query_ref, column_ref, *refs = refs
    sum_ref, total_ref, plan_ref, plan_smem, late_smem, copy_sem = refs
    packed = out_ref.shape[1]
    rows = 2 * packed
    blocks = rows // LANES
    last = 2 * rows // WBLK
    low_packed = low_lanes((packed, LANES))
    core = core_ref[0]

    low = low_lanes((8, LANES))
    real = lax.broadcasted_iota(jnp.int32, (8, LANES), 0) < 2 * blocks
    for index, (mine_ref, theirs_ref) in enumerate(zip(mine_refs, theirs_refs)):
        for ref, side in ((mine_ref, core), (theirs_ref, 1 - core)):
            key_ref[index, pl.ds(pl.multiple_of(side * rows, LANES), rows)] = ref[:rows]
    key_ref[:, 2 * rows :] = jnp.zeros((sources, 2 * LANES, LANES), jnp.bfloat16)
    bounds = []
    for index in range(sources):
        tile = mine_refs[index][rows : rows + ID_ROWS].astype(jnp.float32)
        ids = tile[:8] * 256.0 + tile[8:]
        bounds.append(ids[2 * blocks : 2 * blocks + 1])
        even = jnp.where(real, ids, -1.0)
        window_ref[index, 0] = even
        window_ref[index, 1] = jnp.where(
            low, swap_halves(even), swap_halves(pltpu.roll(even, 7, 0))
        )

    bounds = jnp.concatenate(bounds, axis=0)
    slot = lax.broadcasted_iota(jnp.int32, (sources, LANES), 1)
    lows = jnp.where(slot < last, bounds, jnp.inf)
    highs = jnp.where(slot < last, pltpu.roll(bounds, LANES - last, 1), jnp.inf)
    begins = [
        jnp.where(core == 0, bounds[:, at : at + 1], bounds[:, at + last // 2 : at + last // 2 + 1])
        for at in range(0, last // 2, 2)
    ]
    ends = [
        jnp.where(core == 0, bounds[:, at : at + 1], bounds[:, at + last // 2 : at + last // 2 + 1])
        for at in range(last + 1, last + last // 2, 2)
    ]
    first = jnp.full((sources, LANES), float(last), jnp.float32)
    beyond = first
    for source in range(sources):
        for block in range(blocks):
            here = slot == source * blocks + block
            begin, end = (edges[block][source : source + 1] for edges in (begins, ends))
            first = jnp.where(
                here, jnp.sum(jnp.where(highs < begin, 1.0, 0.0), axis=1, keepdims=True), first
            )
            beyond = jnp.where(
                here, jnp.sum(jnp.where(lows <= end, 1.0, 0.0), axis=1, keepdims=True), beyond
            )
    plan_ref[0] = first.astype(jnp.int32)
    plan_ref[1] = jnp.floor((beyond - first + 3.0) * 0.25).astype(jnp.int32)
    plan_copy = pltpu.make_async_copy(plan_ref, plan_smem, copy_sem.at[0])
    plan_copy.start()
    plan_copy.wait()

    def fold(pair, other, turn, query_part, query_ids, sums, total):
        start = jnp.minimum(plan_smem[0, other, pair] + 4 * turn, last)
        keyval = key_ref[other, pl.ds(pl.multiple_of(start * WBLK, WBLK), 2 * LANES)]
        scores = lax.dot_general(
            query_part, keyval, (((1,), (1,)), ((), ())), preferred_element_type=jnp.float32
        )
        weights = [
            jnp.where(
                query_ids == window_ref[other, start % 2, pl.ds(start // 2 + g, 1)],
                jnp.exp(scores[:, g * LANES : (g + 1) * LANES]),
                0.0,
            )
            for g in range(2)
        ]
        rounded = jnp.concatenate([part.astype(jnp.bfloat16) for part in weights], axis=1)
        return (
            sums + weights[0] + weights[1],
            total + jnp.dot(rounded, keyval, preferred_element_type=jnp.float32),
        )

    for source, ref in enumerate(mine_refs):
        wire = ref[rows + ID_ROWS :].astype(jnp.float32)
        query = jnp.concatenate(
            [jnp.where(low_packed, wire, 0.0), jnp.where(low_packed, swap_halves(wire), 0.0)],
            axis=0,
        ).astype(jnp.bfloat16)
        for block in range(blocks):
            query_ref[source * blocks + block] = query[block * LANES : (block + 1) * LANES]

    def sweep(source, carry):
        for block in range(blocks):
            at = source * blocks + block
            query_part = query_ref[at]
            query_ids = columns_of(window_ref[source, 0, pl.ds(core * blocks + block, 1)])
            column_ref[at] = query_ids
            sums = jnp.zeros((LANES, LANES), jnp.float32)
            total = jnp.zeros((LANES, LANES), jnp.float32)
            for other in range(sources):
                sums, total = fold(at, other, 0, query_part, query_ids, sums, total)
            sum_ref[at] = sums
            total_ref[at] = total
        return carry

    lax.fori_loop(0, sources, sweep, 0)
    spare = sources * blocks
    query_ref[spare] = jnp.zeros((LANES, LANES), jnp.bfloat16)
    column_ref[spare] = jnp.zeros((LANES, LANES), jnp.float32)
    sum_ref[spare] = jnp.zeros((LANES, LANES), jnp.float32)
    total_ref[spare] = jnp.zeros((LANES, LANES), jnp.float32)

    count = jnp.int32(0)
    for other in range(sources):
        for at in range(sources * blocks):
            late_smem[count] = other * LANES + at
            count = count + jnp.where(plan_smem[1, other, at] > 1, 1, 0)
    for i in range(BATCH):
        late_smem[count + i] = spare

    def visit(index, carry):
        pairs = [late_smem[index * BATCH + i] for i in range(BATCH)]
        pairs = [(pair // LANES, pair % LANES) for pair in pairs]
        turns = functools.reduce(jnp.maximum, [plan_smem[1, other, at] for other, at in pairs])

        def more(turn, carry):
            for other, at in pairs:
                sum_ref[at], total_ref[at] = fold(
                    at, other, turn, query_ref[at], column_ref[at], sum_ref[at], total_ref[at]
                )
            return carry

        return lax.fori_loop(1, turns, more, carry)

    lax.fori_loop(0, (count + BATCH - 1) // BATCH, visit, 0)

    for source in range(sources):
        mixed = jnp.concatenate(
            [
                total_ref[at] / jnp.sum(sum_ref[at], axis=-1, keepdims=True)
                for at in range(source * blocks, (source + 1) * blocks)
            ],
            axis=0,
        )
        out_ref[source ^ seq_ref[0]] = jnp.where(low_packed, swap_halves(mixed[:packed]), mixed[packed:]).astype(
            jnp.bfloat16
        )


def window_mixing(core, seq, mine, theirs, packed):
    sources = len(mine)
    rows = 2 * packed
    blocks = rows // LANES
    vmem = pl.BlockSpec(memory_space=pltpu.VMEM)
    smem = pl.BlockSpec(memory_space=pltpu.SMEM)
    return pl.pallas_call(
        window_kernel,
        out_shape=jax.ShapeDtypeStruct((sources, packed, LANES), jnp.bfloat16),
        in_specs=[smem] * 2 + [vmem] * (2 * sources),
        out_specs=vmem,
        scratch_shapes=[
            pltpu.VMEM((sources, 2 * rows + 2 * LANES, LANES), jnp.bfloat16),
            pltpu.VMEM((sources, 2, 8, LANES), jnp.float32),
            pltpu.VMEM((sources * blocks + 1, LANES, LANES), jnp.bfloat16),
            pltpu.VMEM((sources * blocks + 1, LANES, LANES), jnp.float32),
            pltpu.VMEM((sources * blocks + 1, LANES, LANES), jnp.float32),
            pltpu.VMEM((sources * blocks + 1, LANES, LANES), jnp.float32),
            pltpu.VMEM((2, sources, LANES), jnp.int32),
            pltpu.SMEM((2, sources, LANES), jnp.int32),
            pltpu.SMEM((sources * sources * blocks + 2 * BATCH,), jnp.int32),
            pltpu.SemaphoreType.DMA((1,)),
        ],
        compiler_params=pltpu.CompilerParams(vmem_limit_bytes=24 * MEGA),
        cost_estimate=pl.CostEstimate(
            flops=80 * LANES * (sources * packed) ** 2,
            transcendentals=2 * (sources * packed) ** 2,
            bytes_accessed=4 * sources * mine[0].size,
        ),
    )(core, seq, *mine, *theirs)


def fetch(refs, local_ref, copy_sem):
    copies = [
        pltpu.make_async_copy(ref, local_ref.at[index], copy_sem.at[index])
        for index, ref in enumerate(refs)
    ]
    for copy in copies:
        copy.start()
    return copies


def mix_heads(core, own_ref, other_ref, order, weight_ref, copies, mix_ref):
    heads, share, _ = own_ref.shape
    rows = 2 * share
    low = low_lanes((share, LANES))
    for half, ref in enumerate((own_ref, other_ref)):
        offset = pl.multiple_of((core if half == 0 else 1 - core) * rows, LANES)
        for pair in range(heads // 2):
            holder = core if pair < heads // 4 else 1 - core
            head = holder * (heads // 2) + (pair % (heads // 4)) * 2
            first, second = (ref[at].astype(jnp.float32) for at in (head, head + 1))
            at = pair * LANES
            mix_ref[pl.ds(offset, share), at : at + LANES] = jnp.where(
                low, first, swap_halves(second)
            ).astype(jnp.bfloat16)
            mix_ref[pl.ds(offset + share, share), at : at + LANES] = jnp.where(
                low, swap_halves(first), second
            ).astype(jnp.bfloat16)
    mix = jnp.dot(order, mix_ref[...], preferred_element_type=jnp.float32).astype(jnp.bfloat16)
    depth = weight_ref.shape[1]
    for copy in copies:
        copy.wait()
    return sum(
        jnp.dot(
            mix[:, i * depth : (i + 1) * depth], weight_ref[i], preferred_element_type=jnp.float32
        )
        for i in range(len(copies))
    )


def near_kernel(
    core_ref,
    rank_ref,
    vox_ref,
    own_ref,
    other_ref,
    weight_ref,
    other_weight_ref,
    hidden_ref,
    order_ref,
    token_ref,
    mix_ref,
    column_ref,
    local_ref,
    copy_sem,
):
    core = core_ref[0]
    copies = fetch((weight_ref, other_weight_ref), local_ref, copy_sem)
    token_ref[...] = jnp.zeros_like(token_ref)
    rows = hidden_ref.shape[0]
    share = rows // 2
    groups = 2 * rows // LANES
    for group in range(groups):
        column_ref[group * LANES : (group + 1) * LANES] = columns_of(rank_ref[group : group + 1])
    begin = pl.multiple_of(core * share, 64)
    ranks = jnp.concatenate(
        [column_ref[pl.ds(begin, share)], column_ref[pl.ds(begin + rows, share)]], axis=0
    )
    lane = lax.broadcasted_iota(jnp.int32, (rows, LANES), 1).astype(jnp.float32)
    order = jnp.concatenate(
        [one_hot(ranks == lane + float(group * LANES)) for group in range(groups)], axis=1
    )
    order_ref[...] = order
    values = jnp.concatenate(
        [vox_ref[pl.ds(begin, share)], vox_ref[pl.ds(begin + rows, share)]], axis=0
    ).astype(jnp.float32)
    hidden_ref[...] = values + mix_heads(
        core, own_ref, other_ref, order, local_ref, copies, mix_ref
    )


def far_kernel(
    core_ref,
    chip_ref,
    base_ref,
    order_ref,
    gain_ref,
    own_ref,
    other_ref,
    weight_ref,
    other_weight_ref,
    query_weight_ref,
    other_query_weight_ref,
    hidden_ref,
    query_ref,
    other_query_ref,
    mix_ref,
    kept_ref,
    local_ref,
    copy_sem,
    query_local_ref,
    query_sem,
):
    share = hidden_ref.shape[0]
    copies = fetch((weight_ref, other_weight_ref), local_ref, copy_sem)
    query_copies = fetch((query_weight_ref, other_query_weight_ref), query_local_ref, query_sem)
    hidden = base_ref[...] + mix_heads(
        core_ref[0], own_ref, other_ref, order_ref[...], local_ref, copies, mix_ref
    )
    kept_ref[...] = hidden
    hidden_ref[...] = kept_ref[pl.ds(pl.multiple_of(chip_ref[0] * share, 64), share)]
    spread = jnp.mean(hidden * hidden, axis=-1, keepdims=True)
    normed = (hidden * lax.rsqrt(spread + 1e-06) * gain_ref[...]).astype(jnp.bfloat16)
    for index, out in enumerate((query_ref, other_query_ref)):
        query_copies[index].wait()
        queries = jnp.dot(normed, query_local_ref[index], preferred_element_type=jnp.float32)
        out[...] = (queries.astype(jnp.bfloat16).astype(jnp.float32) * HD ** (-0.5)).astype(
            jnp.bfloat16
        )


def whole(array):
    return pl.BlockSpec(array.shape, lambda step: (0,) * array.ndim)


def near_part(core, ranks, voxels, mixes, weights):
    row_count, width = voxels.shape
    rows = row_count // 2
    heads = mixes[0].shape[0]
    outs = (
        jax.ShapeDtypeStruct((rows, width), jnp.float32),
        jax.ShapeDtypeStruct((rows, row_count), jnp.bfloat16),
        jax.ShapeDtypeStruct((8, LANES), jnp.float32),
    )
    return pl.pallas_call(
        near_kernel,
        out_shape=outs,
        grid=(1,),
        in_specs=[pl.BlockSpec(memory_space=pltpu.SMEM)]
        + [whole(array) for array in (ranks, voxels, *mixes)]
        + [pl.BlockSpec(memory_space=pltpu.HBM)] * len(weights),
        out_specs=tuple(whole(out) for out in outs),
        scratch_shapes=[
            pltpu.VMEM((row_count, heads * HD), jnp.bfloat16),
            pltpu.VMEM((row_count, LANES), jnp.float32),
            pltpu.VMEM((len(weights), *weights[0].shape), jnp.bfloat16),
            pltpu.SemaphoreType.DMA((len(weights),)),
        ],
        compiler_params=pltpu.CompilerParams(vmem_limit_bytes=24 * MEGA),
        cost_estimate=pl.CostEstimate(
            flops=10 * rows * width * width, transcendentals=0, bytes_accessed=8 * width * width
        ),
    )(core, ranks, voxels, *mixes, *weights)


def far_part(core, chip, base, order, gain, mixes, weights, query_weights):
    rows, width = base.shape
    share = rows // 2
    local_width = query_weights[0].shape[1]
    heads = mixes[0].shape[0]
    outs = (
        jax.ShapeDtypeStruct((share, width), jnp.float32),
        jax.ShapeDtypeStruct((rows, local_width), jnp.bfloat16),
        jax.ShapeDtypeStruct((rows, local_width), jnp.bfloat16),
    )
    return pl.pallas_call(
        far_kernel,
        out_shape=outs,
        grid=(1,),
        in_specs=[pl.BlockSpec(memory_space=pltpu.SMEM)] * 2
        + [whole(array) for array in (base, order, gain, *mixes)]
        + [pl.BlockSpec(memory_space=pltpu.HBM)] * (len(weights) + len(query_weights)),
        out_specs=tuple(whole(out) for out in outs),
        scratch_shapes=[
            pltpu.VMEM((2 * rows, heads * HD), jnp.bfloat16),
            pltpu.VMEM((rows, width), jnp.float32),
            pltpu.VMEM((len(weights), *weights[0].shape), jnp.bfloat16),
            pltpu.SemaphoreType.DMA((len(weights),)),
            pltpu.VMEM((len(query_weights), *query_weights[0].shape), jnp.bfloat16),
            pltpu.SemaphoreType.DMA((len(query_weights),)),
        ],
        compiler_params=pltpu.CompilerParams(vmem_limit_bytes=24 * MEGA),
        cost_estimate=pl.CostEstimate(
            flops=10 * rows * width * width, transcendentals=rows, bytes_accessed=8 * width * width
        ),
    )(core, chip, base, order, gain, *mixes, *weights, *query_weights)


def cross_kernel(chip_ref, *refs):
    query_refs, piece_refs, out_refs, score_ref = refs[:2], refs[2:-5], refs[-5:-1], refs[-1]
    rows, local_width = query_refs[0].shape
    share = rows // 2
    low = low_lanes((rows, LANES))
    zero = jnp.zeros((), jnp.bfloat16)
    chunk = piece_refs[0].shape[0]
    chip = chip_ref[0]

    def lane_groups(values):
        return [values[:, g : g + LANES] for g in range(0, chunk, LANES)]

    for turn, query_ref in enumerate(query_refs):
        for pair in range(0, local_width, LANES):
            mixes = []
            for head in range(2):
                query = jnp.where(low == (head == 0), query_ref[:, pair : pair + LANES], zero)
                peak = jnp.full((rows, LANES), -jnp.inf, jnp.float32)
                for index, ref in enumerate(piece_refs):
                    scores = lax.dot_general(
                        query,
                        ref[:, pair : pair + LANES],
                        (((1,), (1,)), ((), ())),
                        preferred_element_type=jnp.float32,
                    )
                    score_ref[head, :, index * chunk : (index + 1) * chunk] = scores
                    peak = functools.reduce(jnp.maximum, lane_groups(scores), peak)
                row_max = jnp.max(peak, axis=-1, keepdims=True)
                sums = jnp.zeros((rows, LANES), jnp.float32)
                total = jnp.zeros((rows, LANES), jnp.float32)
                for index, ref in enumerate(piece_refs):
                    weights = jnp.exp(
                        score_ref[head, :, index * chunk : (index + 1) * chunk] - row_max
                    )
                    sums = functools.reduce(jnp.add, lane_groups(weights), sums)
                    total = total + jnp.dot(
                        weights.astype(jnp.bfloat16),
                        ref[:, local_width + pair : local_width + pair + LANES],
                        preferred_element_type=jnp.float32,
                    )
                mixes.append(total / jnp.sum(sums, axis=-1, keepdims=True))
            mixed = jnp.where(low, mixes[0], mixes[1])
            halves = (mixed[:share], mixed[share:])
            for side, out_ref in enumerate(out_refs[2 * turn : 2 * turn + 2]):
                out_ref[:, pair : pair + LANES] = jnp.where(
                    chip == side, halves[0], halves[1]
                ).astype(jnp.bfloat16)


def cross_mixing(chip, queries, pieces):
    rows, local_width = queries[0].shape
    tokens = sum(piece.shape[0] for piece in pieces)
    block = pl.BlockSpec(memory_space=pltpu.VMEM)
    return pl.pallas_call(
        cross_kernel,
        out_shape=[jax.ShapeDtypeStruct((rows // 2, local_width), jnp.bfloat16)] * 4,
        in_specs=[pl.BlockSpec(memory_space=pltpu.SMEM)] + [block] * (2 + len(pieces)),
        out_specs=[block] * 4,
        scratch_shapes=[pltpu.VMEM((2, rows, tokens), jnp.float32)],
        compiler_params=pltpu.CompilerParams(vmem_limit_bytes=28 * MEGA),
    )(chip, *queries, *pieces)


def finish_kernel(base_ref, *refs):
    mix_refs, weight_refs, out_ref = refs[:3], refs[3:6], refs[6]
    total = base_ref[...]
    for mix_ref, weight_ref in zip(mix_refs, weight_refs):
        total = total + jnp.dot(mix_ref[...], weight_ref[...], preferred_element_type=jnp.float32)
    out_ref[...] = total.astype(jnp.bfloat16)


def finish(base, mixes, weights):
    operands = (base, *mixes, *weights)
    return pl.pallas_call(
        finish_kernel,
        out_shape=jax.ShapeDtypeStruct(base.shape, jnp.bfloat16),
        in_specs=[pl.BlockSpec(memory_space=pltpu.VMEM)] * len(operands),
        out_specs=pl.BlockSpec(memory_space=pltpu.VMEM),
        compiler_params=pltpu.CompilerParams(vmem_limit_bytes=12 * MEGA),
    )(*operands)


def swap(array, pairs):
    return lax.ppermute(array, "mp", pairs)


def across(array, pairs):
    return lax.ppermute(array, "seq", pairs)


def spread_out(blobs):
    count = len(blobs)
    return [blobs[0]] + [
        across(blobs[step], [(i, i ^ step) for i in range(count)]) for step in range(1, count)
    ]


def by_head(
    voxels,
    destination,
    cond,
    norm_gain,
    qkv_weight,
    self_out_weight,
    cross_norm_gain,
    cross_q_weight,
    cond_kv_weight,
    cross_out_weight,
):
    model_index = lax.axis_index("mp").astype(jnp.int32)
    seq = lax.axis_index("seq").astype(jnp.int32).reshape(1)
    core = (model_index % 2).reshape(1)
    chip = (model_index // 2).reshape(1)
    row_count, width = voxels.shape
    rows = row_count // 2
    share = rows // 2

    other_qkv = swap(qkv_weight, CORE_SWAP)
    cond_pair = [
        jnp.dot(cond, cond_kv_weight[part], preferred_element_type=jnp.float32).astype(jnp.bfloat16)
        for part in range(2)
    ]
    own_piece = jnp.concatenate(cond_pair, axis=1)
    voxels, own_piece = lax.optimization_barrier((voxels, own_piece))
    *sent, ranks = project(
        core,
        seq,
        voxels,
        norm_gain.reshape(1, width),
        destination.reshape(row_count // LANES, LANES),
        qkv_weight,
        other_qkv,
    )

    mine = spread_out(sent)
    theirs = [swap(blob, CORE_SWAP) for blob in mine]
    late_piece, *mine = lax.optimization_barrier((own_piece, *mine))
    side_piece = across(late_piece, SIDE_SWAP)
    next_piece = across(late_piece, NEXT_SWAP)
    skip_piece = across(late_piece, SKIP_SWAP)
    mixed = window_mixing(core, seq, mine, theirs, share)
    mixed, side_piece, next_piece, skip_piece = lax.optimization_barrier(
        (mixed, side_piece, next_piece, skip_piece)
    )

    near = lax.all_to_all(mixed, "seq", split_axis=0, concat_axis=0, tiled=True)
    last_piece = across(skip_piece, NEXT_SWAP)
    skip_side_piece = across(skip_piece, SIDE_SWAP)
    chip_self = swap(self_out_weight, CHIP_SWAP)
    far = swap(near, CHIP_SWAP)
    near_other = swap(near, CORE_SWAP)
    far, last_piece, skip_side_piece, chip_self = lax.optimization_barrier(
        (far, last_piece, skip_side_piece, chip_self)
    )
    last_side_piece = across(last_piece, SIDE_SWAP)
    next_side_piece = across(side_piece, NEXT_SWAP)
    far_other = swap(far, CORE_SWAP)
    pieces = [
        own_piece,
        side_piece,
        next_piece,
        next_side_piece,
        skip_piece,
        skip_side_piece,
        last_piece,
        last_side_piece,
    ]
    base, order, token = near_part(
        core,
        ranks,
        voxels,
        (near, near_other),
        (self_out_weight, swap(self_out_weight, CORE_SWAP)),
    )
    own_hidden, own_query, other_query = far_part(
        core,
        chip,
        base,
        order,
        cross_norm_gain.reshape(1, width),
        (far, far_other),
        (chip_self, swap(chip_self, CORE_SWAP)),
        (cross_q_weight, swap(cross_q_weight, CORE_SWAP)),
    )

    asked = swap(other_query, CORE_SWAP)
    late_weight, own_query = lax.optimization_barrier((cross_out_weight, own_query))
    chip_cross = swap(late_weight, CHIP_SWAP)
    kept, to_chip, to_core, to_both = cross_mixing(chip, (own_query, asked), pieces)
    kept, chip_cross = lax.optimization_barrier((kept, chip_cross))
    weights = (chip_cross, swap(chip_cross, CORE_SWAP), swap(cross_out_weight, CORE_SWAP))
    mixes = (swap(to_chip, CHIP_SWAP), swap(to_both, BOTH_SWAP), swap(to_core, CORE_SWAP))
    base = own_hidden + jnp.dot(kept, cross_out_weight, preferred_element_type=jnp.float32)
    return finish(base, mixes, weights)


def rms_norm(matrix, gain):
    values = matrix.astype(jnp.float32)
    spread = jnp.mean(values * values, axis=-1, keepdims=True)
    return (values * lax.rsqrt(spread + 1e-06) * gain).astype(jnp.bfloat16)


def window_attention(queries, keyset, valset, occupied, head_count):
    slot_count = queries.shape[0]
    window_count = slot_count // WBLK
    query_heads = queries.reshape(window_count, WBLK, head_count, HD)
    key_heads = keyset.reshape(window_count, WBLK, head_count, HD)
    value_heads = valset.reshape(window_count, WBLK, head_count, HD)
    scores = jnp.einsum(
        "wqhd,wkhd->whqk", query_heads, key_heads, preferred_element_type=jnp.float32
    ) * HD ** (-0.5)
    diagonal = (
        jnp.arange(WBLK, dtype=jnp.int32)[:, None] == jnp.arange(WBLK, dtype=jnp.int32)[None, :]
    )
    allowed = occupied.reshape(window_count, 1, WBLK) | diagonal[None]
    weights = jnp.where(allowed[:, None], jnp.exp(scores), 0.0)
    totals = jnp.sum(weights, axis=-1)
    mixed = jnp.einsum(
        "whqk,wkhd->wqhd",
        weights.astype(jnp.bfloat16),
        value_heads,
        preferred_element_type=jnp.float32,
    )
    mixed = mixed / jnp.transpose(totals, (0, 2, 1))[:, :, :, None]
    return mixed.astype(jnp.bfloat16).reshape(slot_count, head_count * HD)


def by_owner(
    voxels,
    destination,
    cond,
    norm_gain,
    qkv_weight,
    self_out_weight,
    cross_norm_gain,
    cross_q_weight,
    cond_kv_weight,
    cross_out_weight,
):
    peer_count = lax.axis_size("seq")
    part_count = lax.axis_size("mp")
    model_index = lax.axis_index("mp")
    row_count = voxels.shape[0]
    local_width = qkv_weight.shape[2]
    head_count = local_width // HD
    capacity = 2 * row_count // peer_count
    slot_count = peer_count * capacity
    owner_ids = destination // slot_count
    slot_ids = destination % slot_count
    matches = (owner_ids[:, None] == jnp.arange(peer_count, dtype=jnp.int32)[None, :]).astype(
        jnp.int32
    )
    within = jnp.sum(matches * (jnp.cumsum(matches, axis=0) - 1), axis=1)
    send_index = owner_ids * capacity + within
    normed = rms_norm(voxels, norm_gain)
    place_buffer = (
        jnp.full((slot_count,), slot_count, jnp.int32)
        .at[send_index]
        .set(slot_ids)
        .reshape(peer_count, capacity)
    )
    projected = jnp.einsum(
        "rd,cdh->rch", normed, qkv_weight, preferred_element_type=jnp.float32
    ).astype(jnp.bfloat16)
    send_buffer = (
        jnp.zeros((slot_count, 3 * local_width), jnp.bfloat16)
        .at[send_index]
        .set(projected.reshape(row_count, 3 * local_width))
    )
    received, places = (
        lax.all_to_all(
            send_buffer.reshape(peer_count, capacity, 3 * local_width),
            "seq",
            split_axis=0,
            concat_axis=0,
            tiled=True,
        ),
        lax.all_to_all(place_buffer, "seq", split_axis=0, concat_axis=0, tiled=True),
    )
    received = received.reshape(slot_count, 3 * local_width)
    places = places.reshape(slot_count)
    layout = (
        jnp.zeros((slot_count, 3 * local_width), jnp.bfloat16).at[places].set(received, mode="drop")
    )
    occupied = jnp.zeros((slot_count,), jnp.bool_).at[places].set(True, mode="drop")
    mixed = window_attention(
        layout[:, :local_width],
        layout[:, local_width : 2 * local_width],
        layout[:, 2 * local_width :],
        occupied,
        head_count,
    )
    outgoing = mixed[jnp.minimum(places, slot_count - 1)]
    returned = lax.all_to_all(
        outgoing.reshape(peer_count, capacity, local_width),
        "seq",
        split_axis=0,
        concat_axis=0,
        tiled=True,
    )
    window_mix = returned.reshape(slot_count, local_width)[send_index]
    row_share = row_count // part_count
    summed_out = lax.psum(
        jnp.dot(window_mix, self_out_weight, preferred_element_type=jnp.float32), "mp"
    )
    hidden = voxels.astype(jnp.float32) + summed_out
    normed2 = rms_norm(hidden, cross_norm_gain)
    own_hidden = lax.dynamic_slice_in_dim(hidden, model_index * row_share, row_share, 0)
    cross_query = (
        jnp.dot(normed2, cross_q_weight, preferred_element_type=jnp.float32)
        .astype(jnp.bfloat16)
        .reshape(row_count, head_count, HD)
    )
    cond_pair = jnp.einsum(
        "td,cdh->cth", cond, cond_kv_weight, preferred_element_type=jnp.float32
    ).astype(jnp.bfloat16)

    def fold_block(running, key_block, value_block):
        row_max, totals, mixed_sum = running
        scores = jnp.einsum(
            "qhd,khd->qhk", cross_query, key_block, preferred_element_type=jnp.float32
        ) * HD ** (-0.5)
        new_max = jnp.maximum(row_max, jnp.max(scores, axis=-1))
        rescale = jnp.exp(row_max - new_max)
        weights = jnp.exp(scores - new_max[:, :, None])
        totals = totals * rescale + jnp.sum(weights, axis=-1)
        update = jnp.einsum(
            "qhk,khd->qhd",
            weights.astype(jnp.bfloat16),
            value_block,
            preferred_element_type=jnp.float32,
        )
        return (new_max, totals, mixed_sum * rescale[:, :, None] + update)

    start_state = (
        jnp.full((row_count, head_count), -1e30, jnp.float32),
        jnp.zeros((row_count, head_count), jnp.float32),
        jnp.zeros((row_count, head_count, HD), jnp.float32),
    )
    key_piece = lax.all_gather(cond_pair[0], "seq", axis=0, tiled=True)
    value_piece = lax.all_gather(cond_pair[1], "seq", axis=0, tiled=True)
    token_count = key_piece.shape[0]
    sub_block = math.gcd(token_count, 512)
    key_blocks = key_piece.reshape(token_count // sub_block, sub_block, head_count, HD)
    value_blocks = value_piece.reshape(token_count // sub_block, sub_block, head_count, HD)

    def advance(state, operands):
        return (fold_block(state, operands[0], operands[1]), None)

    folded, unused = lax.scan(advance, start_state, (key_blocks, value_blocks))
    row_max, totals, mixed_sum = folded
    cross_mix = (
        (mixed_sum / totals[:, :, None]).astype(jnp.bfloat16).reshape(row_count, local_width)
    )
    cross_sum = lax.psum_scatter(
        jnp.dot(cross_mix, cross_out_weight, preferred_element_type=jnp.float32),
        "mp",
        scatter_dimension=0,
        tiled=True,
    )
    return (own_hidden + cross_sum).astype(jnp.bfloat16)


def solution(mesh):
    heads_match = mesh.shape["mp"] == 4 and mesh.shape["seq"] == 8
    return jax.shard_map(
        by_head if heads_match else by_owner,
        mesh=mesh,
        in_specs=(
            P("seq", None),
            P("seq"),
            P("seq", None),
            P(),
            P(None, None, "mp"),
            P("mp", None),
            P(),
            P(None, "mp"),
            P(None, None, "mp"),
            P("mp", None),
        ),
        out_specs=P(("seq", "mp"), None),
        check_vma=False,
    )
```

```python
import functools
import math

import jax
import jax.numpy as jnp
from jax import lax
from jax.experimental import pallas as pl
from jax.experimental.pallas import tpu as pltpu
from jax.sharding import PartitionSpec as P

HD = 64
WBLK = 64
LANES = 128
ID_ROWS = 16
MEGA = 1024 * 1024
BATCH = 8
CORE_SWAP = ((0, 1), (1, 0), (2, 3), (3, 2))
CHIP_SWAP = ((0, 2), (2, 0), (1, 3), (3, 1))
BOTH_SWAP = ((0, 3), (3, 0), (1, 2), (2, 1))
SIDE_SWAP = tuple((i, i ^ 1) for i in range(8))
NEXT_SWAP = tuple((i, i ^ 2) for i in range(8))
SKIP_SWAP = tuple((i, i ^ 4) for i in range(8))


def low_lanes(shape):
    return lax.broadcasted_iota(jnp.int32, shape, 1) < HD


def swap_halves(values):
    return pltpu.roll(values, HD, 1)


def columns_of(row):
    return jnp.transpose(jnp.broadcast_to(row, (LANES, LANES)))


def one_hot(condition):
    return jnp.where(condition, 1.0, 0.0).astype(jnp.bfloat16)


def project_kernel(
    core_ref, seq_ref, vox_ref, gain_ref, place_ref, own_ref, other_ref, *refs
):
    *out_refs, rank_ref, normed_ref, ids_ref, blob_ref, local_ref, copy_sem = refs
    vox_copy = pltpu.make_async_copy(vox_ref, local_ref, copy_sem.at[0])
    step = pl.program_id(0)
    rows = normed_ref.shape[0]
    packed = rows // 2
    groups = place_ref.shape[0]

    @pl.when(step == 0)
    def _():
        vox_copy.start()
        places = place_ref[...].astype(jnp.float32)
        place_rows = [places[g : g + 1] for g in range(groups)]
        place_columns = [columns_of(row) for row in place_rows]
        blank = jnp.zeros((8 - groups, LANES), jnp.float32)
        lane = lax.broadcasted_iota(jnp.int32, (LANES, LANES), 1).astype(jnp.float32)
        rank_rows = [
            sum(
                jnp.sum(jnp.where(column < row, 1.0, 0.0), axis=0, keepdims=True)
                for column in place_columns
            )
            for row in place_rows
        ]
        rank_columns = [
            jnp.sum(sum(jnp.where(row < column, 1.0, 0.0) for row in place_rows), axis=1, keepdims=True)
            for column in place_columns
        ]
        window_rows = [
            jnp.floor(
                sum(
                    jnp.sum(
                        jnp.where(rank == lane + float(g * LANES), column, 0.0), axis=0, keepdims=True
                    )
                    for rank, column in zip(rank_columns, place_columns)
                )
                * (1.0 / WBLK)
            )
            for g in range(groups)
        ]
        slot = lax.broadcasted_iota(jnp.int32, (1, LANES), 1)
        bounds = jnp.zeros((1, LANES), jnp.float32)
        for block in range(2 * groups):
            begin = (block % 2) * WBLK
            row = window_rows[block // 2]
            bounds = jnp.where(slot == block, row[:, begin : begin + 1], bounds)
            bounds = jnp.where(
                slot == block + 2 * groups, row[:, begin + WBLK - 1 : begin + WBLK], bounds
            )
        windows = jnp.concatenate(
            window_rows + [bounds] + [jnp.zeros_like(bounds)] * (7 - groups), axis=0
        )
        high = jnp.floor(windows * (1.0 / 256.0))
        ids_ref[...] = jnp.concatenate([high, windows - 256.0 * high], axis=0).astype(jnp.bfloat16)
        rank_ref[...] = jnp.concatenate(rank_rows + [blank], axis=0)
        wanted = (lax.broadcasted_iota(jnp.int32, (rows, LANES), 0) + core_ref[0] * rows).astype(
            jnp.float32
        )
        order = jnp.concatenate([one_hot(row == wanted) for row in rank_rows], axis=1)
        vox_copy.wait()
        values = jnp.dot(order, local_ref[...], preferred_element_type=jnp.float32)
        spread = jnp.mean(values * values, axis=-1, keepdims=True)
        normed_ref[...] = (values * lax.rsqrt(spread + 1e-06) * gain_ref[...]).astype(jnp.bfloat16)

    def emit(weight_ref, holder):
        normed = normed_ref[...]
        low = low_lanes((rows, LANES))
        low_packed = low_lanes((packed, LANES))
        query, key, value = (
            jnp.dot(normed, weight_ref[part], preferred_element_type=jnp.float32)
            for part in range(3)
        )
        query = query * HD ** (-0.5)
        for at in range(0, weight_ref.shape[2], LANES):
            keys, values = key[:, at : at + LANES], value[:, at : at + LANES]
            first, second = query[:packed, at : at + LANES], query[packed:, at : at + LANES]
            pairs = (
                (
                    jnp.where(low, keys, swap_halves(values)),
                    jnp.where(low_packed, first, swap_halves(second)),
                ),
                (
                    jnp.where(low, swap_halves(keys), values),
                    jnp.where(low_packed, swap_halves(first), second),
                ),
            )
            for side, (keyval, queries) in enumerate(pairs):
                head = holder * (weight_ref.shape[2] // HD) + at // HD + side
                target = head ^ seq_ref[0]
                blob_ref[target, :rows] = keyval.astype(jnp.bfloat16)
                blob_ref[target, rows : rows + ID_ROWS] = ids_ref[...]
                blob_ref[target, rows + ID_ROWS :] = queries.astype(jnp.bfloat16)

    @pl.when(step == 0)
    def _():
        emit(own_ref, core_ref[0])

    @pl.when(step == 1)
    def _():
        emit(other_ref, 1 - core_ref[0])
        for target, out_ref in enumerate(out_refs):
            out_ref[...] = blob_ref[target]


def project(core, seq, vox, gain, places, own_weight, other_weight):
    row_count, width = vox.shape
    rows = row_count // 2
    local_width = own_weight.shape[2]
    heads = 2 * local_width // HD
    blob = rows + ID_ROWS + rows // 2

    def fixed(array):
        return pl.BlockSpec(array.shape, lambda step, *refs: (0,) * array.ndim)

    outs = [jax.ShapeDtypeStruct((blob, LANES), jnp.bfloat16)] * heads
    outs.append(jax.ShapeDtypeStruct((8, LANES), jnp.float32))
    operands = (vox, gain, places, own_weight, other_weight)
    return pl.pallas_call(
        project_kernel,
        out_shape=outs,
        grid_spec=pltpu.PrefetchScalarGridSpec(
            num_scalar_prefetch=2,
            grid=(2,),
            in_specs=[pl.BlockSpec(memory_space=pltpu.HBM)]
            + [fixed(operand) for operand in operands[1:]],
            out_specs=[fixed(out) for out in outs],
            scratch_shapes=[
                pltpu.VMEM((rows, width), jnp.bfloat16),
                pltpu.VMEM((ID_ROWS, LANES), jnp.bfloat16),
                pltpu.VMEM((heads, blob, LANES), jnp.bfloat16),
                pltpu.VMEM((row_count, width), jnp.bfloat16),
                pltpu.SemaphoreType.DMA((1,)),
            ],
        ),
        compiler_params=pltpu.CompilerParams(vmem_limit_bytes=28 * MEGA),
    )(core, seq, *operands)


def window_kernel(
    core_ref,
    seq_ref,
    *refs,
):
    sources = (len(refs) - 10) // 2
    mine_refs, theirs_refs, refs = refs[:sources], refs[sources : 2 * sources], refs[2 * sources :]
    out_ref, key_ref, window_ref, query_ref, column_ref, *refs = refs
    sum_ref, total_ref, plan_ref, plan_smem, late_smem, copy_sem = refs
    packed = out_ref.shape[1]
    rows = 2 * packed
    blocks = rows // LANES
    last = 2 * rows // WBLK
    low_packed = low_lanes((packed, LANES))
    core = core_ref[0]

    low = low_lanes((8, LANES))
    real = lax.broadcasted_iota(jnp.int32, (8, LANES), 0) < 2 * blocks
    for index, (mine_ref, theirs_ref) in enumerate(zip(mine_refs, theirs_refs)):
        for ref, side in ((mine_ref, core), (theirs_ref, 1 - core)):
            key_ref[index, pl.ds(pl.multiple_of(side * rows, LANES), rows)] = ref[:rows]
    key_ref[:, 2 * rows :] = jnp.zeros((sources, 2 * LANES, LANES), jnp.bfloat16)
    bounds = []
    for index in range(sources):
        tile = mine_refs[index][rows : rows + ID_ROWS].astype(jnp.float32)
        ids = tile[:8] * 256.0 + tile[8:]
        bounds.append(ids[2 * blocks : 2 * blocks + 1])
        even = jnp.where(real, ids, -1.0)
        window_ref[index, 0] = even
        window_ref[index, 1] = jnp.where(
            low, swap_halves(even), swap_halves(pltpu.roll(even, 7, 0))
        )

    bounds = jnp.concatenate(bounds, axis=0)
    slot = lax.broadcasted_iota(jnp.int32, (sources, LANES), 1)
    lows = jnp.where(slot < last, bounds, jnp.inf)
    highs = jnp.where(slot < last, pltpu.roll(bounds, LANES - last, 1), jnp.inf)
    begins = [
        jnp.where(core == 0, bounds[:, at : at + 1], bounds[:, at + last // 2 : at + last // 2 + 1])
        for at in range(0, last // 2, 2)
    ]
    ends = [
        jnp.where(core == 0, bounds[:, at : at + 1], bounds[:, at + last // 2 : at + last // 2 + 1])
        for at in range(last + 1, last + last // 2, 2)
    ]
    first = jnp.full((sources, LANES), float(last), jnp.float32)
    beyond = first
    for source in range(sources):
        for block in range(blocks):
            here = slot == source * blocks + block
            begin, end = (edges[block][source : source + 1] for edges in (begins, ends))
            first = jnp.where(
                here, jnp.sum(jnp.where(highs < begin, 1.0, 0.0), axis=1, keepdims=True), first
            )
            beyond = jnp.where(
                here, jnp.sum(jnp.where(lows <= end, 1.0, 0.0), axis=1, keepdims=True), beyond
            )
    plan_ref[0] = first.astype(jnp.int32)
    plan_ref[1] = jnp.floor((beyond - first + 3.0) * 0.25).astype(jnp.int32)
    plan_copy = pltpu.make_async_copy(plan_ref, plan_smem, copy_sem.at[0])
    plan_copy.start()
    plan_copy.wait()

    def fold(pair, other, turn, query_part, query_ids, sums, total):
        start = jnp.minimum(plan_smem[0, other, pair] + 4 * turn, last)
        keyval = key_ref[other, pl.ds(pl.multiple_of(start * WBLK, WBLK), 2 * LANES)]
        scores = lax.dot_general(
            query_part, keyval, (((1,), (1,)), ((), ())), preferred_element_type=jnp.float32
        )
        weights = [
            jnp.where(
                query_ids == window_ref[other, start % 2, pl.ds(start // 2 + g, 1)],
                jnp.exp(scores[:, g * LANES : (g + 1) * LANES]),
                0.0,
            )
            for g in range(2)
        ]
        rounded = jnp.concatenate([part.astype(jnp.bfloat16) for part in weights], axis=1)
        return (
            sums + weights[0] + weights[1],
            total + jnp.dot(rounded, keyval, preferred_element_type=jnp.float32),
        )

    for source, ref in enumerate(mine_refs):
        wire = ref[rows + ID_ROWS :].astype(jnp.float32)
        query = jnp.concatenate(
            [jnp.where(low_packed, wire, 0.0), jnp.where(low_packed, swap_halves(wire), 0.0)],
            axis=0,
        ).astype(jnp.bfloat16)
        for block in range(blocks):
            query_ref[source * blocks + block] = query[block * LANES : (block + 1) * LANES]

    def sweep(source, carry):
        for block in range(blocks):
            at = source * blocks + block
            query_part = query_ref[at]
            query_ids = columns_of(window_ref[source, 0, pl.ds(core * blocks + block, 1)])
            column_ref[at] = query_ids
            sums = jnp.zeros((LANES, LANES), jnp.float32)
            total = jnp.zeros((LANES, LANES), jnp.float32)
            for other in range(sources):
                sums, total = fold(at, other, 0, query_part, query_ids, sums, total)
            sum_ref[at] = sums
            total_ref[at] = total
        return carry

    lax.fori_loop(0, sources, sweep, 0, unroll=4)
    spare = sources * blocks
    query_ref[spare] = jnp.zeros((LANES, LANES), jnp.bfloat16)
    column_ref[spare] = jnp.zeros((LANES, LANES), jnp.float32)
    sum_ref[spare] = jnp.zeros((LANES, LANES), jnp.float32)
    total_ref[spare] = jnp.zeros((LANES, LANES), jnp.float32)

    count = jnp.int32(0)
    for other in range(sources):
        for at in range(sources * blocks):
            late_smem[count] = other * LANES + at
            count = count + jnp.where(plan_smem[1, other, at] > 1, 1, 0)
    for i in range(BATCH):
        late_smem[count + i] = spare

    def visit(index, carry):
        pairs = [late_smem[index * BATCH + i] for i in range(BATCH)]
        pairs = [(pair // LANES, pair % LANES) for pair in pairs]
        turns = functools.reduce(jnp.maximum, [plan_smem[1, other, at] for other, at in pairs])

        def more(turn, carry):
            nothing = jnp.zeros((LANES, LANES), jnp.float32)
            parts = [
                fold(at, other, turn, query_ref[at], column_ref[at], nothing, nothing)
                for other, at in pairs
            ]
            for (other, at), (sums, total) in zip(pairs, parts):
                sum_ref[at] = sum_ref[at] + sums
                total_ref[at] = total_ref[at] + total
            return carry

        return lax.fori_loop(1, turns, more, carry)

    lax.fori_loop(0, (count + BATCH - 1) // BATCH, visit, 0)

    for source in range(sources):
        mixed = jnp.concatenate(
            [
                total_ref[at] / jnp.sum(sum_ref[at], axis=-1, keepdims=True)
                for at in range(source * blocks, (source + 1) * blocks)
            ],
            axis=0,
        )
        out_ref[source ^ seq_ref[0]] = jnp.where(low_packed, swap_halves(mixed[:packed]), mixed[packed:]).astype(
            jnp.bfloat16
        )


def window_mixing(core, seq, mine, theirs, packed):
    sources = len(mine)
    rows = 2 * packed
    blocks = rows // LANES
    vmem = pl.BlockSpec(memory_space=pltpu.VMEM)
    smem = pl.BlockSpec(memory_space=pltpu.SMEM)
    return pl.pallas_call(
        window_kernel,
        out_shape=jax.ShapeDtypeStruct((sources, packed, LANES), jnp.bfloat16),
        in_specs=[smem] * 2 + [vmem] * (2 * sources),
        out_specs=vmem,
        scratch_shapes=[
            pltpu.VMEM((sources, 2 * rows + 2 * LANES, LANES), jnp.bfloat16),
            pltpu.VMEM((sources, 2, 8, LANES), jnp.float32),
            pltpu.VMEM((sources * blocks + 1, LANES, LANES), jnp.bfloat16),
            pltpu.VMEM((sources * blocks + 1, LANES, LANES), jnp.float32),
            pltpu.VMEM((sources * blocks + 1, LANES, LANES), jnp.float32),
            pltpu.VMEM((sources * blocks + 1, LANES, LANES), jnp.float32),
            pltpu.VMEM((2, sources, LANES), jnp.int32),
            pltpu.SMEM((2, sources, LANES), jnp.int32),
            pltpu.SMEM((sources * sources * blocks + 2 * BATCH,), jnp.int32),
            pltpu.SemaphoreType.DMA((1,)),
        ],
        compiler_params=pltpu.CompilerParams(vmem_limit_bytes=24 * MEGA),
        cost_estimate=pl.CostEstimate(
            flops=80 * LANES * (sources * packed) ** 2,
            transcendentals=2 * (sources * packed) ** 2,
            bytes_accessed=4 * sources * mine[0].size,
        ),
    )(core, seq, *mine, *theirs)


def fetch(refs, local_ref, copy_sem):
    copies = [
        pltpu.make_async_copy(ref, local_ref.at[index], copy_sem.at[index])
        for index, ref in enumerate(refs)
    ]
    for copy in copies:
        copy.start()
    return copies


def mix_heads(core, own_ref, other_ref, order, weight_ref, copies, mix_ref):
    heads, share, _ = own_ref.shape
    rows = 2 * share
    low = low_lanes((share, LANES))
    for half, ref in enumerate((own_ref, other_ref)):
        offset = pl.multiple_of((core if half == 0 else 1 - core) * rows, LANES)
        for pair in range(heads // 2):
            holder = core if pair < heads // 4 else 1 - core
            head = holder * (heads // 2) + (pair % (heads // 4)) * 2
            first, second = (ref[at].astype(jnp.float32) for at in (head, head + 1))
            at = pair * LANES
            mix_ref[pl.ds(offset, share), at : at + LANES] = jnp.where(
                low, first, swap_halves(second)
            ).astype(jnp.bfloat16)
            mix_ref[pl.ds(offset + share, share), at : at + LANES] = jnp.where(
                low, swap_halves(first), second
            ).astype(jnp.bfloat16)
    mix = jnp.dot(order, mix_ref[...], preferred_element_type=jnp.float32).astype(jnp.bfloat16)
    depth = weight_ref.shape[1]
    for copy in copies:
        copy.wait()
    return sum(
        jnp.dot(
            mix[:, i * depth : (i + 1) * depth], weight_ref[i], preferred_element_type=jnp.float32
        )
        for i in range(len(copies))
    )


def near_kernel(
    core_ref,
    rank_ref,
    vox_ref,
    own_ref,
    other_ref,
    weight_ref,
    other_weight_ref,
    hidden_ref,
    order_ref,
    token_ref,
    mix_ref,
    column_ref,
    local_ref,
    copy_sem,
):
    core = core_ref[0]
    copies = fetch((weight_ref, other_weight_ref), local_ref, copy_sem)
    token_ref[...] = jnp.zeros_like(token_ref)
    rows = hidden_ref.shape[0]
    share = rows // 2
    groups = 2 * rows // LANES
    for group in range(groups):
        column_ref[group * LANES : (group + 1) * LANES] = columns_of(rank_ref[group : group + 1])
    begin = pl.multiple_of(core * share, 64)
    ranks = jnp.concatenate(
        [column_ref[pl.ds(begin, share)], column_ref[pl.ds(begin + rows, share)]], axis=0
    )
    lane = lax.broadcasted_iota(jnp.int32, (rows, LANES), 1).astype(jnp.float32)
    order = jnp.concatenate(
        [one_hot(ranks == lane + float(group * LANES)) for group in range(groups)], axis=1
    )
    order_ref[...] = order
    values = jnp.concatenate(
        [vox_ref[pl.ds(begin, share)], vox_ref[pl.ds(begin + rows, share)]], axis=0
    ).astype(jnp.float32)
    hidden_ref[...] = values + mix_heads(
        core, own_ref, other_ref, order, local_ref, copies, mix_ref
    )


def far_kernel(
    core_ref,
    chip_ref,
    base_ref,
    order_ref,
    gain_ref,
    own_ref,
    other_ref,
    weight_ref,
    other_weight_ref,
    query_weight_ref,
    other_query_weight_ref,
    hidden_ref,
    query_ref,
    other_query_ref,
    mix_ref,
    kept_ref,
    local_ref,
    copy_sem,
    query_local_ref,
    query_sem,
):
    share = hidden_ref.shape[0]
    copies = fetch((weight_ref, other_weight_ref), local_ref, copy_sem)
    query_copies = fetch((query_weight_ref, other_query_weight_ref), query_local_ref, query_sem)
    hidden = base_ref[...] + mix_heads(
        core_ref[0], own_ref, other_ref, order_ref[...], local_ref, copies, mix_ref
    )
    kept_ref[...] = hidden
    hidden_ref[...] = kept_ref[pl.ds(pl.multiple_of(chip_ref[0] * share, 64), share)]
    spread = jnp.mean(hidden * hidden, axis=-1, keepdims=True)
    normed = (hidden * lax.rsqrt(spread + 1e-06) * gain_ref[...]).astype(jnp.bfloat16)
    for index, out in enumerate((query_ref, other_query_ref)):
        query_copies[index].wait()
        queries = jnp.dot(normed, query_local_ref[index], preferred_element_type=jnp.float32)
        out[...] = (queries.astype(jnp.bfloat16).astype(jnp.float32) * HD ** (-0.5)).astype(
            jnp.bfloat16
        )


def whole(array):
    return pl.BlockSpec(array.shape, lambda step: (0,) * array.ndim)


def near_part(core, ranks, voxels, mixes, weights):
    row_count, width = voxels.shape
    rows = row_count // 2
    heads = mixes[0].shape[0]
    outs = (
        jax.ShapeDtypeStruct((rows, width), jnp.float32),
        jax.ShapeDtypeStruct((rows, row_count), jnp.bfloat16),
        jax.ShapeDtypeStruct((8, LANES), jnp.float32),
    )
    return pl.pallas_call(
        near_kernel,
        out_shape=outs,
        grid=(1,),
        in_specs=[pl.BlockSpec(memory_space=pltpu.SMEM)]
        + [whole(array) for array in (ranks, voxels, *mixes)]
        + [pl.BlockSpec(memory_space=pltpu.HBM)] * len(weights),
        out_specs=tuple(whole(out) for out in outs),
        scratch_shapes=[
            pltpu.VMEM((row_count, heads * HD), jnp.bfloat16),
            pltpu.VMEM((row_count, LANES), jnp.float32),
            pltpu.VMEM((len(weights), *weights[0].shape), jnp.bfloat16),
            pltpu.SemaphoreType.DMA((len(weights),)),
        ],
        compiler_params=pltpu.CompilerParams(vmem_limit_bytes=24 * MEGA),
        cost_estimate=pl.CostEstimate(
            flops=10 * rows * width * width, transcendentals=0, bytes_accessed=8 * width * width
        ),
    )(core, ranks, voxels, *mixes, *weights)


def far_part(core, chip, base, order, gain, mixes, weights, query_weights):
    rows, width = base.shape
    share = rows // 2
    local_width = query_weights[0].shape[1]
    heads = mixes[0].shape[0]
    outs = (
        jax.ShapeDtypeStruct((share, width), jnp.float32),
        jax.ShapeDtypeStruct((rows, local_width), jnp.bfloat16),
        jax.ShapeDtypeStruct((rows, local_width), jnp.bfloat16),
    )
    return pl.pallas_call(
        far_kernel,
        out_shape=outs,
        grid=(1,),
        in_specs=[pl.BlockSpec(memory_space=pltpu.SMEM)] * 2
        + [whole(array) for array in (base, order, gain, *mixes)]
        + [pl.BlockSpec(memory_space=pltpu.HBM)] * (len(weights) + len(query_weights)),
        out_specs=tuple(whole(out) for out in outs),
        scratch_shapes=[
            pltpu.VMEM((2 * rows, heads * HD), jnp.bfloat16),
            pltpu.VMEM((rows, width), jnp.float32),
            pltpu.VMEM((len(weights), *weights[0].shape), jnp.bfloat16),
            pltpu.SemaphoreType.DMA((len(weights),)),
            pltpu.VMEM((len(query_weights), *query_weights[0].shape), jnp.bfloat16),
            pltpu.SemaphoreType.DMA((len(query_weights),)),
        ],
        compiler_params=pltpu.CompilerParams(vmem_limit_bytes=24 * MEGA),
        cost_estimate=pl.CostEstimate(
            flops=10 * rows * width * width, transcendentals=rows, bytes_accessed=8 * width * width
        ),
    )(core, chip, base, order, gain, *mixes, *weights, *query_weights)


def cross_kernel(chip_ref, *refs):
    query_refs, piece_refs, out_refs, score_ref = refs[:2], refs[2:-5], refs[-5:-1], refs[-1]
    rows, local_width = query_refs[0].shape
    share = rows // 2
    low = low_lanes((rows, LANES))
    zero = jnp.zeros((), jnp.bfloat16)
    chunk = piece_refs[0].shape[0]
    chip = chip_ref[0]

    def lane_groups(values):
        return [values[:, g : g + LANES] for g in range(0, chunk, LANES)]

    for turn, query_ref in enumerate(query_refs):
        for pair in range(0, local_width, LANES):
            mixes = []
            for head in range(2):
                query = jnp.where(low == (head == 0), query_ref[:, pair : pair + LANES], zero)
                peak = jnp.full((rows, LANES), -jnp.inf, jnp.float32)
                for index, ref in enumerate(piece_refs):
                    scores = lax.dot_general(
                        query,
                        ref[:, pair : pair + LANES],
                        (((1,), (1,)), ((), ())),
                        preferred_element_type=jnp.float32,
                    )
                    score_ref[head, :, index * chunk : (index + 1) * chunk] = scores
                    peak = functools.reduce(jnp.maximum, lane_groups(scores), peak)
                row_max = jnp.max(peak, axis=-1, keepdims=True)
                sums = jnp.zeros((rows, LANES), jnp.float32)
                total = jnp.zeros((rows, LANES), jnp.float32)
                for index, ref in enumerate(piece_refs):
                    weights = jnp.exp(
                        score_ref[head, :, index * chunk : (index + 1) * chunk] - row_max
                    )
                    sums = functools.reduce(jnp.add, lane_groups(weights), sums)
                    total = total + jnp.dot(
                        weights.astype(jnp.bfloat16),
                        ref[:, local_width + pair : local_width + pair + LANES],
                        preferred_element_type=jnp.float32,
                    )
                mixes.append(total / jnp.sum(sums, axis=-1, keepdims=True))
            mixed = jnp.where(low, mixes[0], mixes[1])
            halves = (mixed[:share], mixed[share:])
            for side, out_ref in enumerate(out_refs[2 * turn : 2 * turn + 2]):
                out_ref[:, pair : pair + LANES] = jnp.where(
                    chip == side, halves[0], halves[1]
                ).astype(jnp.bfloat16)


def cross_mixing(chip, queries, pieces):
    rows, local_width = queries[0].shape
    tokens = sum(piece.shape[0] for piece in pieces)
    block = pl.BlockSpec(memory_space=pltpu.VMEM)
    return pl.pallas_call(
        cross_kernel,
        out_shape=[jax.ShapeDtypeStruct((rows // 2, local_width), jnp.bfloat16)] * 4,
        in_specs=[pl.BlockSpec(memory_space=pltpu.SMEM)] + [block] * (2 + len(pieces)),
        out_specs=[block] * 4,
        scratch_shapes=[pltpu.VMEM((2, rows, tokens), jnp.float32)],
        compiler_params=pltpu.CompilerParams(vmem_limit_bytes=28 * MEGA),
    )(chip, *queries, *pieces)


def finish_kernel(base_ref, *refs):
    mix_refs, weight_refs, out_ref = refs[:3], refs[3:6], refs[6]
    total = base_ref[...]
    for mix_ref, weight_ref in zip(mix_refs, weight_refs):
        total = total + jnp.dot(mix_ref[...], weight_ref[...], preferred_element_type=jnp.float32)
    out_ref[...] = total.astype(jnp.bfloat16)


def finish(base, mixes, weights):
    operands = (base, *mixes, *weights)
    return pl.pallas_call(
        finish_kernel,
        out_shape=jax.ShapeDtypeStruct(base.shape, jnp.bfloat16),
        in_specs=[pl.BlockSpec(memory_space=pltpu.VMEM)] * len(operands),
        out_specs=pl.BlockSpec(memory_space=pltpu.VMEM),
        compiler_params=pltpu.CompilerParams(vmem_limit_bytes=12 * MEGA),
    )(*operands)


def swap(array, pairs):
    return lax.ppermute(array, "mp", pairs)


def across(array, pairs):
    return lax.ppermute(array, "seq", pairs)


def spread_out(blobs):
    count = len(blobs)
    return [blobs[0]] + [
        across(blobs[step], [(i, i ^ step) for i in range(count)]) for step in range(1, count)
    ]


def by_head(
    voxels,
    destination,
    cond,
    norm_gain,
    qkv_weight,
    self_out_weight,
    cross_norm_gain,
    cross_q_weight,
    cond_kv_weight,
    cross_out_weight,
):
    model_index = lax.axis_index("mp").astype(jnp.int32)
    seq = lax.axis_index("seq").astype(jnp.int32).reshape(1)
    core = (model_index % 2).reshape(1)
    chip = (model_index // 2).reshape(1)
    row_count, width = voxels.shape
    rows = row_count // 2
    share = rows // 2

    other_qkv = swap(qkv_weight, CORE_SWAP)
    cond_pair = [
        jnp.dot(cond, cond_kv_weight[part], preferred_element_type=jnp.float32).astype(jnp.bfloat16)
        for part in range(2)
    ]
    own_piece = jnp.concatenate(cond_pair, axis=1)
    destination, own_piece = lax.optimization_barrier((destination, own_piece))
    *sent, ranks = project(
        core,
        seq,
        voxels,
        norm_gain.reshape(1, width),
        destination.reshape(row_count // LANES, LANES),
        qkv_weight,
        other_qkv,
    )

    mine = spread_out(sent)
    theirs = [swap(blob, CORE_SWAP) for blob in mine]
    late_piece, *mine = lax.optimization_barrier((own_piece, *mine))
    side_piece = across(late_piece, SIDE_SWAP)
    next_piece = across(late_piece, NEXT_SWAP)
    skip_piece = across(late_piece, SKIP_SWAP)
    mixed = window_mixing(core, seq, mine, theirs, share)
    mixed, side_piece, next_piece, skip_piece = lax.optimization_barrier(
        (mixed, side_piece, next_piece, skip_piece)
    )

    near = lax.all_to_all(mixed, "seq", split_axis=0, concat_axis=0, tiled=True)
    last_piece = across(skip_piece, NEXT_SWAP)
    skip_side_piece = across(skip_piece, SIDE_SWAP)
    chip_self = swap(self_out_weight, CHIP_SWAP)
    far = swap(near, CHIP_SWAP)
    near_other = swap(near, CORE_SWAP)
    far, last_piece, skip_side_piece, chip_self = lax.optimization_barrier(
        (far, last_piece, skip_side_piece, chip_self)
    )
    last_side_piece = across(last_piece, SIDE_SWAP)
    next_side_piece = across(side_piece, NEXT_SWAP)
    far_other = swap(far, CORE_SWAP)
    pieces = [
        own_piece,
        side_piece,
        next_piece,
        next_side_piece,
        skip_piece,
        skip_side_piece,
        last_piece,
        last_side_piece,
    ]
    base, order, token = near_part(
        core,
        ranks,
        voxels,
        (near, near_other),
        (self_out_weight, swap(self_out_weight, CORE_SWAP)),
    )
    own_hidden, own_query, other_query = far_part(
        core,
        chip,
        base,
        order,
        cross_norm_gain.reshape(1, width),
        (far, far_other),
        (chip_self, swap(chip_self, CORE_SWAP)),
        (cross_q_weight, swap(cross_q_weight, CORE_SWAP)),
    )

    asked = swap(other_query, CORE_SWAP)
    late_weight, own_query = lax.optimization_barrier((cross_out_weight, own_query))
    chip_cross = swap(late_weight, CHIP_SWAP)
    kept, to_chip, to_core, to_both = cross_mixing(chip, (own_query, asked), pieces)
    kept, chip_cross = lax.optimization_barrier((kept, chip_cross))
    weights = (chip_cross, swap(chip_cross, CORE_SWAP), swap(cross_out_weight, CORE_SWAP))
    mixes = (swap(to_chip, CHIP_SWAP), swap(to_both, BOTH_SWAP), swap(to_core, CORE_SWAP))
    base = own_hidden + jnp.dot(kept, cross_out_weight, preferred_element_type=jnp.float32)
    return finish(base, mixes, weights)


def rms_norm(matrix, gain):
    values = matrix.astype(jnp.float32)
    spread = jnp.mean(values * values, axis=-1, keepdims=True)
    return (values * lax.rsqrt(spread + 1e-06) * gain).astype(jnp.bfloat16)


def window_attention(queries, keyset, valset, occupied, head_count):
    slot_count = queries.shape[0]
    window_count = slot_count // WBLK
    query_heads = queries.reshape(window_count, WBLK, head_count, HD)
    key_heads = keyset.reshape(window_count, WBLK, head_count, HD)
    value_heads = valset.reshape(window_count, WBLK, head_count, HD)
    scores = jnp.einsum(
        "wqhd,wkhd->whqk", query_heads, key_heads, preferred_element_type=jnp.float32
    ) * HD ** (-0.5)
    diagonal = (
        jnp.arange(WBLK, dtype=jnp.int32)[:, None] == jnp.arange(WBLK, dtype=jnp.int32)[None, :]
    )
    allowed = occupied.reshape(window_count, 1, WBLK) | diagonal[None]
    weights = jnp.where(allowed[:, None], jnp.exp(scores), 0.0)
    totals = jnp.sum(weights, axis=-1)
    mixed = jnp.einsum(
        "whqk,wkhd->wqhd",
        weights.astype(jnp.bfloat16),
        value_heads,
        preferred_element_type=jnp.float32,
    )
    mixed = mixed / jnp.transpose(totals, (0, 2, 1))[:, :, :, None]
    return mixed.astype(jnp.bfloat16).reshape(slot_count, head_count * HD)


def by_owner(
    voxels,
    destination,
    cond,
    norm_gain,
    qkv_weight,
    self_out_weight,
    cross_norm_gain,
    cross_q_weight,
    cond_kv_weight,
    cross_out_weight,
):
    peer_count = lax.axis_size("seq")
    part_count = lax.axis_size("mp")
    model_index = lax.axis_index("mp")
    row_count = voxels.shape[0]
    local_width = qkv_weight.shape[2]
    head_count = local_width // HD
    capacity = 2 * row_count // peer_count
    slot_count = peer_count * capacity
    owner_ids = destination // slot_count
    slot_ids = destination % slot_count
    matches = (owner_ids[:, None] == jnp.arange(peer_count, dtype=jnp.int32)[None, :]).astype(
        jnp.int32
    )
    within = jnp.sum(matches * (jnp.cumsum(matches, axis=0) - 1), axis=1)
    send_index = owner_ids * capacity + within
    normed = rms_norm(voxels, norm_gain)
    place_buffer = (
        jnp.full((slot_count,), slot_count, jnp.int32)
        .at[send_index]
        .set(slot_ids)
        .reshape(peer_count, capacity)
    )
    projected = jnp.einsum(
        "rd,cdh->rch", normed, qkv_weight, preferred_element_type=jnp.float32
    ).astype(jnp.bfloat16)
    send_buffer = (
        jnp.zeros((slot_count, 3 * local_width), jnp.bfloat16)
        .at[send_index]
        .set(projected.reshape(row_count, 3 * local_width))
    )
    received, places = (
        lax.all_to_all(
            send_buffer.reshape(peer_count, capacity, 3 * local_width),
            "seq",
            split_axis=0,
            concat_axis=0,
            tiled=True,
        ),
        lax.all_to_all(place_buffer, "seq", split_axis=0, concat_axis=0, tiled=True),
    )
    received = received.reshape(slot_count, 3 * local_width)
    places = places.reshape(slot_count)
    layout = (
        jnp.zeros((slot_count, 3 * local_width), jnp.bfloat16).at[places].set(received, mode="drop")
    )
    occupied = jnp.zeros((slot_count,), jnp.bool_).at[places].set(True, mode="drop")
    mixed = window_attention(
        layout[:, :local_width],
        layout[:, local_width : 2 * local_width],
        layout[:, 2 * local_width :],
        occupied,
        head_count,
    )
    outgoing = mixed[jnp.minimum(places, slot_count - 1)]
    returned = lax.all_to_all(
        outgoing.reshape(peer_count, capacity, local_width),
        "seq",
        split_axis=0,
        concat_axis=0,
        tiled=True,
    )
    window_mix = returned.reshape(slot_count, local_width)[send_index]
    row_share = row_count // part_count
    summed_out = lax.psum(
        jnp.dot(window_mix, self_out_weight, preferred_element_type=jnp.float32), "mp"
    )
    hidden = voxels.astype(jnp.float32) + summed_out
    normed2 = rms_norm(hidden, cross_norm_gain)
    own_hidden = lax.dynamic_slice_in_dim(hidden, model_index * row_share, row_share, 0)
    cross_query = (
        jnp.dot(normed2, cross_q_weight, preferred_element_type=jnp.float32)
        .astype(jnp.bfloat16)
        .reshape(row_count, head_count, HD)
    )
    cond_pair = jnp.einsum(
        "td,cdh->cth", cond, cond_kv_weight, preferred_element_type=jnp.float32
    ).astype(jnp.bfloat16)

    def fold_block(running, key_block, value_block):
        row_max, totals, mixed_sum = running
        scores = jnp.einsum(
            "qhd,khd->qhk", cross_query, key_block, preferred_element_type=jnp.float32
        ) * HD ** (-0.5)
        new_max = jnp.maximum(row_max, jnp.max(scores, axis=-1))
        rescale = jnp.exp(row_max - new_max)
        weights = jnp.exp(scores - new_max[:, :, None])
        totals = totals * rescale + jnp.sum(weights, axis=-1)
        update = jnp.einsum(
            "qhk,khd->qhd",
            weights.astype(jnp.bfloat16),
            value_block,
            preferred_element_type=jnp.float32,
        )
        return (new_max, totals, mixed_sum * rescale[:, :, None] + update)

    start_state = (
        jnp.full((row_count, head_count), -1e30, jnp.float32),
        jnp.zeros((row_count, head_count), jnp.float32),
        jnp.zeros((row_count, head_count, HD), jnp.float32),
    )
    key_piece = lax.all_gather(cond_pair[0], "seq", axis=0, tiled=True)
    value_piece = lax.all_gather(cond_pair[1], "seq", axis=0, tiled=True)
    token_count = key_piece.shape[0]
    sub_block = math.gcd(token_count, 512)
    key_blocks = key_piece.reshape(token_count // sub_block, sub_block, head_count, HD)
    value_blocks = value_piece.reshape(token_count // sub_block, sub_block, head_count, HD)

    def advance(state, operands):
        return (fold_block(state, operands[0], operands[1]), None)

    folded, unused = lax.scan(advance, start_state, (key_blocks, value_blocks))
    row_max, totals, mixed_sum = folded
    cross_mix = (
        (mixed_sum / totals[:, :, None]).astype(jnp.bfloat16).reshape(row_count, local_width)
    )
    cross_sum = lax.psum_scatter(
        jnp.dot(cross_mix, cross_out_weight, preferred_element_type=jnp.float32),
        "mp",
        scatter_dimension=0,
        tiled=True,
    )
    return (own_hidden + cross_sum).astype(jnp.bfloat16)


def solution(mesh):
    heads_match = mesh.shape["mp"] == 4 and mesh.shape["seq"] == 8
    return jax.shard_map(
        by_head if heads_match else by_owner,
        mesh=mesh,
        in_specs=(
            P("seq", None),
            P("seq"),
            P("seq", None),
            P(),
            P(None, None, "mp"),
            P("mp", None),
            P(),
            P(None, "mp"),
            P(None, None, "mp"),
            P("mp", None),
        ),
        out_specs=P(("seq", "mp"), None),
        check_vma=False,
    )
```
